32 devices in a mesh: dp: 8 (over z, y), narrow: 4 (over x, core).
Axes of the slice: x: 2, y: 2, z: 4, core: 2. Of those that a mesh axis runs over, the one named last changes fastest.
Arguments:
- tokens: bfloat16 [25088, 768], P(('dp', 'narrow')), may hold values from -6 to 6
- input_projection: bfloat16 [3, 768, 768], P(None, None, 'narrow'), may hold values from -0.21875 to 0.21875
- input_bias: float32 [2, 768], replicated, may hold values from -3 to 3
- position_bias: float32 [169, 24], replicated, may hold values from -4 to 4
- output_projection: bfloat16 [768, 768], P('narrow'), may hold values from -0.5 to 0.5
- inner_weight: bfloat16 [768, 3072], P(None, 'narrow'), may hold values from -0.21875 to 0.21875
- inner_bias: float32 [3072], replicated, may hold values from -2 to 2
- outer_weight: bfloat16 [3072, 768], P('narrow'), may hold values from -0.109375 to 0.109375
- norm_gains: float32 [3, 768], replicated, may hold values from 0.5 to 1.5
- offsets: float32 [5, 768], replicated, may hold values from -2 to 2
- head_first: bfloat16 [768, 2048], replicated, may hold values from -0.21875 to 0.21875
- head_first_bias: float32 [2048], replicated, may hold values from -2 to 2
- head_second: bfloat16 [2048, 2048], replicated, may hold values from -0.125 to 0.125
- head_second_bias: float32 [2048], replicated, may hold values from -2 to 2
- head_third: bfloat16 [2048, 256], replicated, may hold values from -0.125 to 0.125
- head_third_bias: float32 [256], replicated, may hold values from -2 to 2
- prototype_direction: bfloat16 [256, 65536], P(None, ('dp', 'narrow')), may hold values from -6 to 6
- prototype_gain: float32 [65536], P(('dp', 'narrow')), may hold values from 10 to 40
- crop_windows: int32 [8, 4], P('dp'), may hold values from 1 to 49, as said below
- first_epoch: int32 [65536], P(('dp', 'narrow')), may hold values 0 or 1
- feature_cotangent: bfloat16 [25088, 768], P(('dp', 'narrow')), may hold values from -6 to 6
- logit_cotangent: bfloat16 [32, 65536], P(None, ('dp', 'narrow')), may hold values from -6 to 6
Outputs:
- features: bfloat16 [25088, 768], P(('dp', 'narrow'))
- logits: float32 [32, 65536], P(None, ('dp', 'narrow'))
- tokens_grad: float32 [25088, 768], P(('dp', 'narrow'))
- input_projection_grad: float32 [3, 768, 768], P(None, 'dp', 'narrow')
- input_bias_grad: float32 [2, 768], replicated
- position_bias_grad: float32 [169, 24], replicated
- output_projection_grad: float32 [768, 768], P('narrow', 'dp')
- inner_weight_grad: float32 [768, 3072], P('dp', 'narrow')
- inner_bias_grad: float32 [3072], replicated
- outer_weight_grad: float32 [3072, 768], P('narrow', 'dp')
- norm_gains_grad: float32 [3, 768], replicated
- offsets_grad: float32 [5, 768], replicated
- head_first_grad: float32 [768, 2048], P(None, 'dp')
- head_first_bias_grad: float32 [2048], P('dp')
- head_second_grad: float32 [2048, 2048], P(None, 'dp')
- head_second_bias_grad: float32 [2048], P('dp')
- head_third_grad: float32 [2048, 256], P('dp')
- head_third_bias_grad: float32 [256], P('dp')
- prototype_direction_grad: float32 [256, 65536], P(None, ('dp', 'narrow'))
- prototype_gain_grad: float32 [65536], P(('dp', 'narrow'))
The draws below stay inside these ranges and needn't reach their ends.
Inputs may be any that keep to these rules, and one draw needn't show every extreme that they name: `crop_windows`: each row sums to 64; one entry of each row, at a place drawn from the seed, is exactly 49, and the others sum to 15.
All inputs are finite; a program needn't handle non-finite values. No bound on the sum of `first_epoch` on one device may be relied on, other than what follows from the above.
Results may differ from the reference program's by a relative error of at most 0.017.
The reference program's roundings to bfloat16 on the way count: a program that leaves them out, or rounds other values in their place, can miss the bound.
Values may be sent and summed in bfloat16 or wider, within the bound.
No kernel may reach another device: no remote copies, remote signals or barrier semaphores. Data moves between devices by JAX's collectives and lax.ppermute only.
A program may use at most 192 MiB of HBM per device.

```python
import math
import jax
import jax.numpy as jnp
from jax import lax

D = 768
HEADS = 24
FF = 3072
HH = 2048
BOT = 256
PROTO = 65536
WIN_DEV = 64
CROP_DEV = 4
MOST_WIN = 49
TOKENS = 25088
CROPS = 32
N_DP = 8


def crop_row(key):
    rest = WIN_DEV - MOST_WIN
    others = CROP_DEV - 1
    cut_key, place_key = jax.random.split(key)
    if others > 1:
        cuts = jnp.sort(jax.random.permutation(cut_key, rest - 1)[:others - 1].astype(jnp.int32) + 1)
        bounds = jnp.concatenate([jnp.zeros((1,), jnp.int32), cuts, jnp.full((1,), rest, jnp.int32)])
    else:
        bounds = jnp.array([0, rest], jnp.int32)
    parts = (bounds[1:] - bounds[:-1]).astype(jnp.int32)
    place = jax.random.randint(place_key, (), 0, CROP_DEV).astype(jnp.int32)
    slots = jnp.arange(CROP_DEV, dtype=jnp.int32)
    before = parts[jnp.clip(slots, 0, others - 1)]
    after = parts[jnp.clip(slots - 1, 0, others - 1)]
    return jnp.where(slots < place, before, jnp.where(slots == place, MOST_WIN, after)).astype(jnp.int32)


def draw_crop_windows(key, part):
    key = jax.random.fold_in(key, 7)
    keys = jax.random.split(key, N_DP)
    return jax.vmap(crop_row)(keys).astype(jnp.int32)


def touch_ends(drawn, own_key, low, top_value):
    longest = drawn.shape.index(max(drawn.shape))
    spots = []
    for shift in (0, 1):
        where = [jax.random.randint(jax.random.fold_in(own_key, axis), (), 0, length) for axis, length in enumerate(drawn.shape)]
        where[longest] = (where[longest] + shift) % drawn.shape[longest]
        spots.append(tuple(where))
    return drawn.at[spots[0]].set(low).at[spots[1]].set(top_value)


def strengthened(values, rng, source, target, blocks, factor):
    def block_of(axis_at):
        return (jnp.arange(values.shape[axis_at]) // (values.shape[axis_at] // blocks)).reshape((-1,) + (1,) * (values.ndim - 1 - axis_at))

    first = jax.random.permutation(rng, blocks)[block_of(target)]
    second = (block_of(target) + blocks // 2) % blocks
    return jnp.where((block_of(source) == first) | (block_of(source) == second), factor * values, values)


def level_of(own_key, extent, cuts, low, high):
    loudness, own = 1.0, jax.random.fold_in(own_key, 6)
    for position, shards_of in cuts:
        steps = jnp.exp(jax.random.uniform(jax.random.fold_in(own, position), (shards_of,), jnp.float32, low / len(cuts), high / len(cuts)))
        loudness = loudness * jnp.repeat(steps, extent[position] // shards_of).reshape([-1 if axis == position else 1 for axis in range(len(extent))])
    return loudness


def gaussian(stream_key, dims, width, most, cuts=(), kind=jnp.bfloat16):
    factor_of = level_of(stream_key, dims, cuts, -0.22, 0.18) if cuts else 1.0
    values = jax.random.normal(stream_key, dims, jnp.float32) * width * factor_of
    return jnp.minimum(jnp.maximum(values, -most), most).astype(kind)


def noise_with(rng, extent, width, most, shards, heavy, held_as=jnp.bfloat16):
    result = width * jax.random.normal(rng, extent, jnp.float32)
    if shards:
        result = result * level_of(rng, extent, shards, -0.22, 0.18)
    return jnp.clip(strengthened(result, jax.random.fold_in(rng, 3), *heavy), -most, most).astype(held_as)


def setup_inputs(seed: int = 0) -> dict:
    seeds = jax.random.split(jax.random.key(seed), 23)
    tokens = gaussian(seeds[0], (TOKENS, D), 1.0, 6.0, ((0, 32),))
    input_projection = gaussian(seeds[1], (3, D, D), D ** -0.5, 0.21875, ((2, 4),))
    input_bias = gaussian(seeds[2], (2, D), 0.5, 3.0, (), jnp.float32)
    position_bias = gaussian(seeds[3], (169, HEADS), 1.0, 4.0, (), jnp.float32)
    output_projection = gaussian(seeds[4], (D, D), (D // 7) ** -0.5, 0.5, ((0, 4),))
    inner_weight = gaussian(seeds[5], (D, FF), D ** -0.5, 0.21875, ((1, 4),))
    inner_bias = gaussian(seeds[6], (FF,), 0.3, 2.0, (), jnp.float32)
    outer_weight = gaussian(seeds[7], (FF, D), FF ** -0.5, 0.109375, ((0, 4),))
    norm_gains = jnp.clip(1.0 + 0.1 * jax.random.normal(seeds[8], (3, D), jnp.float32), 0.5, 1.5)
    offsets = gaussian(seeds[9], (5, D), 0.3, 2.0, (), jnp.float32)
    head_first = gaussian(seeds[10], (D, HH), D ** -0.5, 0.21875)
    head_first_bias = gaussian(seeds[11], (HH,), 0.3, 2.0, (), jnp.float32)
    head_second = gaussian(seeds[12], (HH, HH), HH ** -0.5, 0.125)
    head_second_bias = gaussian(seeds[13], (HH,), 0.3, 2.0, (), jnp.float32)
    head_third = gaussian(seeds[14], (HH, BOT), HH ** -0.5, 0.125)
    head_third_bias = gaussian(seeds[15], (BOT,), 0.3, 2.0, (), jnp.float32)
    prototype_direction = gaussian(seeds[16], (BOT, PROTO), 1.0, 6.0, ((1, 32),))
    prototype_gain = jnp.clip(jnp.exp(math.log(40.0) - 1.3862944 * jax.random.uniform(seeds[17], (PROTO,), jnp.float32) ** level_of(seeds[17], (PROTO,), ((0, 32),), -0.2, 0.2)), 10.0, 40.0)
    crop_windows = draw_crop_windows(jax.random.fold_in(seeds[22], 71), 0)
    first_epoch = touch_ends((jax.random.randint(seeds[19], (PROTO,), 0, 2) < 1).astype(jnp.int32), jax.random.fold_in(seeds[19], 1), 0, 1)
    feature_cotangent = gaussian(seeds[20], (TOKENS, D), 1.0, 6.0, ((0, 32),))
    logit_cotangent = noise_with(seeds[21], (CROPS, PROTO), 1.0, 6.0, ((1, 32),), (1, 0, 32, 2.75))
    return dict(tokens=tokens, input_projection=input_projection, input_bias=input_bias, position_bias=position_bias, output_projection=output_projection, inner_weight=inner_weight, inner_bias=inner_bias, outer_weight=outer_weight, norm_gains=norm_gains, offsets=offsets, head_first=head_first, head_first_bias=head_first_bias, head_second=head_second, head_second_bias=head_second_bias, head_third=head_third, head_third_bias=head_third_bias, prototype_direction=prototype_direction, prototype_gain=prototype_gain, crop_windows=crop_windows, first_epoch=first_epoch, feature_cotangent=feature_cotangent, logit_cotangent=logit_cotangent)


HIGH = lax.Precision.HIGHEST
window_side = 7

@jax.custom_vjp
def low(v):
    return lax.optimization_barrier(v.astype(jnp.bfloat16)).astype(jnp.float32)

@jax.custom_vjp
def low_back(v):
    return v

def low_keep(v):
    return (low(v), None)

def low_pass(kept, grad):
    return (grad,)

def back_keep(v):
    return (v, None)

def back_low(kept, grad):
    return (low(grad),)
low.defvjp(low_keep, low_pass)
low_back.defvjp(back_keep, back_low)

def layer_norm(values, gain, shift):
    center = values - lax.optimization_barrier(jnp.mean(values, axis=-1, keepdims=True))
    spread = lax.optimization_barrier(jnp.mean(center * center, axis=-1, keepdims=True))
    return center * lax.rsqrt(spread + 1e-05) * gain + shift

def gelu_exact(values):
    return jax.nn.gelu(values, approximate=False)

def normalize_rows(values):
    return values * lax.rsqrt(lax.optimization_barrier(jnp.sum(values * values, axis=-1, keepdims=True)) + 1e-06)

def offset_table():
    places = jnp.arange(window_side * window_side, dtype=jnp.int32)
    row_of = places // window_side
    col_of = places % window_side
    offset = (row_of[:, None] - row_of[None, :] + window_side - 1) * (2 * window_side - 1) + (col_of[:, None] - col_of[None, :] + window_side - 1)
    entries = jnp.arange((2 * window_side - 1) ** 2, dtype=jnp.int32)
    return (offset.reshape(-1)[:, None] == entries[None, :]).astype(jnp.float32)

def product(left, right):
    return jnp.dot(left, right, precision=HIGH, preferred_element_type=jnp.float32)

def window_attention(query_rows, key_rows, value_rows, pair_bias):
    scale = query_rows.shape[-1] ** (-0.5)
    scores = jnp.einsum('wihd,wjhd->whij', query_rows, key_rows, precision=HIGH) * scale + pair_bias
    scores = low_back(scores)
    weights = low(jax.nn.softmax(scores, axis=-1))
    return jnp.einsum('whij,wjhd->wihd', weights, value_rows, precision=HIGH)

def forward(tokens, input_projection, input_bias, position_bias, output_projection, inner_weight, inner_bias, outer_weight, norm_gains, offsets, head_first, head_first_bias, head_second, head_second_bias, head_third, head_third_bias, prototype_direction, prototype_gain, crop_of_token, crop_tokens):
    count = tokens.shape[0]
    heads = position_bias.shape[1]
    normed_one = low(layer_norm(tokens, norm_gains[0], offsets[0]))
    query_rows = low(low_back(product(normed_one, input_projection[0]) + input_bias[0]))
    key_rows = low(low_back(product(normed_one, input_projection[1])))
    value_rows = low(low_back(product(normed_one, input_projection[2]) + input_bias[1]))
    pair_bias = product(offset_table(), position_bias).T.reshape(heads, 49, 49)

    def grouped(values):
        return values.reshape(N_DP, WIN_DEV, 49, heads, D // heads)

    def attend_group(triple):
        return window_attention(triple[0], triple[1], triple[2], pair_bias)
    attended = lax.map(jax.checkpoint(attend_group), (grouped(query_rows), grouped(key_rows), grouped(value_rows)))
    attended = low(low_back(attended.reshape(count, D)))
    mixed = tokens + low_back(product(attended, output_projection)) + offsets[1]
    normed_two = low(layer_norm(mixed, norm_gains[1], offsets[2]))
    inner_pre = low_back(product(normed_two, inner_weight) + inner_bias)
    inner_act = low(gelu_exact(inner_pre))
    block_out = mixed + low_back(product(inner_act, outer_weight)) + offsets[3]
    normed_head = layer_norm(block_out, norm_gains[2], offsets[4])
    pooled = jax.ops.segment_sum(normed_head, crop_of_token, num_segments=CROPS) / crop_tokens[:, None]
    pooled = low(pooled)
    first_pre = low_back(product(pooled, head_first) + head_first_bias)
    first_act = low(gelu_exact(first_pre))
    second_pre = low_back(product(first_act, head_second) + head_second_bias)
    second_act = low(gelu_exact(second_pre))
    embedded = low_back(product(second_act, head_third)) + head_third_bias
    units = low(normalize_rows(embedded))
    column_scale = lax.rsqrt(lax.optimization_barrier(jnp.sum(prototype_direction * prototype_direction, axis=0, keepdims=True)) + 1e-06)
    columns = low(prototype_gain * prototype_direction * column_scale)
    logits = product(units, columns)
    return (block_out, logits)

def reference(tokens, input_projection, input_bias, position_bias, output_projection, inner_weight, inner_bias, outer_weight, norm_gains, offsets, head_first, head_first_bias, head_second, head_second_bias, head_third, head_third_bias, prototype_direction, prototype_gain, crop_windows, first_epoch, feature_cotangent, logit_cotangent):
    ends = jnp.cumsum(crop_windows, axis=1).astype(jnp.int32)
    window_ids = jnp.arange(WIN_DEV, dtype=jnp.int32)
    local_crop = lax.optimization_barrier(jnp.sum((window_ids[None, :, None] >= ends[:, None, :]).astype(jnp.int32), axis=2)).astype(jnp.int32)
    crop_of_window = local_crop + (jnp.arange(N_DP, dtype=jnp.int32) * CROP_DEV)[:, None]
    crop_of_token = jnp.repeat(crop_of_window.reshape(-1), 49).astype(jnp.int32)
    crop_tokens = (crop_windows.reshape(-1) * 49).astype(jnp.float32)
    floats = tuple((item.astype(jnp.float32) for item in (tokens, input_projection, input_bias, position_bias, output_projection, inner_weight, inner_bias, outer_weight, norm_gains, offsets, head_first, head_first_bias, head_second, head_second_bias, head_third, head_third_bias, prototype_direction, prototype_gain)))

    def wrapped(*params):
        return forward(*params, crop_of_token, crop_tokens)
    outputs, back = jax.vjp(wrapped, *floats)
    grads = back((feature_cotangent.astype(jnp.float32), logit_cotangent.astype(jnp.float32)))
    keep = (1 - first_epoch).astype(jnp.float32)
    return (outputs[0].astype(jnp.bfloat16), outputs[1], grads[0], grads[1], grads[2], grads[3], grads[4], grads[5], grads[6], grads[7], grads[8], grads[9], grads[10], grads[11], grads[12], grads[13], grads[14], grads[15], grads[16] * keep[None, :], grads[17] * keep)
```

```python
import functools

import jax
import jax.numpy as jnp
from jax import lax
from jax.experimental import pallas as pl
from jax.experimental.pallas import tpu as pltpu
from jax.sharding import PartitionSpec as P

HIGH = lax.Precision.HIGHEST
F32 = jnp.float32
BF16 = jnp.bfloat16
SIDE = 7
SPOTS = SIDE * SIDE
PAD = 64
VMEM_LIMIT = 60 * 1024 * 1024
NEG = -1e30


def dot(left, right):
    return jnp.dot(left, right, preferred_element_type=F32)


def dot_left(left, right):
    return lax.dot_general(left, right, (((0,), (0,)), ((), ())), preferred_element_type=F32)


def dot_right(left, right):
    return lax.dot_general(left, right, (((1,), (1,)), ((), ())), preferred_element_type=F32)


def call(body, outs, ins, **kw):
    scratch = kw.pop("scratch", ())
    return pl.pallas_call(
        body,
        out_shape=outs,
        in_specs=[pl.BlockSpec(memory_space=pltpu.VMEM)] * len(ins),
        out_specs=jax.tree.map(lambda _: pl.BlockSpec(memory_space=pltpu.VMEM), outs),
        scratch_shapes=scratch,
        compiler_params=pltpu.CompilerParams(vmem_limit_bytes=VMEM_LIMIT),
        **kw,
    )(*ins)


def shape(dims, kind):
    return jax.ShapeDtypeStruct(dims, kind)


def norm_parts(values):
    center = values - jnp.mean(values, axis=-1, keepdims=True)
    spread = jnp.mean(center * center, axis=-1, keepdims=True)
    inv = lax.rsqrt(spread + 1e-05)
    return center * inv, inv


def norm_back(nhat, inv, gain, grad):
    scaled = grad * gain
    first = jnp.mean(scaled, axis=-1, keepdims=True)
    second = jnp.mean(scaled * nhat, axis=-1, keepdims=True)
    return (scaled - first - nhat * second) * inv


def gelu_pair(pre):
    bell = jnp.exp(pre * pre * -0.5)
    dist = jnp.abs(pre) * (0.3275911 * 0.70710678118654752) + 1.0
    inv = 1.0 / dist
    poly = 0.5 * 1.061405429
    for coef in (-1.453152027, 1.421413741, -0.284496736, 0.254829592):
        poly = poly * inv + 0.5 * coef
    tail = poly * inv * bell
    cdf = jnp.where(pre < 0.0, tail, 1.0 - tail)
    return pre * cdf, cdf + pre * (bell * 0.3989422804014327)


def norm_one_body(windows, tokens, gain, shift, padded, flat):
    rows = tokens.shape[0]
    step = 112
    for r in range(0, rows, step):
        nhat, _ = norm_parts(tokens[r : r + step, :].astype(F32))
        flat[r : r + step, :] = nhat * gain[...] + shift[...]
    place = lax.broadcasted_iota(jnp.int32, (PAD, 1), 0)
    for w in range(windows):
        block = flat[w * SPOTS : w * SPOTS + PAD, :]
        padded[w * PAD : (w + 1) * PAD, :] = jnp.where(place < SPOTS, block, 0.0).astype(BF16)


def head_masks(heads, size):
    lane = lax.broadcasted_iota(jnp.int32, (PAD, heads * size), 1) // size
    return [lane == h for h in range(heads)]


def spread_heads(values, masks):
    zero = jnp.zeros_like(values)
    return jnp.concatenate([jnp.where(m, values, zero) for m in masks], axis=0)


def fold_heads(values, masks):
    total = values[0:PAD, :]
    for h in range(1, len(masks)):
        total = jnp.where(masks[h], values[h * PAD : (h + 1) * PAD, :], total)
    return total


def attend_body(heads, scale, padded, weight, bias, table, q_out, k_out, v_out, p_out, att_out):
    rows, width = q_out.shape
    size = width // heads
    x = padded[...]
    q_out[...] = (dot(x, weight[0]) + bias[0:1, :]).astype(BF16)
    k_out[...] = dot(x, weight[1]).astype(BF16)
    v_out[...] = (dot(x, weight[2]) + bias[1:2, :]).astype(BF16)
    masks = head_masks(heads, size)

    def window(w, carry):
        here = pl.ds(pl.multiple_of(w * PAD, PAD), PAD)
        spread = spread_heads(q_out[here, :], masks)
        scores = dot_right(k_out[here, :], spread) * scale + table[...]
        top = jnp.max(scores, axis=0, keepdims=True)
        e = jnp.exp(scores - top)
        probs = (e * (1.0 / jnp.sum(e, axis=0, keepdims=True))).astype(BF16)
        p_out[here, :] = probs
        att_out[here, :] = fold_heads(dot_left(probs, v_out[here, :]), masks).astype(BF16)
        return carry

    lax.fori_loop(0, rows // PAD, window, 0, unroll=4)


def attend_back_body(
    heads, scale, low, weight, q_in, k_in, v_in, p_in, d_out, table_out, sums_out, given
):
    rows, width = q_in.shape
    size = width // heads
    given[...] = dot_right(low[...], weight[...]).astype(BF16)
    masks = head_masks(heads, size)
    table_out[...] = jnp.zeros_like(table_out)

    def window(w, carry):
        here = pl.ds(pl.multiple_of(w * PAD, PAD), PAD)
        qs = spread_heads(q_in[here, :], masks)
        gs = spread_heads(given[here, :], masks)
        probs_low = p_in[here, :]
        probs = probs_low.astype(F32)
        prob_grad = dot_right(v_in[here, :], gs)
        mean = jnp.sum(probs * prob_grad, axis=0, keepdims=True)
        score_low = (probs * (prob_grad - mean)).astype(BF16)
        table_out[...] += score_low.astype(F32)
        dq = (fold_heads(dot_left(score_low, k_in[here, :]), masks) * scale).astype(BF16)
        dk = (dot(score_low, qs) * scale).astype(BF16)
        dv = dot(probs_low, gs).astype(BF16)
        d_out[here, 0:width] = dq
        d_out[here, width : 2 * width] = dk
        d_out[here, 2 * width : 3 * width] = dv
        return carry

    lax.fori_loop(0, rows // PAD, window, 0, unroll=4)
    sums_out[...] = jnp.sum(d_out[...].astype(F32), axis=0, keepdims=True)


def mixed_body(windows, count, *refs):
    att, wo = refs[:count], refs[count : 2 * count]
    tokens, vecs, mixed, normed = refs[2 * count :]
    for w in range(windows):
        here = slice(w * PAD, (w + 1) * PAD)
        total = dot(att[0][here, :], wo[0][...])
        for k in range(1, count):
            total = total + dot(att[k][here, :], wo[k][...])
        mixed[w * SPOTS : (w + 1) * SPOTS, :] = total[0:SPOTS, :]
    step = 112
    for r in range(0, tokens.shape[0], step):
        rows = slice(r, r + step)
        value = tokens[rows, :].astype(F32) + mixed[rows, :] + vecs[0:1, :]
        mixed[rows, :] = value
        nhat, _ = norm_parts(value)
        normed[rows, :] = (nhat * vecs[1:2, :] + vecs[2:3, :]).astype(BF16)


def inner_body(blocks, count, *refs):
    normed, mixed, bias = refs[:3]
    wi, wo = refs[3 : 3 + count], refs[3 + count : 3 + 2 * count]
    vecs, crop, act_out, slope_out, block_out, features, pool, total = refs[3 + 2 * count :]
    step = pl.program_id(0)

    @pl.when(step == 0)
    def _():
        total[...] = jnp.zeros_like(total)

    for k in range(count):

        @pl.when(step // blocks == k)
        def _(k=k):
            pre = dot(normed[...], wi[k][...]) + bias[0]
            act, slope = gelu_pair(pre)
            act = act.astype(BF16)
            act_out[...] = act
            slope_out[...] = slope.astype(BF16)
            total[...] += dot(act, wo[k][...])

    @pl.when(step == blocks * count - 1)
    def _():
        crops = pool.shape[0]
        sums = [jnp.zeros((1, total.shape[1]), F32)] * crops
        rows_step = 112
        for r in range(0, total.shape[0], rows_step):
            rows = slice(r, r + rows_step)
            value = mixed[rows, :] + total[rows, :] + vecs[0:1, :]
            block_out[rows, :] = value
            features[rows, :] = value.astype(BF16)
            nhat, _ = norm_parts(value)
            head = nhat * vecs[1:2, :] + vecs[2:3, :]
            for c in range(crops):
                sums[c] = sums[c] + jnp.sum(
                    jnp.where(crop[rows, :] == c, head, 0.0), axis=0, keepdims=True
                )
        for c in range(crops):
            pool[c : c + 1, :] = sums[c]


def head_back_body(block_out, cotangent, crop, pooled_grad, gain, grad_out, low_out, sums_out):
    crops = pooled_grad.shape[0]
    step = 112
    gain_sum = jnp.zeros((1, block_out.shape[1]), F32)
    shift_sum = gain_sum
    bias_sum = gain_sum
    for r in range(0, block_out.shape[0], step):
        rows = slice(r, r + step)
        nhat, inv = norm_parts(block_out[rows, :])
        grad = jnp.zeros(nhat.shape, F32)
        for c in range(crops):
            grad = jnp.where(crop[rows, :] == c, pooled_grad[c : c + 1, :], grad)
        gain_sum = gain_sum + jnp.sum(grad * nhat, axis=0, keepdims=True)
        shift_sum = shift_sum + jnp.sum(grad, axis=0, keepdims=True)
        out = cotangent[rows, :].astype(F32) + norm_back(nhat, inv, gain[...], grad)
        bias_sum = bias_sum + jnp.sum(out, axis=0, keepdims=True)
        grad_out[rows, :] = out
        low_out[rows, :] = out.astype(BF16)
    sums_out[0:1, :] = gain_sum
    sums_out[1:2, :] = shift_sum
    sums_out[2:3, :] = bias_sum


def mixed_back_body(windows, mixed, out_grad, normed_grad, gain, grad_out, low_out, sums_out, flat):
    rows_all = mixed.shape[0]
    step = 112
    gain_sum = jnp.zeros((1, mixed.shape[1]), F32)
    shift_sum = gain_sum
    bias_sum = gain_sum
    for r in range(0, rows_all, step):
        rows = slice(r, r + step)
        nhat, inv = norm_parts(mixed[rows, :])
        grad = normed_grad[rows, :]
        gain_sum = gain_sum + jnp.sum(grad * nhat, axis=0, keepdims=True)
        shift_sum = shift_sum + jnp.sum(grad, axis=0, keepdims=True)
        out = out_grad[rows, :] + norm_back(nhat, inv, gain[...], grad)
        bias_sum = bias_sum + jnp.sum(out, axis=0, keepdims=True)
        grad_out[rows, :] = out
        flat[rows, :] = out
    sums_out[0:1, :] = gain_sum
    sums_out[1:2, :] = shift_sum
    sums_out[2:3, :] = bias_sum
    place = lax.broadcasted_iota(jnp.int32, (PAD, 1), 0)
    for w in range(windows):
        block = flat[w * SPOTS : w * SPOTS + PAD, :]
        low_out[w * PAD : (w + 1) * PAD, :] = jnp.where(place < SPOTS, block, 0.0).astype(BF16)


def tokens_back_body(windows, count, *refs):
    grads, weights = refs[:count], refs[count : 2 * count]
    tokens, mixed_grad, gain, grad_out, sums_out, flat = refs[2 * count :]
    width = weights[0].shape[2]
    for w in range(windows):
        here = slice(w * PAD, (w + 1) * PAD)
        total = jnp.zeros((PAD, tokens.shape[1]), F32)
        for k in range(count):
            for part in range(3):
                total = total + dot_right(
                    grads[k][here, part * width : (part + 1) * width], weights[k][part]
                )
        flat[w * SPOTS : (w + 1) * SPOTS, :] = total[0:SPOTS, :]
    step = 112
    gain_sum = jnp.zeros((1, tokens.shape[1]), F32)
    shift_sum = gain_sum
    for r in range(0, tokens.shape[0], step):
        rows = slice(r, r + step)
        nhat, inv = norm_parts(tokens[rows, :].astype(F32))
        grad = flat[rows, :]
        gain_sum = gain_sum + jnp.sum(grad * nhat, axis=0, keepdims=True)
        shift_sum = shift_sum + jnp.sum(grad, axis=0, keepdims=True)
        grad_out[rows, :] = mixed_grad[rows, :] + norm_back(nhat, inv, gain[...], grad)
    sums_out[0:1, :] = gain_sum
    sums_out[1:2, :] = shift_sum


def swap(values, axis, bit):
    return lax.ppermute(values, axis, [(i, i ^ bit) for i in range(lax.axis_size(axis))])


def bits_of(axis):
    size = lax.axis_size(axis)
    bit, found = 1, []
    while bit < size:
        found.append(bit)
        bit *= 2
    return found


def has_bit(axis, bit):
    return (lax.axis_index(axis) // bit) % 2 == 1


def sum_over(values, axes):
    for axis in axes:
        for bit in bits_of(axis):
            values = values + swap(values, axis, bit)
    return values


def gather_over(values, axis):
    for bit in bits_of(axis):
        other = swap(values, axis, bit)
        upper = has_bit(axis, bit)
        values = jnp.concatenate(
            [jnp.where(upper, other, values), jnp.where(upper, values, other)], axis=0
        )
    return values


def by_distance(values, axis):
    for bit in bits_of(axis):
        size = values.shape[0]
        folded = values.reshape(size // (2 * bit), 2, bit, *values.shape[1:])
        folded = jnp.where(has_bit(axis, bit), folded[:, ::-1], folded)
        values = folded.reshape(values.shape)
    return values


def gathered(weight):
    found = [weight]
    for bit in bits_of("narrow"):
        found = found + [swap(w, "narrow", bit) for w in found]
    return found


def halve_rows(values, bit, low):
    groups, rows, columns = values.shape
    folded = values.reshape(groups // 2, 2, rows, columns)
    mine = lax.axis_index("dp") // bit % 2
    keep = lax.dynamic_index_in_dim(folded, mine, 1, keepdims=False)
    send = lax.dynamic_index_in_dim(folded, 1 - mine, 1, keepdims=False).astype(low)
    return keep, send


def scatter_sum(parts, row_first):
    groups = lax.axis_size("dp")
    parts = [p.reshape(groups, p.shape[0] // groups, p.shape[1]) for p in parts]
    narrow_bits = bits_of("narrow")
    dp_bits = bits_of("dp")

    def over_narrow(parts, bit):
        kept = [p for k, p in enumerate(parts) if not k & bit]
        sent = [p for k, p in enumerate(parts) if k & bit]
        return [a.astype(F32) + swap(b.astype(BF16), "narrow", bit).astype(F32) for a, b in zip(kept, sent)]

    def over_dp(parts, bit):
        done = []
        for p in parts:
            keep, send = halve_rows(p, bit, BF16)
            done.append(keep.astype(F32) + swap(send, "dp", bit).astype(F32))
        return done

    parts = [p for p in parts]
    def drop(parts):
        kept = parts[0::2]
        sent = parts[1::2]
        return kept, sent

    steps = [("narrow", b) for b in narrow_bits] + [("dp", b) for b in dp_bits]
    if row_first:
        steps = (
            [("narrow", narrow_bits[0]), ("dp", dp_bits[0])]
            + [("narrow", b) for b in narrow_bits[1:]]
            + [("dp", b) for b in dp_bits[1:]]
        )
    for axis, bit in steps:
        if axis == "narrow":
            kept, sent = drop(parts)
            parts = [
                a.astype(F32) + swap(b.astype(BF16), "narrow", bit).astype(F32)
                for a, b in zip(kept, sent)
            ]
        else:
            parts = over_dp(parts, bit)
    return parts[0].reshape(parts[0].shape[1:])


def gelu_exact(values):
    return jax.nn.gelu(values, approximate=False)


def gelu_back(pre, cotangent):
    return jax.vjp(gelu_exact, pre)[1](cotangent)[0]


def normalize_rows(values):
    return values * lax.rsqrt(jnp.sum(values * values, axis=-1, keepdims=True) + 1e-06)


def offset_table():
    places = jnp.arange(PAD, dtype=jnp.int32)
    row_of = places // SIDE
    col_of = places % SIDE
    offset = (row_of[None, :] - row_of[:, None] + SIDE - 1) * (2 * SIDE - 1) + (
        col_of[None, :] - col_of[:, None] + SIDE - 1
    )
    inside = (places[:, None] < SPOTS) & (places[None, :] < SPOTS)
    offset = jnp.where(inside, offset, -1)
    entries = jnp.arange((2 * SIDE - 1) ** 2, dtype=jnp.int32)
    return (offset.reshape(-1)[:, None] == entries[None, :]).astype(F32)


def shards(
    tokens,
    input_projection,
    input_bias,
    position_bias,
    output_projection,
    inner_weight,
    inner_bias,
    outer_weight,
    norm_gains,
    offsets,
    head_first,
    head_first_bias,
    head_second,
    head_second_bias,
    head_third,
    head_third_bias,
    prototype_direction,
    prototype_gain,
    crop_windows,
    first_epoch,
    feature_cotangent,
    logit_cotangent,
):
    rows, width = tokens.shape
    windows = rows // SPOTS
    narrow_index = lax.axis_index("narrow")
    dp_index = lax.axis_index("dp")
    count = lax.axis_size("narrow")
    groups = lax.axis_size("dp")
    quarter = input_projection.shape[2]
    hidden = inner_weight.shape[1]
    heads = position_bias.shape[1] // count
    size = quarter // heads
    scale = size ** (-0.5)
    crops = crop_windows.shape[1]
    padded_rows = windows * PAD

    w_in = gathered(input_projection)
    w_att = gathered(output_projection)
    w_inner = gathered(inner_weight)
    w_outer = gathered(outer_weight)

    direction = prototype_direction.astype(F32)
    column_inv = lax.rsqrt(jnp.sum(direction * direction, axis=0, keepdims=True) + 1e-06)
    columns_low = (prototype_gain * direction * column_inv).astype(BF16)
    unit_grad = sum_over(dot_right(logit_cotangent, columns_low), ("narrow", "dp"))

    bias_in = by_distance(input_bias.reshape(2, count, quarter).swapaxes(0, 1), "narrow")
    bias_inner = by_distance(inner_bias.reshape(count, 1, hidden), "narrow")
    table = offset_table()
    spread = jnp.dot(table, position_bias, precision=HIGH, preferred_element_type=F32)
    spread = spread.reshape(PAD, PAD, count, heads).transpose(2, 0, 3, 1)
    inside = (jnp.arange(PAD) < SPOTS)[None, :, None, None]
    spread = jnp.where(inside, spread, NEG).reshape(count, PAD, heads * PAD)
    spread = by_distance(spread, "narrow")

    ends = jnp.cumsum(crop_windows[0])
    row_window = narrow_index * windows + jnp.arange(rows, dtype=jnp.int32) // SPOTS
    crop_of_row = jnp.sum((row_window[:, None] >= ends[None, :]).astype(jnp.int32), axis=1, keepdims=True)
    crop_tokens = (crop_windows[0] * SPOTS).astype(F32)

    gains = norm_gains.reshape(3, 1, width)
    padded = call(
        functools.partial(norm_one_body, windows),
        shape((padded_rows, width), BF16),
        (tokens, norm_gains[0:1], offsets[0:1]),
        scratch=[pltpu.VMEM((rows + 16, width), F32)],
    )
    q, k_, v, probs, attended = [], [], [], [], []
    for k in range(count):
        got = call(
            functools.partial(attend_body, heads, scale),
            (
                shape((padded_rows, quarter), BF16),
                shape((padded_rows, quarter), BF16),
                shape((padded_rows, quarter), BF16),
                shape((padded_rows, heads * PAD), BF16),
                shape((padded_rows, quarter), BF16),
            ),
            (padded, w_in[k], bias_in[k], spread[k]),
        )
        for keep, value in zip((q, k_, v, probs, attended), got):
            keep.append(value)
    mixed, normed_two = call(
        functools.partial(mixed_body, windows, count),
        (shape((rows, width), F32), shape((rows, width), BF16)),
        (*attended, *w_att, tokens, jnp.concatenate([offsets[1:2], norm_gains[1:2], offsets[2:3]])),
    )
    blocks = 3
    block = hidden // blocks
    steps = blocks * count

    def block_at(k, column):
        def index(s):
            b = jnp.clip(s - k * blocks, 0, blocks - 1)
            return (0, b) if column else (b, 0)

        return index

    whole = lambda s: (0, 0)
    act, slope, block_out, features, pool = pl.pallas_call(
        functools.partial(inner_body, blocks, count),
        grid=(steps,),
        out_shape=(
            shape((rows, hidden * count), BF16),
            shape((rows, hidden * count), BF16),
            shape((rows, width), F32),
            shape((rows, width), BF16),
            shape((crops, width), F32),
        ),
        in_specs=[
            pl.BlockSpec((rows, width), whole),
            pl.BlockSpec((rows, width), whole),
            pl.BlockSpec((1, 1, block), lambda s: (s // blocks, 0, s % blocks)),
            *[pl.BlockSpec((width, block), block_at(k, True)) for k in range(count)],
            *[pl.BlockSpec((block, width), block_at(k, False)) for k in range(count)],
            pl.BlockSpec((3, width), whole),
            pl.BlockSpec((rows, 1), whole),
        ],
        out_specs=(
            pl.BlockSpec((rows, block), lambda s: (0, s)),
            pl.BlockSpec((rows, block), lambda s: (0, s)),
            pl.BlockSpec((rows, width), whole),
            pl.BlockSpec((rows, width), whole),
            pl.BlockSpec((crops, width), whole),
        ),
        scratch_shapes=[pltpu.VMEM((rows, width), F32)],
        compiler_params=pltpu.CompilerParams(vmem_limit_bytes=VMEM_LIMIT),
    )(
        normed_two,
        mixed,
        bias_inner,
        *w_inner,
        *w_outer,
        jnp.concatenate([offsets[3:4], norm_gains[2:3], offsets[4:5]]),
        crop_of_row,
    )

    pooled_own = (sum_over(pool, ("narrow",)) / crop_tokens[:, None]).astype(BF16)
    pooled = gather_over(pooled_own, "dp")
    first_pre = dot(pooled, head_first) + head_first_bias
    first_act = gelu_exact(first_pre).astype(BF16)
    second_pre = dot(first_act, head_second) + head_second_bias
    second_act = gelu_exact(second_pre).astype(BF16)
    embedded = dot(second_act, head_third) + head_third_bias
    units = normalize_rows(embedded).astype(BF16)
    embed_grad = jax.vjp(normalize_rows, embedded)[1](unit_grad)[0]
    embed_low = embed_grad.astype(BF16)
    second_low = gelu_back(second_pre, dot_right(embed_low, head_third)).astype(BF16)
    first_low = gelu_back(first_pre, dot_right(second_low, head_second)).astype(BF16)
    own_low = lax.dynamic_slice_in_dim(first_low, dp_index * crops, crops, 0)
    pooled_grad = dot_right(own_low, head_first) / crop_tokens[:, None]

    out_grad, out_low, head_sums = call(
        head_back_body,
        (shape((rows, width), F32), shape((rows, width), BF16), shape((3, width), F32)),
        (block_out, feature_cotangent, crop_of_row, pooled_grad, norm_gains[2:3]),
    )
    normed_two_grad = None
    inner_parts, outer_parts, inner_sums = [None] * count, [None] * count, [None] * count
    order = [k for k in range(count) if k % 2] + [k for k in range(count) if not k % 2]
    for k in order:
        here = slice(k * hidden, (k + 1) * hidden)
        act_k, slope_k = act[:, here], slope[:, here]
        pre_grad = (dot_right(out_low, w_outer[k]) * slope_k.astype(F32)).astype(BF16)
        kind = BF16 if k % 2 else F32
        outer_parts[k] = dot_left(out_low, act_k).astype(kind)
        inner_parts[k] = dot_left(normed_two, pre_grad).astype(kind)
        inner_sums[k] = jnp.sum(pre_grad.astype(F32), axis=0)
        share = dot_right(pre_grad, w_inner[k])
        normed_two_grad = share if normed_two_grad is None else normed_two_grad + share
    outer_sum = scatter_sum(outer_parts, True)
    inner_sum = scatter_sum(inner_parts, False)
    mixed_grad, mixed_low, mixed_sums = call(
        functools.partial(mixed_back_body, windows),
        (shape((rows, width), F32), shape((padded_rows, width), BF16), shape((3, width), F32)),
        (mixed, out_grad, normed_two_grad, norm_gains[1:2]),
        scratch=[pltpu.VMEM((rows + 16, width), F32)],
    )
    input_grads, pair_grads, input_sums = [None] * count, [None] * count, [None] * count
    attend_parts, input_parts = [None] * count, [None] * count
    for k in order:
        input_grads[k], pair_grads[k], input_sums[k] = call(
            functools.partial(attend_back_body, heads, scale),
            (
                shape((padded_rows, 3 * quarter), BF16),
                shape((PAD, heads * PAD), F32),
                shape((1, 3 * quarter), F32),
            ),
            (mixed_low, w_att[k], q[k], k_[k], v[k], probs[k]),
            scratch=[pltpu.VMEM((padded_rows, quarter), BF16)],
        )
        kind = BF16 if k % 2 else F32
        attend_parts[k] = dot_left(mixed_low, attended[k]).astype(kind)
        input_parts[k] = dot_left(padded, input_grads[k]).astype(kind)
    joined = [jnp.concatenate([a, b], axis=1) for a, b in zip(input_parts, attend_parts)]
    joined_sum = scatter_sum(joined, False)
    tokens_grad, token_sums = call(
        functools.partial(tokens_back_body, windows, count),
        (shape((rows, width), F32), shape((2, width), F32)),
        (*input_grads, *w_in, tokens, mixed_grad, norm_gains[0:1]),
        scratch=[pltpu.VMEM((rows, width), F32)],
    )

    pair_grad = jnp.stack(pair_grads).reshape(count, PAD, heads, PAD)
    pair_grad = by_distance(pair_grad, "narrow").transpose(1, 3, 0, 2).reshape(PAD * PAD, count * heads)
    table_grad = lax.dot_general(
        table, pair_grad, (((0,), (0,)), ((), ())), precision=HIGH, preferred_element_type=F32
    )
    input_sum = by_distance(jnp.stack(input_sums).reshape(count, 3, quarter), "narrow")
    input_sum = input_sum.swapaxes(0, 1).reshape(3, count * quarter)
    inner_bias_sum = by_distance(jnp.stack(inner_sums), "narrow")
    pieces = [
        token_sums[0:1], mixed_sums[0:1], head_sums[0:1],
        token_sums[1:2], mixed_sums[2:3], mixed_sums[1:2], head_sums[2:3], head_sums[1:2],
        input_sum[0:1], input_sum[2:3],
        inner_bias_sum, table_grad,
    ]
    flat = jnp.concatenate([p.reshape(-1) for p in pieces])
    small = sum_over(flat, ("narrow", "dp"))
    gain_total = small[: 3 * width].reshape(3, width)
    offset_total = small[3 * width : 8 * width].reshape(5, width)
    bias_total = small[8 * width : 10 * width].reshape(2, width)
    inner_total = small[10 * width : 10 * width + hidden * count]
    table_total = small[10 * width + hidden * count :].reshape(table_grad.shape)

    logits = dot(units, columns_low)
    column_grad = dot_left(units, logit_cotangent)
    keep = (1 - first_epoch).astype(F32)[None, :]
    along = jnp.sum(column_grad * direction, axis=0, keepdims=True)
    gain_grad = (keep * column_inv * along)[0]
    direction_grad = (keep * prototype_gain) * (
        column_inv * column_grad - (column_inv**3 * along) * direction
    )

    def own(values):
        share = values.shape[1] // groups
        return lax.dynamic_slice_in_dim(values, dp_index * share, share, 1)

    own_first, own_second = own(first_low), own(second_low)
    own_embed = own(embed_grad)

    attend_sum = joined_sum[:, 3 * quarter :]
    input_total = jnp.stack([joined_sum[:, i * quarter : (i + 1) * quarter] for i in range(3)])
    return (
        features,
        logits,
        tokens_grad,
        input_total,
        bias_total,
        table_total,
        attend_sum.T,
        inner_sum,
        inner_total,
        outer_sum.T,
        gain_total,
        offset_total,
        dot_left(pooled, own_first),
        jnp.sum(own_first.astype(F32), axis=0),
        dot_left(first_act, own_second),
        jnp.sum(own_second.astype(F32), axis=0),
        dot_left(own(second_act), embed_low),
        jnp.sum(own_embed, axis=0),
        direction_grad,
        gain_grad,
    )


def solution(mesh):
    placed = (
        P(("dp", "narrow"), None),
        P(None, None, "narrow"),
        P(),
        P(),
        P("narrow", None),
        P(None, "narrow"),
        P(),
        P("narrow", None),
        P(),
        P(),
        P(),
        P(),
        P(),
        P(),
        P(),
        P(),
        P(None, ("dp", "narrow")),
        P(("dp", "narrow")),
        P("dp", None),
        P(("dp", "narrow")),
        P(("dp", "narrow"), None),
        P(None, ("dp", "narrow")),
    )
    return jax.shard_map(
        shards,
        mesh=mesh,
        in_specs=placed,
        out_specs=(
            P(("dp", "narrow"), None),
            P(None, ("dp", "narrow")),
            P(("dp", "narrow"), None),
            P(None, "dp", "narrow"),
            P(),
            P(),
            P("narrow", "dp"),
            P("dp", "narrow"),
            P(),
            P("narrow", "dp"),
            P(),
            P(),
            P(None, "dp"),
            P("dp"),
            P(None, "dp"),
            P("dp"),
            P("dp", None),
            P("dp"),
            P(None, ("dp", "narrow")),
            P(("dp", "narrow")),
        ),
        check_vma=False,
    )
```

```python
import functools

import jax
import jax.numpy as jnp
from jax import lax
from jax.experimental import pallas as pl
from jax.experimental.pallas import tpu as pltpu
from jax.sharding import PartitionSpec as P

HIGH = lax.Precision.HIGHEST
F32 = jnp.float32
BF16 = jnp.bfloat16
SIDE = 7
SPOTS = SIDE * SIDE
PAD = 64
LANES = 128
CHUNK = 112
VMEM_LIMIT = 60 * 1024 * 1024
NEG = -1e30


def dot(left, right):
    return jnp.dot(left, right, preferred_element_type=F32)


def dot_left(left, right):
    return lax.dot_general(left, right, (((0,), (0,)), ((), ())), preferred_element_type=F32)


def dot_right(left, right):
    return lax.dot_general(left, right, (((1,), (1,)), ((), ())), preferred_element_type=F32)


def cost(us):
    return pl.CostEstimate(flops=0, bytes_accessed=int(us * 3.3e6), transcendentals=0)


def call(body, outs, ins, **kw):
    scratch = kw.pop("scratch", ())
    return pl.pallas_call(
        body,
        out_shape=outs,
        in_specs=[pl.BlockSpec(memory_space=pltpu.VMEM)] * len(ins),
        out_specs=jax.tree.map(lambda _: pl.BlockSpec(memory_space=pltpu.VMEM), outs),
        scratch_shapes=scratch,
        compiler_params=pltpu.CompilerParams(vmem_limit_bytes=VMEM_LIMIT),
        cost_estimate=cost(kw.pop("us")),
        **kw,
    )(*ins)


def shape(dims, kind):
    return jax.ShapeDtypeStruct(dims, kind)


def norm_parts(values):
    center = values - jnp.mean(values, axis=-1, keepdims=True)
    spread = jnp.mean(center * center, axis=-1, keepdims=True)
    inv = lax.rsqrt(spread + 1e-05)
    return center * inv, inv


def norm_back(nhat, inv, gain, grad):
    scaled = grad * gain
    first = jnp.mean(scaled, axis=-1, keepdims=True)
    second = jnp.mean(scaled * nhat, axis=-1, keepdims=True)
    return (scaled - first - nhat * second) * inv


def gelu_pair(pre):
    bell = jnp.exp(pre * pre * -0.5)
    dist = jnp.abs(pre) * (0.3275911 * 0.70710678118654752) + 1.0
    inv = 1.0 / dist
    poly = 0.5 * 1.061405429
    for coef in (-1.453152027, 1.421413741, -0.284496736, 0.254829592):
        poly = poly * inv + 0.5 * coef
    tail = poly * inv * bell
    cdf = jnp.where(pre < 0.0, tail, 1.0 - tail)
    return pre * cdf, cdf + pre * (bell * 0.3989422804014327)


def widen(windows, flat, padded):
    place = lax.broadcasted_iota(jnp.int32, (PAD, 1), 0)
    for w in range(windows):
        block = flat[w * SPOTS : w * SPOTS + PAD, :]
        padded[w * PAD : (w + 1) * PAD, :] = jnp.where(place < SPOTS, block, 0.0).astype(BF16)


def norm_one_body(windows, tokens, gains, offsets, padded, flat):
    for r in range(0, tokens.shape[0], CHUNK):
        nhat, _ = norm_parts(tokens[r : r + CHUNK, :].astype(F32))
        flat[r : r + CHUNK, :] = nhat * gains[0:1, :] + offsets[0:1, :]
    widen(windows, flat, padded)


def head_masks(size):
    lane = lax.broadcasted_iota(jnp.int32, (PAD, LANES), 1) // size
    return [lane == h for h in range(LANES // size)]


def spread_heads(values, masks):
    zero = jnp.zeros_like(values)
    return jnp.concatenate([jnp.where(m, values, zero) for m in masks], axis=0)


def fold_heads(values, masks):
    total = values[0:PAD, :]
    for h in range(1, len(masks)):
        total = jnp.where(masks[h], values[h * PAD : (h + 1) * PAD, :], total)
    return total


def attend_body(size, scale, padded, near, far, bias, table, qkv_out, p_out, att_out, stacked):
    quarter = near.shape[1]
    width = 2 * quarter
    per = LANES // size * PAD

    @pl.when(pl.program_id(0) == 0)
    def _():
        stacked[:, 0:quarter, :] = near[...]
        stacked[:, quarter:width, :] = far[...]

    x = padded[...]
    q = (dot_right(x, stacked[0]) + bias[0:1, :]).astype(BF16)
    k = dot_right(x, stacked[1]).astype(BF16)
    v = (dot_right(x, stacked[2]) + bias[1:2, :]).astype(BF16)
    qkv_out[:, 0:width] = q
    qkv_out[:, width : 2 * width] = k
    qkv_out[:, 2 * width : 3 * width] = v
    masks = head_masks(size)
    items = [
        (slice(w * PAD, (w + 1) * PAD), g) for w in range(x.shape[0] // PAD) for g in range(width // LANES)
    ]
    lanes = lambda g: slice(g * LANES, (g + 1) * LANES)
    scores = [
        dot_right(k[r, lanes(g)], spread_heads(q[r, lanes(g)], masks)) * scale
        + table[:, g * per : (g + 1) * per]
        for r, g in items
    ]
    e = [jnp.exp(s - jnp.max(s, axis=0, keepdims=True)) for s in scores]
    probs = [(s * (1.0 / jnp.sum(s, axis=0, keepdims=True))).astype(BF16) for s in e]
    folded = [fold_heads(dot_left(p, v[r, lanes(g)]), masks) for p, (r, g) in zip(probs, items)]
    for (r, g), p, o in zip(items, probs, folded):
        p_out[r, g * per : (g + 1) * per] = p
        att_out[r, lanes(g)] = o.astype(BF16)


def attend_back_body(size, scale, low, weight, qkv0, qkv1, p0, p1, d_out, table_out, sums_out):
    width = qkv0.shape[1] // 3
    per = LANES // size * PAD
    pair_groups = width // LANES

    @pl.when(pl.program_id(0) == 0)
    def _():
        table_out[...] = jnp.zeros_like(table_out)
        sums_out[...] = jnp.zeros_like(sums_out)

    given = dot_right(low[...], weight[...]).astype(BF16)
    masks = head_masks(size)
    windows = low.shape[0] // PAD
    both = 2
    for first in range(0, windows, both):
        items = [
            (slice(w * PAD, (w + 1) * PAD), pair, g)
            for w in range(first, first + both)
            for pair in range(2)
            for g in range(pair_groups)
        ]
        qkv = (qkv0, qkv1)
        probs_of = (p0, p1)

        def part(item, t):
            r, pair, g = item
            return qkv[pair][r, t * width + g * LANES : t * width + (g + 1) * LANES]

        gs = [
            spread_heads(given[r, pair * width + g * LANES : pair * width + (g + 1) * LANES], masks)
            for r, pair, g in items
        ]
        prob_grad = [dot_right(part(i, 2), s) for i, s in zip(items, gs)]
        low_probs = [probs_of[pair][r, g * per : (g + 1) * per] for r, pair, g in items]
        probs = [p.astype(F32) for p in low_probs]
        weighed = [p * s for p, s in zip(probs, prob_grad)]
        score_low = [
            (t - p * jnp.sum(t, axis=0, keepdims=True)).astype(BF16) for p, t in zip(probs, weighed)
        ]
        dv = [dot(p, s).astype(BF16) for p, s in zip(low_probs, gs)]
        dk = [
            (dot(s, spread_heads(part(i, 0), masks)) * scale).astype(BF16)
            for i, s in zip(items, score_low)
        ]
        dq = [
            (fold_heads(dot_left(s, part(i, 1)), masks) * scale).astype(BF16)
            for i, s in zip(items, score_low)
        ]
        for (r, pair, g), *parts in zip(items, dq, dk, dv):
            for t, value in enumerate(parts):
                at = (pair * 3 + t) * width + g * LANES
                d_out[r, at : at + LANES] = value
        for pair in range(2):
            for g in range(pair_groups):
                mine = [n for n, (_, p, h) in enumerate(items) if (p, h) == (pair, g)]
                at = (pair * pair_groups + g) * per
                table_out[:, at : at + per] += sum(score_low[n].astype(F32) for n in mine)
                for t, values in enumerate((dq, dk, dv)):
                    at = (pair * 3 + t) * width + g * LANES
                    sums_out[0:1, at : at + LANES] += sum(
                        jnp.sum(values[n].astype(F32), axis=0, keepdims=True) for n in mine
                    )


def mixed_body(windows, count, att0, att1, *refs):
    wo = refs[:count]
    tokens, gains, offsets, mixed, normed, stacked = refs[count:]
    quarter = wo[0].shape[0]
    half = att0.shape[1]
    for k in range(count):
        stacked[k * quarter : (k + 1) * quarter, :] = wo[k][...]
    group = 4
    for first in range(0, windows, group):
        here = slice(first * PAD, (first + group) * PAD)
        total = dot(att0[here, :], stacked[0:half, :]) + dot(att1[here, :], stacked[half : 2 * half, :])
        for w in range(group):
            at = (first + w) * SPOTS
            mixed[at : at + SPOTS, :] = total[w * PAD : w * PAD + SPOTS, :]
    for r in range(0, tokens.shape[0], CHUNK):
        rows = slice(r, r + CHUNK)
        value = tokens[rows, :].astype(F32) + mixed[rows, :] + offsets[1:2, :]
        mixed[rows, :] = value
        nhat, _ = norm_parts(value)
        normed[rows, :] = (nhat * gains[1:2, :] + offsets[2:3, :]).astype(BF16)


def copies_of(pairs, sems, first=0):
    return [pltpu.make_async_copy(a, b, sems.at[first + i]) for i, (a, b) in enumerate(pairs)]


def pieces_of(pieces, target):
    at, pairs = 0, []
    for p in pieces:
        pairs.append((p, target.at[pl.ds(at, p.shape[0]), :]))
        at += p.shape[0]
    return pairs


def inner_body(count, pieces, started, last, *refs):
    refs = list(refs)
    take = lambda n: [refs.pop(0) for _ in range(n)]
    normed, bias = take(2)
    wi = take(count)
    wo = [take(pieces) for _ in range(count)]
    before = take(1)[0] if started else None
    if last:
        mixed, gains, offsets, crop = take(4)
    act_out, slope_out = take(count), take(count)
    if last:
        block_out, features, pool = take(3)
    else:
        total_out = take(1)[0]
    x, wi_v, wo_v, act, slope, total, sems, out_sems = take(8)
    if last:
        mixed_v = take(1)[0]
    pairs = [(normed, x)]
    for k in range(count):
        pairs += [(wi[k], wi_v.at[k])] + pieces_of(wo[k], wo_v.at[k])
    if started:
        pairs.append((before, total))
    if last:
        pairs.append((mixed, mixed_v))
    copies = copies_of(pairs, sems)
    for c in copies:
        c.start()
    copies.pop(0).wait()
    weights = [[copies.pop(0) for _ in range(1 + pieces)] for _ in range(count)]
    half = x.shape[0] // 2
    work = [(k, h) for k in range(count) for h in range(2)]

    def first(k, h):
        if h == 0:
            weights[k][0].wait()
        return dot(x[h * half : (h + 1) * half, :], wi_v[k]) + bias[k]

    out_pairs = [p for k in range(count) for p in ((act.at[k], act_out[k]), (slope.at[k], slope_out[k]))]
    if not last:
        out_pairs.append((total, total_out))
    outs = copies_of(out_pairs, out_sems)
    ahead = first(*work[0])
    for n, (k, h) in enumerate(work):
        pre = ahead
        if n + 1 < len(work):
            ahead = first(*work[n + 1])
        rows = slice(h * half, (h + 1) * half)
        value, grad = gelu_pair(pre)
        value = value.astype(BF16)
        act[k, rows, :] = value
        slope[k, rows, :] = grad.astype(BF16)
        if h == 1:
            outs[2 * k].start()
            outs[2 * k + 1].start()
        else:
            for c in weights[k][1:]:
                c.wait()
            if n == 0 and started:
                copies.pop(0).wait()
        share = dot(value, wo_v[k])
        if k == 0 and not started:
            total[rows, :] = share
        else:
            total[rows, :] += share
    if last:
        copies.pop(0).wait()
        crops = pool.shape[0]
        sums = [jnp.zeros((1, total.shape[1]), F32)] * crops
        for r in range(0, total.shape[0], CHUNK):
            rows = slice(r, r + CHUNK)
            value = mixed_v[rows, :] + total[rows, :] + offsets[3:4, :]
            block_out[rows, :] = value
            features[rows, :] = value.astype(BF16)
            nhat, _ = norm_parts(value)
            head = nhat * gains[2:3, :] + offsets[4:5, :]
            for c in range(crops):
                sums[c] = sums[c] + jnp.sum(jnp.where(crop[rows, :] == c, head, 0.0), axis=0, keepdims=True)
        for c in range(crops):
            pool[c : c + 1, :] = sums[c]
    else:
        outs[-1].start()
    for c in outs:
        c.wait()


def head_back_body(block_out, cotangent, crop, pooled_grad, gains, grad_out, low_out, sums_out):
    crops = pooled_grad.shape[0]

    @pl.when(pl.program_id(0) == 0)
    def _():
        sums_out[...] = jnp.zeros_like(sums_out)

    nhat, inv = norm_parts(block_out[...])
    grad = jnp.zeros(nhat.shape, F32)
    for c in range(crops):
        grad = jnp.where(crop[...] == c, pooled_grad[c : c + 1, :], grad)
    out = cotangent[...].astype(F32) + norm_back(nhat, inv, gains[2:3, :], grad)
    grad_out[...] = out
    low_out[...] = out.astype(BF16)
    sums_out[0:1, :] += jnp.sum(grad * nhat, axis=0, keepdims=True)
    sums_out[1:2, :] += jnp.sum(grad, axis=0, keepdims=True)
    sums_out[2:3, :] += jnp.sum(out, axis=0, keepdims=True)


def inner_back_body(windows, pieces, started, last, *refs):
    refs = list(refs)
    take = lambda n: [refs.pop(0) for _ in range(n)]
    low_in, normed, act_in, slope_in, wi_in = take(5)
    wo_in = take(pieces)
    before = take(1)[0] if started else None
    if last:
        mixed, out_grad, gains = take(3)
    outer_out, inner_out, sums_out = take(3)
    if last:
        grad_out, low_out, norm_sums = take(3)
    else:
        total_out = take(1)[0]
    low, x, act, slope, wi, wo, outer, inner, pre, total, sems, out_sems = take(12)
    pairs = [(low_in, low)] + pieces_of(wo_in, wo) + [(slope_in, slope), (act_in, act), (normed, x), (wi_in, wi)]
    if started:
        pairs.append((before, total))
    rows_all = total.shape[0]
    if last:
        mixed_v, flat = take(2)
        pairs += [(mixed, mixed_v), (out_grad, flat.at[pl.ds(0, rows_all), :])]
    copies = copies_of(pairs, sems)
    for c in copies:
        c.start()
    wait = lambda n: [copies.pop(0).wait() for _ in range(n)]
    outs = copies_of([(outer, outer_out), (inner, inner_out)] + ([] if last else [(total, total_out)]), out_sems)
    wait(1 + pieces)
    raw = dot_right(low[...], wo[...])
    wait(2)
    outer_value = dot_left(low[...], act[...])
    value = (raw * slope[...].astype(F32)).astype(BF16)
    pre[...] = value
    sums_out[...] = jnp.sum(value.astype(F32), axis=0, keepdims=True)
    outer[...] = outer_value.astype(BF16)
    outs[0].start()
    wait(2)
    share = dot_right(pre[...], wi[...])
    if started:
        wait(1)
        total[...] += share
    else:
        total[...] = share
    if not last:
        outs[2].start()
    inner[...] = dot_left(x[...], pre[...]).astype(BF16)
    outs[1].start()
    if last:
        wait(2)
        gain_sum = jnp.zeros((1, total.shape[1]), F32)
        shift_sum = gain_sum
        bias_sum = gain_sum
        for r in range(0, rows_all, CHUNK):
            rows = slice(r, r + CHUNK)
            nhat, inv = norm_parts(mixed_v[rows, :])
            grad = total[rows, :]
            gain_sum = gain_sum + jnp.sum(grad * nhat, axis=0, keepdims=True)
            shift_sum = shift_sum + jnp.sum(grad, axis=0, keepdims=True)
            out = flat[rows, :] + norm_back(nhat, inv, gains[1:2, :], grad)
            bias_sum = bias_sum + jnp.sum(out, axis=0, keepdims=True)
            grad_out[rows, :] = out
            flat[rows, :] = out
        norm_sums[0:1, :] = gain_sum
        norm_sums[1:2, :] = shift_sum
        norm_sums[2:3, :] = bias_sum
        widen(windows, flat, low_out)
    for c in outs:
        c.wait()


def weight_grad_body(x, low, d, att0, att1, even_a, odd_a, even_b, odd_b):
    width = att0.shape[1]
    quarter = width // 2
    big = dot_left(x[...], d[...])
    for t, (even, odd, at) in enumerate(((even_a, odd_a, 0), (even_a, odd_a, 1), (even_b, odd_b, 0))):
        lanes = slice(at * quarter, (at + 1) * quarter)
        even[0, :, lanes] = big[:, t * width : t * width + quarter].astype(BF16)
        odd[0, :, lanes] = big[:, t * width + quarter : (t + 1) * width].astype(BF16)
    for pair, att in enumerate((att0, att1)):

        @pl.when(pl.program_id(0) == 1 - pair)
        def _(att=att):
            side = dot_left(low[...], att[...])
            even_b[0, :, quarter:width] = side[:, 0:quarter].astype(BF16)
            odd_b[0, :, quarter:width] = side[:, quarter:width].astype(BF16)


def tokens_back_body(windows, grads, stacked0, stacked1, tokens, mixed_grad, gains, head, mid, ends, grad_out, packed, flat):
    half = stacked0.shape[0]
    group = 4
    for first in range(0, windows, group):
        here = slice(first * PAD, (first + group) * PAD)
        total = dot(grads[here, 0:half], stacked0[...]) + dot(grads[here, half : 2 * half], stacked1[...])
        for w in range(group):
            at = (first + w) * SPOTS
            flat[at : at + SPOTS, :] = total[w * PAD : w * PAD + SPOTS, :]
    gain_sum = jnp.zeros((1, tokens.shape[1]), F32)
    shift_sum = gain_sum
    for r in range(0, tokens.shape[0], CHUNK):
        rows = slice(r, r + CHUNK)
        nhat, inv = norm_parts(tokens[rows, :].astype(F32))
        grad = flat[rows, :]
        gain_sum = gain_sum + jnp.sum(grad * nhat, axis=0, keepdims=True)
        shift_sum = shift_sum + jnp.sum(grad, axis=0, keepdims=True)
        grad_out[rows, :] = mixed_grad[rows, :] + norm_back(nhat, inv, gains[0:1, :], grad)
    packed[0:1, :] = gain_sum
    packed[1:2, :] = mid[0:1, :]
    packed[2:3, :] = head[0:1, :]
    packed[3:4, :] = shift_sum
    packed[4:5, :] = mid[2:3, :]
    packed[5:6, :] = mid[1:2, :]
    packed[6:7, :] = head[2:3, :]
    packed[7:8, :] = head[1:2, :]
    packed[8 : 8 + ends.shape[0], :] = ends[...]


def swap(values, axis, bit):
    return lax.ppermute(values, axis, [(i, i ^ bit) for i in range(lax.axis_size(axis))])


def bits_of(axis):
    size = lax.axis_size(axis)
    bit, found = 1, []
    while bit < size:
        found.append(bit)
        bit *= 2
    return found


def has_bit(axis, bit):
    return (lax.axis_index(axis) // bit) % 2 == 1


def after(values, *others):
    return lax.optimization_barrier((values, *others))[0]


def sum_over(values, axes):
    for axis in axes:
        for bit in bits_of(axis):
            values = values + swap(values, axis, bit)
    return values


def ordered(mine, other, upper):
    return jnp.concatenate([jnp.where(upper, other, mine), jnp.where(upper, mine, other)], axis=0)


def gather_over(values, axis):
    for bit in bits_of(axis):
        values = ordered(values, swap(values, axis, bit), has_bit(axis, bit))
    return values


def by_distance(values, axis):
    for bit in bits_of(axis):
        size = values.shape[0]
        folded = values.reshape(size // (2 * bit), 2, bit, *values.shape[1:])
        folded = jnp.where(has_bit(axis, bit), folded[:, ::-1], folded)
        values = folded.reshape(values.shape)
    return values


def own_half(values, share):
    halves = values.reshape(2, values.shape[0] // 2, *values.shape[1:])
    return lax.dynamic_index_in_dim(halves, lax.axis_index("dp") // share % 2, 0, keepdims=False)


def halve_rows(values, bit):
    groups, rows, columns = values.shape
    folded = values.reshape(groups // 2, 2, rows, columns)
    mine = lax.axis_index("dp") // bit % 2
    keep = lax.dynamic_index_in_dim(folded, mine, 1, keepdims=False)
    send = lax.dynamic_index_in_dim(folded, 1 - mine, 1, keepdims=False)
    return keep, send


def add(kept, got):
    return kept.astype(F32) + got.astype(F32)


def gelu_exact(values):
    return jax.nn.gelu(values, approximate=False)


def gelu_back(pre, cotangent):
    return jax.vjp(gelu_exact, pre)[1](cotangent)[0]


def normalize_rows(values):
    return values * lax.rsqrt(jnp.sum(values * values, axis=-1, keepdims=True) + 1e-06)


def offset_table():
    places = jnp.arange(PAD, dtype=jnp.int32)
    row_of = places // SIDE
    col_of = places % SIDE
    offset = (row_of[None, :] - row_of[:, None] + SIDE - 1) * (2 * SIDE - 1) + (
        col_of[None, :] - col_of[:, None] + SIDE - 1
    )
    inside = (places[:, None] < SPOTS) & (places[None, :] < SPOTS)
    offset = jnp.where(inside, offset, -1)
    entries = jnp.arange((2 * SIDE - 1) ** 2, dtype=jnp.int32)
    return (offset.reshape(-1)[:, None] == entries[None, :]).astype(F32)


def shards(
    tokens,
    input_projection,
    input_bias,
    position_bias,
    output_projection,
    inner_weight,
    inner_bias,
    outer_weight,
    norm_gains,
    offsets,
    head_first,
    head_first_bias,
    head_second,
    head_second_bias,
    head_third,
    head_third_bias,
    prototype_direction,
    prototype_gain,
    crop_windows,
    first_epoch,
    feature_cotangent,
    logit_cotangent,
):
    rows, width = tokens.shape
    windows = rows // SPOTS
    narrow_index = lax.axis_index("narrow")
    dp_index = lax.axis_index("dp")
    count = lax.axis_size("narrow")
    groups = lax.axis_size("dp")
    quarter = input_projection.shape[2]
    hidden = inner_weight.shape[1]
    heads = position_bias.shape[1] // count
    size = quarter // heads
    scale = size ** (-0.5)
    crops = crop_windows.shape[1]
    padded_rows = windows * PAD

    near, far = bits_of("narrow")
    data_bits = bits_of("dp")
    share, share_too = data_bits[0], data_bits[1]

    w_in0 = input_projection.swapaxes(1, 2)
    w_in1 = swap(w_in0, "narrow", near)
    w_in2 = swap(w_in0, "narrow", far)
    att_half = swap(own_half(output_projection, share_too), "narrow", far)
    w_att1 = swap(output_projection, "narrow", near)
    w_inner1 = swap(inner_weight, "narrow", near)
    w_outer1 = swap(outer_weight, "narrow", near)
    upper_inner, lower_inner = jnp.split(inner_weight, 2)
    upper_outer, lower_outer = jnp.split(outer_weight, 2)

    bias_in = by_distance(input_bias.reshape(2, count, quarter).swapaxes(0, 1), "narrow")
    bias_in = bias_in.swapaxes(0, 1).reshape(2, count * quarter)
    bias_inner = by_distance(inner_bias.reshape(count, 1, hidden), "narrow")
    table = offset_table()
    turned = by_distance(position_bias.T.reshape(count, heads, -1), "narrow").reshape(count * heads, -1)
    spread = jnp.dot(table, turned.T, precision=HIGH, preferred_element_type=F32)
    spread = spread.reshape(PAD, PAD, count * heads).transpose(0, 2, 1)
    inside = (jnp.arange(PAD) < SPOTS)[:, None, None]
    spread = jnp.where(inside, spread, NEG).reshape(PAD, count * heads * PAD)

    ends = jnp.cumsum(crop_windows[0])
    row_window = narrow_index * windows + jnp.arange(rows, dtype=jnp.int32) // SPOTS
    crop_of_row = jnp.sum((row_window[:, None] >= ends[None, :]).astype(jnp.int32), axis=1, keepdims=True)
    crop_tokens = (crop_windows[0] * SPOTS).astype(F32)

    padded = call(
        functools.partial(norm_one_body, windows),
        shape((padded_rows, width), BF16),
        (tokens, norm_gains, offsets),
        scratch=[pltpu.VMEM((rows + 16, width), F32)],
        us=3.5,
    )
    half = 2 * quarter
    pair_lanes = 2 * heads * PAD
    batch = 4 * PAD
    by_row = lambda n: pl.BlockSpec((batch, n), lambda i: (i, 0))
    fixed = lambda *dims: pl.BlockSpec(dims, lambda i: (0,) * len(dims))
    qkv, probs, attended, stacked_in = [], [], [], []

    def attend(pair, x, first, second):
        got = pl.pallas_call(
            functools.partial(attend_body, size, scale),
            grid=(padded_rows // batch,),
            out_shape=(
                shape((padded_rows, 3 * half), BF16),
                shape((padded_rows, pair_lanes), BF16),
                shape((padded_rows, half), BF16),
                shape((3, half, width), BF16),
            ),
            in_specs=[
                by_row(width),
                fixed(3, quarter, width),
                fixed(3, quarter, width),
                fixed(2, half),
                pl.BlockSpec((PAD, pair_lanes), lambda i, pair=pair: (0, pair)),
            ],
            out_specs=(by_row(3 * half), by_row(pair_lanes), by_row(half), fixed(3, half, width)),
            compiler_params=pltpu.CompilerParams(vmem_limit_bytes=VMEM_LIMIT),
            cost_estimate=cost(9.0),
        )(x, first, second, bias_in[:, pair * half : (pair + 1) * half], spread)
        for keep, value in zip((qkv, probs, attended, stacked_in), got):
            keep.append(value)
        return got

    direction = prototype_direction.astype(F32)
    column_inv = lax.rsqrt(jnp.sum(direction * direction, axis=0, keepdims=True) + 1e-06)
    columns_low = (prototype_gain * direction * column_inv).astype(BF16)
    unit_share = dot_right(logit_cotangent, columns_low)

    def whole_of(mine, other, bit):
        return ordered(mine, other, has_bit("dp", bit))

    def bring(weight, bit, *others):
        return swap(own_half(after(weight, *others), bit), "narrow", far)

    w_in2, att_half, w_in1 = after((w_in2, att_half, w_in1), padded, spread, unit_share)
    w_in3 = swap(w_in2, "narrow", near)
    att_rest = swap(att_half, "dp", share_too)
    inner_a = bring(upper_inner, share, w_in2)
    got = attend(0, after(padded, w_in2), w_in0, w_in1)
    w_in3, att_rest, inner_a = after((w_in3, att_rest, inner_a), got)
    w_att2 = whole_of(att_half, att_rest, share_too)
    w_att3 = swap(w_att2, "narrow", near)
    inner_a_rest = swap(inner_a, "dp", share)
    inner_b = bring(lower_inner, share, inner_a)
    got = attend(1, after(padded, w_att2), w_in2, w_in3)
    w_att3, inner_a_rest, inner_b = after((w_att3, inner_a_rest, inner_b), got)
    inner_b_rest = swap(inner_b, "dp", share)
    outer_a = bring(upper_outer, share_too, inner_b)
    mixed, normed_two, stacked_att = call(
        functools.partial(mixed_body, windows, count),
        (shape((rows, width), F32), shape((rows, width), BF16), shape((count * quarter, width), BF16)),
        (*attended, output_projection, w_att1, w_att2, w_att3, after(tokens, inner_b), norm_gains, offsets),
        us=6.0,
    )
    inner_b_rest, outer_a = after((inner_b_rest, outer_a), mixed)
    w_inner2 = jnp.concatenate([whole_of(inner_a, inner_a_rest, share), whole_of(inner_b, inner_b_rest, share)])
    w_inner3 = swap(w_inner2, "narrow", near)
    outer_a_rest = swap(outer_a, "dp", share_too)
    outer_b = bring(lower_outer, share, outer_a)

    anywhere = pl.BlockSpec(memory_space=pl.ANY)
    held = pl.BlockSpec(memory_space=pltpu.VMEM)
    row_held = pltpu.VMEM((rows, width), F32)
    low_held = pltpu.VMEM((rows, width), BF16)
    act_shape = shape((rows, hidden), BF16)

    def inner_call(x, bias, wi, wo, before=(), ending=()):
        n, pieces = len(wi), len(wo[0])
        wo = [p for w in wo for p in w]
        last = bool(ending)
        tail_shape = (shape((rows, width), F32),)
        tail_spec = (anywhere,)
        if last:
            tail_shape += (shape((rows, width), BF16), shape((crops, width), F32))
            tail_spec = (held,) * 3
        return pl.pallas_call(
            functools.partial(inner_body, n, pieces, bool(before), last),
            out_shape=(act_shape,) * (2 * n) + tail_shape,
            in_specs=[anywhere, held] + [anywhere] * (len(wi) + len(wo) + len(before)) + ([anywhere] + [held] * 3 if last else []),
            out_specs=(anywhere,) * (2 * n) + tail_spec,
            scratch_shapes=[
                low_held,
                pltpu.VMEM((n, width, hidden), BF16),
                pltpu.VMEM((n, hidden, width), BF16),
                pltpu.VMEM((n, rows, hidden), BF16),
                pltpu.VMEM((n, rows, hidden), BF16),
                row_held,
                pltpu.SemaphoreType.DMA((1 + n * (1 + pieces) + len(before) + last,)),
                pltpu.SemaphoreType.DMA((2 * n + 1,)),
            ] + ([row_held] if last else []),
            compiler_params=pltpu.CompilerParams(vmem_limit_bytes=VMEM_LIMIT),
            cost_estimate=cost(16.0 if last else 7.0),
        )(x, bias, *wi, *wo, *before, *ending)

    act0, slope0, inner_total = inner_call(after(normed_two, w_inner2), bias_inner[0:1], [inner_weight], [[outer_weight]])
    outer_a_rest, outer_b, w_inner3 = after((outer_a_rest, outer_b, w_inner3), inner_total)
    outer2_a = whole_of(outer_a, outer_a_rest, share_too)
    outer3_a = swap(outer2_a, "narrow", near)
    outer_b_rest = swap(outer_b, "dp", share)
    act1, slope1, inner_total = inner_call(
        after(normed_two, outer2_a), bias_inner[1:2], [w_inner1], [[w_outer1]], (inner_total,)
    )
    outer3_a, outer_b_rest = after((outer3_a, outer_b_rest), inner_total)
    outer2_b = whole_of(outer_b, outer_b_rest, share)
    outer3_b = swap(outer2_b, "narrow", near)
    outer2, outer3 = [outer2_a, outer2_b], [outer3_a, outer3_b]
    act2, act3, slope2, slope3, block_out, features, pool = inner_call(
        normed_two, bias_inner[2:4], [w_inner2, w_inner3], [outer2, outer3], (inner_total,),
        (mixed, norm_gains, offsets, crop_of_row),
    )

    flat_pool = pool.reshape(-1, LANES)
    pool_rows = flat_pool.shape[0]
    unit_rows = unit_share.reshape(-1, LANES)
    both = sum_over(jnp.concatenate([flat_pool, unit_rows]), ("narrow",))
    gathered, unit_rows = both[:pool_rows], both[pool_rows:]
    per_crop = jnp.repeat(crop_tokens, width // LANES)[:, None]
    gathered = gathered / per_crop
    for bit in data_bits:
        other = swap(jnp.concatenate([gathered, unit_rows]), "dp", bit)
        unit_rows = unit_rows + other[gathered.shape[0] :]
        gathered = ordered(gathered, other[: gathered.shape[0]], has_bit("dp", bit))
    unit_grad = unit_rows.reshape(unit_share.shape)
    pooled = gathered.reshape(-1, width).astype(BF16)
    first_pre = dot(pooled, head_first) + head_first_bias
    first_act = gelu_exact(first_pre).astype(BF16)
    second_pre = dot(first_act, head_second) + head_second_bias
    second_act = gelu_exact(second_pre).astype(BF16)
    embedded = dot(second_act, head_third) + head_third_bias
    units = normalize_rows(embedded).astype(BF16)
    embed_grad = jax.vjp(normalize_rows, embedded)[1](unit_grad)[0]
    embed_low = embed_grad.astype(BF16)
    second_low = gelu_back(second_pre, dot_right(embed_low, head_third)).astype(BF16)
    first_low = gelu_back(first_pre, dot_right(second_low, head_second)).astype(BF16)
    own_low = lax.dynamic_slice_in_dim(first_low, dp_index * crops, crops, 0)
    pooled_grad = dot_right(own_low, head_first) / crop_tokens[:, None]

    split = rows // 2
    by_chunk = lambda n: pl.BlockSpec((split, n), lambda i: (i, 0))
    out_grad, out_low, head_sums = pl.pallas_call(
        head_back_body,
        grid=(2,),
        out_shape=(shape((rows, width), F32), shape((rows, width), BF16), shape((3, width), F32)),
        in_specs=[by_chunk(width), by_chunk(width), by_chunk(1), fixed(crops, width), fixed(*norm_gains.shape)],
        out_specs=(by_chunk(width), by_chunk(width), fixed(3, width)),
        compiler_params=pltpu.CompilerParams(vmem_limit_bytes=VMEM_LIMIT),
        cost_estimate=cost(4.0),
    )(block_out, feature_cotangent, crop_of_row, pooled_grad, norm_gains)

    def by_group(part):
        return part.reshape(groups, part.shape[0] // groups, part.shape[1])

    def inner_back(act, slope, wi, wo, before=(), ending=()):
        last = bool(ending)
        pieces = len(wo)
        outs = [shape((width, hidden), BF16)] * 2 + [shape((1, hidden), F32), shape((rows, width), F32)]
        specs = [anywhere, anywhere, held, held if last else anywhere]
        if last:
            outs += [shape((padded_rows, width), BF16), shape((3, width), F32)]
            specs += [held, held]
        return pl.pallas_call(
            functools.partial(inner_back_body, windows, pieces, bool(before), last),
            out_shape=tuple(outs),
            in_specs=[anywhere] * (5 + pieces + len(before)) + ([anywhere, anywhere, held] if last else []),
            out_specs=tuple(specs),
            scratch_shapes=[
                low_held,
                low_held,
                pltpu.VMEM((rows, hidden), BF16),
                pltpu.VMEM((rows, hidden), BF16),
                pltpu.VMEM((width, hidden), BF16),
                pltpu.VMEM((hidden, width), BF16),
                pltpu.VMEM((width, hidden), BF16),
                pltpu.VMEM((width, hidden), BF16),
                pltpu.VMEM((rows, hidden), BF16),
                row_held,
                pltpu.SemaphoreType.DMA((5 + pieces + len(before) + 2 * last,)),
                pltpu.SemaphoreType.DMA((3,)),
            ] + ([row_held, pltpu.VMEM((rows + 16, width), F32)] if last else []),
            compiler_params=pltpu.CompilerParams(vmem_limit_bytes=VMEM_LIMIT),
            cost_estimate=cost(11.0 if last else 8.0),
        )(out_low, normed_two, act, slope, wi, *wo, *before, *ending)

    o3, i3, sums3, total = inner_back(act3, slope3, w_inner3, outer3)
    got_o3, got_i3 = swap(o3, "narrow", near), swap(i3, "narrow", near)
    o2, i2, sums2, total = inner_back(act2, slope2, w_inner2, outer2, (total,))
    got_o3, got_i3 = after((got_o3, got_i3), total)
    sum_i2 = add(i2, got_i3).astype(BF16)
    keep_o2, send_o2 = halve_rows(by_group(add(o2, got_o3).astype(BF16)), share)
    got_i2 = swap(sum_i2, "narrow", far)
    got_o2 = swap(send_o2, "dp", share)
    o1, i1, sums1, total = inner_back(act1, slope1, w_inner1, [w_outer1], (after(total, sum_i2, send_o2),))
    got_o1, got_i1 = swap(o1, "narrow", near), swap(i1, "narrow", near)
    o0, i0, sums0, mixed_grad, mixed_low, mixed_sums = inner_back(
        act0, slope0, inner_weight, [outer_weight], (total,), (mixed, out_grad, norm_gains)
    )
    got_o1, got_i1, got_o2 = after((got_o1, got_i1, got_o2), mixed_low)
    sum_i0 = add(i0, got_i1).astype(BF16)
    keep_o0, send_o0 = halve_rows(by_group(add(o0, got_o1).astype(BF16)), share)
    far_o = add(keep_o2, got_o2).astype(BF16)
    got_o0 = swap(send_o0, "dp", share)
    got_o = swap(far_o, "narrow", far)
    mixed_low = after(mixed_low, sum_i0, send_o0, far_o)

    input_grads, pair_grads, input_sums = pl.pallas_call(
        functools.partial(attend_back_body, size, scale),
        grid=(padded_rows // batch,),
        out_shape=(
            shape((padded_rows, 6 * half), BF16),
            shape((PAD, 2 * pair_lanes), F32),
            shape((1, 6 * half), F32),
        ),
        in_specs=[
            by_row(width),
            fixed(count * quarter, width),
            by_row(3 * half),
            by_row(3 * half),
            by_row(pair_lanes),
            by_row(pair_lanes),
        ],
        out_specs=(by_row(6 * half), fixed(PAD, 2 * pair_lanes), fixed(1, 6 * half)),
        compiler_params=pltpu.CompilerParams(vmem_limit_bytes=VMEM_LIMIT),
        cost_estimate=cost(13.0),
    )(mixed_low, stacked_att, *qkv, *probs)

    got_i2, got_o0 = after((got_i2, got_o0), input_grads)
    keep_i, send_i = halve_rows(by_group(add(sum_i0, got_i2).astype(BF16)), share)
    got_i = swap(send_i, "dp", share)
    near_o = add(keep_o0, got_o0).astype(BF16)
    input_grads = after(input_grads, send_i, near_o)

    pair_shape = shape((2, width, half), BF16)
    pair_spec = pl.BlockSpec((1, width, half), lambda i: (1 - i, 0, 0))
    even_a, odd_a, even_b, odd_b = pl.pallas_call(
        weight_grad_body,
        grid=(2,),
        out_shape=(pair_shape,) * 4,
        in_specs=[
            fixed(padded_rows, width),
            fixed(padded_rows, width),
            pl.BlockSpec((padded_rows, 3 * half), lambda i: (0, 1 - i)),
            fixed(padded_rows, half),
            fixed(padded_rows, half),
        ],
        out_specs=(pair_spec,) * 4,
        compiler_params=pltpu.CompilerParams(vmem_limit_bytes=VMEM_LIMIT),
        cost_estimate=cost(12.0),
    )(padded, mixed_low, input_grads, *attended)
    got_a, got_b = swap(odd_a, "narrow", near), swap(odd_b, "narrow", near)

    got_i, got_o = after((got_i, got_o), even_a)
    mlp = jnp.concatenate([add(keep_i, got_i), add(near_o, got_o)], axis=2).astype(BF16)
    keep_m, send_m = halve_rows(mlp, data_bits[1])
    got_m = swap(send_m, "dp", data_bits[1])
    got_a, got_b = after((got_a, got_b), send_m)
    sum_a = add(even_a, got_a).astype(BF16)
    keep_b, send_b = halve_rows(add(even_b, got_b).astype(BF16).reshape(2 * groups, width // groups, half), share)
    got_a2 = swap(sum_a[1], "narrow", far)
    got_b2 = swap(send_b, "dp", share)

    pair_grads = after(pair_grads, sum_a, send_b)
    pair_grad = pair_grads.reshape(PAD, count * heads, PAD).transpose(1, 0, 2)
    table_grad = lax.dot_general(
        pair_grad.reshape(count * heads, PAD * PAD), table, (((1,), (0,)), ((), ())),
        precision=HIGH, preferred_element_type=F32,
    )
    offsets_count = table_grad.shape[1]
    table_grad = by_distance(table_grad.reshape(count, heads, offsets_count), "narrow").reshape(table_grad.shape)
    table_rows = jnp.pad(table_grad, ((0, 0), (0, 256 - offsets_count))).reshape(-1, width)
    input_sum = input_sums.reshape(2, 3, 2, quarter).transpose(0, 2, 1, 3).reshape(count, 3, quarter)
    input_sum = by_distance(input_sum, "narrow").swapaxes(0, 1).reshape(3, count * quarter)
    inner_sum = by_distance(jnp.concatenate([sums0, sums1, sums2, sums3]), "narrow").reshape(-1, width)
    ends_in = jnp.concatenate([input_sum[0:1], input_sum[2:3], inner_sum, table_rows])
    packed_rows = 8 + ends_in.shape[0]
    tokens_grad, packed = call(
        functools.partial(tokens_back_body, windows),
        (shape((rows, width), F32), shape((packed_rows, width), F32)),
        (
            input_grads,
            *[v.reshape(3 * half, width) for v in stacked_in],
            tokens,
            mixed_grad,
            norm_gains,
            head_sums,
            mixed_sums,
            ends_in,
        ),
        scratch=[pltpu.VMEM((rows, width), F32)],
        us=10.0,
    )

    small = packed
    small_bits = [("narrow", near), ("narrow", far)] + [("dp", b) for b in data_bits]
    small_got = swap(small, *small_bits[0])
    got_a2, got_b2, got_m, small_got = after((got_a2, got_b2, got_m, small_got), tokens_grad)
    keep_a, send_a = halve_rows(by_group(add(sum_a[0], got_a2).astype(BF16)), share)
    got_a = swap(send_a, "dp", share)
    sum_b = add(keep_b, got_b2).astype(BF16).reshape(2, groups // 2, width // groups, half)
    got_b = swap(sum_b[1], "narrow", far)
    keep_m, send_m = halve_rows(add(keep_m, got_m).astype(BF16), data_bits[2])
    got_m = swap(send_m, "dp", data_bits[2])
    small = small + small_got
    small_got = swap(small, *small_bits[1])

    units, columns_low, direction = after((units, columns_low, direction), send_a, sum_b, send_m)
    logits = dot(units, columns_low)
    column_grad = dot_left(units, logit_cotangent)
    keep = (1 - first_epoch).astype(F32)[None, :]
    along = jnp.sum(column_grad * direction, axis=0, keepdims=True)
    gain_grad = (keep * column_inv * along)[0]
    direction_grad = (keep * prototype_gain) * (
        column_inv * column_grad - (column_inv**3 * along) * direction
    )

    got_a, got_b, small_got = after((got_a, got_b, small_got), direction_grad, logits)
    att_sum = jnp.concatenate([add(keep_a, got_a), add(sum_b[0], got_b)], axis=2).astype(BF16)
    keep_j, send_j = halve_rows(att_sum, data_bits[1])
    got_j = swap(send_j, "dp", data_bits[1])
    small = small + small_got
    small_got = swap(small, *small_bits[2])

    def own(values):
        part = values.shape[1] // groups
        return lax.dynamic_slice_in_dim(values, dp_index * part, part, 1)

    first_low, second_low = after((first_low, second_low), send_j, small)
    own_first, own_second = own(first_low), own(second_low)
    own_embed = own(embed_grad)
    first_grad = dot_left(pooled, own_first)
    second_grad = dot_left(first_act, own_second)
    third_grad = dot_left(own(second_act), embed_low)

    got_j, got_m, small_got = after((got_j, got_m, small_got), first_grad, second_grad, third_grad)
    joined = add(keep_j, got_j)
    for bit in data_bits[2:]:
        keep_j, send_j = halve_rows(joined.astype(BF16), bit)
        joined = add(keep_j, swap(send_j, "dp", bit))
    mlp = add(keep_m, got_m)
    for bit in data_bits[3:]:
        keep_m, send_m = halve_rows(mlp.astype(BF16), bit)
        mlp = add(keep_m, swap(send_m, "dp", bit))
    small = small + small_got
    for place in small_bits[3:]:
        small = small + swap(small, *place)
    inner_total, outer_total = mlp[0, :, :hidden], mlp[0, :, hidden:]
    joined = joined[0]
    attend_total = joined[:, 3 * quarter :]
    input_total = jnp.stack([joined[:, i * quarter : (i + 1) * quarter] for i in range(3)])

    gain_total, offset_total, bias_total = small[0:3], small[3:8], small[8:10]
    inner_bias_total = small[10 : 10 + inner_sum.shape[0]].reshape(-1)
    table_total = small[10 + inner_sum.shape[0] :].reshape(count * heads, 256)[:, :offsets_count].T
    return (
        features,
        logits,
        tokens_grad,
        input_total,
        bias_total,
        table_total,
        attend_total.T,
        inner_total,
        inner_bias_total,
        outer_total.T,
        gain_total,
        offset_total,
        first_grad,
        jnp.sum(own_first.astype(F32), axis=0),
        second_grad,
        jnp.sum(own_second.astype(F32), axis=0),
        third_grad,
        jnp.sum(own_embed, axis=0),
        direction_grad,
        gain_grad,
    )


def solution(mesh):
    placed = (
        P(("dp", "narrow"), None),
        P(None, None, "narrow"),
        P(),
        P(),
        P("narrow", None),
        P(None, "narrow"),
        P(),
        P("narrow", None),
        P(),
        P(),
        P(),
        P(),
        P(),
        P(),
        P(),
        P(),
        P(None, ("dp", "narrow")),
        P(("dp", "narrow")),
        P("dp", None),
        P(("dp", "narrow")),
        P(("dp", "narrow"), None),
        P(None, ("dp", "narrow")),
    )
    return jax.shard_map(
        shards,
        mesh=mesh,
        in_specs=placed,
        out_specs=(
            P(("dp", "narrow"), None),
            P(None, ("dp", "narrow")),
            P(("dp", "narrow"), None),
            P(None, "dp", "narrow"),
            P(),
            P(),
            P("narrow", "dp"),
            P("dp", "narrow"),
            P(),
            P("narrow", "dp"),
            P(),
            P(),
            P(None, "dp"),
            P("dp"),
            P(None, "dp"),
            P("dp"),
            P("dp", None),
            P("dp"),
            P(None, ("dp", "narrow")),
            P(("dp", "narrow")),
        ),
        check_vma=False,
    )
```

```python
import functools

import jax
import jax.numpy as jnp
from jax import lax
from jax.experimental import pallas as pl
from jax.experimental.pallas import tpu as pltpu
from jax.sharding import PartitionSpec as P

HIGH = lax.Precision.HIGHEST
F32 = jnp.float32
BF16 = jnp.bfloat16
SIDE = 7
SPOTS = SIDE * SIDE
PAD = 64
LANES = 128
CHUNK = 112
VMEM_LIMIT = 60 * 1024 * 1024
NEG = -1e30


def dot(left, right):
    return jnp.dot(left, right, preferred_element_type=F32)


def dot_left(left, right):
    return lax.dot_general(left, right, (((0,), (0,)), ((), ())), preferred_element_type=F32)


def dot_right(left, right):
    return lax.dot_general(left, right, (((1,), (1,)), ((), ())), preferred_element_type=F32)


def cost(us):
    return pl.CostEstimate(flops=0, bytes_accessed=int(us * 3.3e6), transcendentals=0)


def call(body, outs, ins, **kw):
    scratch = kw.pop("scratch", ())
    return pl.pallas_call(
        body,
        out_shape=outs,
        in_specs=[pl.BlockSpec(memory_space=pltpu.VMEM)] * len(ins),
        out_specs=jax.tree.map(lambda _: pl.BlockSpec(memory_space=pltpu.VMEM), outs),
        scratch_shapes=scratch,
        compiler_params=pltpu.CompilerParams(vmem_limit_bytes=VMEM_LIMIT),
        cost_estimate=cost(kw.pop("us")),
        **kw,
    )(*ins)


def shape(dims, kind):
    return jax.ShapeDtypeStruct(dims, kind)


def norm_parts(values):
    center = values - jnp.mean(values, axis=-1, keepdims=True)
    spread = jnp.mean(center * center, axis=-1, keepdims=True)
    inv = lax.rsqrt(spread + 1e-05)
    return center * inv, inv


def norm_back(nhat, inv, gain, grad):
    scaled = grad * gain
    first = jnp.mean(scaled, axis=-1, keepdims=True)
    second = jnp.mean(scaled * nhat, axis=-1, keepdims=True)
    return (scaled - first - nhat * second) * inv


def gelu_pair(pre):
    bell = jnp.exp(pre * pre * -0.5)
    dist = jnp.abs(pre) * (0.3275911 * 0.70710678118654752) + 1.0
    inv = 1.0 / dist
    poly = 0.5 * 1.061405429
    for coef in (-1.453152027, 1.421413741, -0.284496736, 0.254829592):
        poly = poly * inv + 0.5 * coef
    tail = poly * inv * bell
    cdf = jnp.where(pre < 0.0, tail, 1.0 - tail)
    return pre * cdf, cdf + pre * (bell * 0.3989422804014327)


def widen(windows, flat, padded):
    place = lax.broadcasted_iota(jnp.int32, (PAD, 1), 0)
    for w in range(windows):
        block = flat[w * SPOTS : w * SPOTS + PAD, :]
        padded[w * PAD : (w + 1) * PAD, :] = jnp.where(place < SPOTS, block, 0.0).astype(BF16)


def norm_one_body(windows, tokens, gains, offsets, padded, flat):
    for r in range(0, tokens.shape[0], CHUNK):
        nhat, _ = norm_parts(tokens[r : r + CHUNK, :].astype(F32))
        flat[r : r + CHUNK, :] = nhat * gains[0:1, :] + offsets[0:1, :]
    widen(windows, flat, padded)


def head_masks(size):
    lane = lax.broadcasted_iota(jnp.int32, (PAD, LANES), 1) // size
    return [lane == h for h in range(LANES // size)]


def spread_heads(values, masks):
    zero = jnp.zeros_like(values)
    return jnp.concatenate([jnp.where(m, values, zero) for m in masks], axis=0)


def fold_heads(values, masks):
    total = values[0:PAD, :]
    for h in range(1, len(masks)):
        total = jnp.where(masks[h], values[h * PAD : (h + 1) * PAD, :], total)
    return total


def attend_body(size, scale, padded, near, far, bias, table, qkv_out, p_out, att_out, stacked):
    quarter = near.shape[1]
    width = 2 * quarter
    per = LANES // size * PAD

    @pl.when(pl.program_id(0) == 0)
    def _():
        stacked[:, 0:quarter, :] = near[...]
        stacked[:, quarter:width, :] = far[...]

    x = padded[...]
    q = (dot_right(x, stacked[0]) + bias[0:1, :]).astype(BF16)
    k = dot_right(x, stacked[1]).astype(BF16)
    v = (dot_right(x, stacked[2]) + bias[1:2, :]).astype(BF16)
    qkv_out[:, 0:width] = q
    qkv_out[:, width : 2 * width] = k
    qkv_out[:, 2 * width : 3 * width] = v
    masks = head_masks(size)
    items = [
        (slice(w * PAD, (w + 1) * PAD), g) for w in range(x.shape[0] // PAD) for g in range(width // LANES)
    ]
    lanes = lambda g: slice(g * LANES, (g + 1) * LANES)
    scores = [
        dot_right(k[r, lanes(g)], spread_heads(q[r, lanes(g)], masks)) * scale
        + table[:, g * per : (g + 1) * per]
        for r, g in items
    ]
    e = [jnp.exp(s - jnp.max(s, axis=0, keepdims=True)) for s in scores]
    probs = [(s * (1.0 / jnp.sum(s, axis=0, keepdims=True))).astype(BF16) for s in e]
    folded = [fold_heads(dot_left(p, v[r, lanes(g)]), masks) for p, (r, g) in zip(probs, items)]
    for (r, g), p, o in zip(items, probs, folded):
        p_out[r, g * per : (g + 1) * per] = p
        att_out[r, lanes(g)] = o.astype(BF16)


def attend_back_body(size, scale, low, weight, qkv0, qkv1, p0, p1, d_out, table_out, sums_out):
    width = qkv0.shape[1] // 3
    per = LANES // size * PAD
    pair_groups = width // LANES

    @pl.when(pl.program_id(0) == 0)
    def _():
        table_out[...] = jnp.zeros_like(table_out)
        sums_out[...] = jnp.zeros_like(sums_out)

    given = dot_right(low[...], weight[...]).astype(BF16)
    masks = head_masks(size)
    windows = low.shape[0] // PAD
    both = 2
    for first in range(0, windows, both):
        items = [
            (slice(w * PAD, (w + 1) * PAD), pair, g)
            for w in range(first, first + both)
            for pair in range(2)
            for g in range(pair_groups)
        ]
        qkv = (qkv0, qkv1)
        probs_of = (p0, p1)

        def part(item, t):
            r, pair, g = item
            return qkv[pair][r, t * width + g * LANES : t * width + (g + 1) * LANES]

        gs = [
            spread_heads(given[r, pair * width + g * LANES : pair * width + (g + 1) * LANES], masks)
            for r, pair, g in items
        ]
        prob_grad = [dot_right(part(i, 2), s) for i, s in zip(items, gs)]
        low_probs = [probs_of[pair][r, g * per : (g + 1) * per] for r, pair, g in items]
        probs = [p.astype(F32) for p in low_probs]
        weighed = [p * s for p, s in zip(probs, prob_grad)]
        score_low = [
            (t - p * jnp.sum(t, axis=0, keepdims=True)).astype(BF16) for p, t in zip(probs, weighed)
        ]
        dv = [dot(p, s).astype(BF16) for p, s in zip(low_probs, gs)]
        dk = [
            (dot(s, spread_heads(part(i, 0), masks)) * scale).astype(BF16)
            for i, s in zip(items, score_low)
        ]
        dq = [
            (fold_heads(dot_left(s, part(i, 1)), masks) * scale).astype(BF16)
            for i, s in zip(items, score_low)
        ]
        for (r, pair, g), *parts in zip(items, dq, dk, dv):
            for t, value in enumerate(parts):
                at = (pair * 3 + t) * width + g * LANES
                d_out[r, at : at + LANES] = value
        for pair in range(2):
            for g in range(pair_groups):
                mine = [n for n, (_, p, h) in enumerate(items) if (p, h) == (pair, g)]
                at = (pair * pair_groups + g) * per
                table_out[:, at : at + per] += sum(score_low[n].astype(F32) for n in mine)
                for t, values in enumerate((dq, dk, dv)):
                    at = (pair * 3 + t) * width + g * LANES
                    sums_out[0:1, at : at + LANES] += sum(
                        jnp.sum(values[n].astype(F32), axis=0, keepdims=True) for n in mine
                    )


def mixed_body(windows, count, att0, att1, *refs):
    wo = refs[:count]
    tokens, gains, offsets, mixed, normed, stacked = refs[count:]
    quarter = wo[0].shape[0]
    half = att0.shape[1]
    for k in range(count):
        stacked[k * quarter : (k + 1) * quarter, :] = wo[k][...]
    group = 4
    for first in range(0, windows, group):
        here = slice(first * PAD, (first + group) * PAD)
        total = dot(att0[here, :], stacked[0:half, :]) + dot(att1[here, :], stacked[half : 2 * half, :])
        for w in range(group):
            at = (first + w) * SPOTS
            mixed[at : at + SPOTS, :] = total[w * PAD : w * PAD + SPOTS, :]
    for r in range(0, tokens.shape[0], CHUNK):
        rows = slice(r, r + CHUNK)
        value = tokens[rows, :].astype(F32) + mixed[rows, :] + offsets[1:2, :]
        mixed[rows, :] = value
        nhat, _ = norm_parts(value)
        normed[rows, :] = (nhat * gains[1:2, :] + offsets[2:3, :]).astype(BF16)


def copies_of(pairs, sems, first=0):
    return [pltpu.make_async_copy(a, b, sems.at[first + i]) for i, (a, b) in enumerate(pairs)]


def pieces_of(pieces, target):
    at, pairs = 0, []
    for p in pieces:
        pairs.append((p, target.at[pl.ds(at, p.shape[0]), :]))
        at += p.shape[0]
    return pairs


def inner_body(count, pieces, started, last, *refs):
    refs = list(refs)
    take = lambda n: [refs.pop(0) for _ in range(n)]
    normed, bias = take(2)
    wi = take(count)
    wo = [take(pieces) for _ in range(count)]
    before = take(1)[0] if started else None
    if last:
        mixed, gains, offsets, crop = take(4)
    act_out, slope_out = take(count), take(count)
    if last:
        block_out, features, pool = take(3)
    else:
        total_out = take(1)[0]
    x, wi_v, wo_v, act, slope, total, sems, out_sems = take(8)
    if last:
        mixed_v = take(1)[0]
    pairs = [(normed, x)]
    for k in range(count):
        pairs += [(wi[k], wi_v.at[k])] + pieces_of(wo[k], wo_v.at[k])
    if started:
        pairs.append((before, total))
    if last:
        pairs.append((mixed, mixed_v))
    copies = copies_of(pairs, sems)
    for c in copies:
        c.start()
    copies.pop(0).wait()
    weights = [[copies.pop(0) for _ in range(1 + pieces)] for _ in range(count)]
    half = x.shape[0] // 2
    work = [(k, h) for k in range(count) for h in range(2)]

    def first(k, h):
        if h == 0:
            weights[k][0].wait()
        return dot(x[h * half : (h + 1) * half, :], wi_v[k]) + bias[k]

    out_pairs = [p for k in range(count) for p in ((act.at[k], act_out[k]), (slope.at[k], slope_out[k]))]
    if not last:
        out_pairs.append((total, total_out))
    outs = copies_of(out_pairs, out_sems)
    ahead = first(*work[0])
    for n, (k, h) in enumerate(work):
        pre = ahead
        if n + 1 < len(work):
            ahead = first(*work[n + 1])
        rows = slice(h * half, (h + 1) * half)
        value, grad = gelu_pair(pre)
        value = value.astype(BF16)
        act[k, rows, :] = value
        slope[k, rows, :] = grad.astype(BF16)
        if h == 1:
            outs[2 * k].start()
            outs[2 * k + 1].start()
        else:
            for c in weights[k][1:]:
                c.wait()
            if n == 0 and started:
                copies.pop(0).wait()
        share = dot(value, wo_v[k])
        if k == 0 and not started:
            total[rows, :] = share
        else:
            total[rows, :] += share
    if last:
        copies.pop(0).wait()
        crops = pool.shape[0]
        sums = [jnp.zeros((1, total.shape[1]), F32)] * crops
        for r in range(0, total.shape[0], CHUNK):
            rows = slice(r, r + CHUNK)
            value = mixed_v[rows, :] + total[rows, :] + offsets[3:4, :]
            block_out[rows, :] = value
            features[rows, :] = value.astype(BF16)
            nhat, _ = norm_parts(value)
            head = nhat * gains[2:3, :] + offsets[4:5, :]
            for c in range(crops):
                sums[c] = sums[c] + jnp.sum(jnp.where(crop[rows, :] == c, head, 0.0), axis=0, keepdims=True)
        for c in range(crops):
            pool[c : c + 1, :] = sums[c]
    else:
        outs[-1].start()
    for c in outs:
        c.wait()


def head_back_body(block_out, cotangent, crop, pooled_grad, gains, grad_out, low_out, sums_out):
    crops = pooled_grad.shape[0]

    @pl.when(pl.program_id(0) == 0)
    def _():
        sums_out[...] = jnp.zeros_like(sums_out)

    nhat, inv = norm_parts(block_out[...])
    grad = jnp.zeros(nhat.shape, F32)
    for c in range(crops):
        grad = jnp.where(crop[...] == c, pooled_grad[c : c + 1, :], grad)
    out = cotangent[...].astype(F32) + norm_back(nhat, inv, gains[2:3, :], grad)
    grad_out[...] = out
    low_out[...] = out.astype(BF16)
    sums_out[0:1, :] += jnp.sum(grad * nhat, axis=0, keepdims=True)
    sums_out[1:2, :] += jnp.sum(grad, axis=0, keepdims=True)
    sums_out[2:3, :] += jnp.sum(out, axis=0, keepdims=True)


def head_body(
    pooled, unit_grad, first_hbm, second_hbm, third_hbm, first_bias, second_bias, third_bias,
    first_act, second_act, units, embed_grad, second_low, first_low, pooled_grad,
    first, second, third, sems,
):
    chunk = 512
    parts = second.shape[0] // chunk
    rows_of = lambda i: pl.ds(i * chunk, chunk)
    pairs = [(first_hbm, first)]
    pairs += [(second_hbm.at[rows_of(i), :], second.at[rows_of(i), :]) for i in range(parts)]
    pairs += [(third_hbm, third)]
    copies = copies_of(pairs, sems)
    for c in copies:
        c.start()
    copies[0].wait()
    act, first_slope = gelu_pair(dot(pooled[...], first[...]) + first_bias[...])
    act = act.astype(BF16)
    first_act[...] = act
    total = second_bias[...]
    for i in range(parts):
        copies[1 + i].wait()
        total = total + dot(act[:, i * chunk : (i + 1) * chunk], second[i * chunk : (i + 1) * chunk, :])
    act, second_slope = gelu_pair(total)
    act = act.astype(BF16)
    second_act[...] = act
    copies[-1].wait()
    embedded = dot(act, third[...]) + third_bias[...]
    inv = lax.rsqrt(jnp.sum(embedded * embedded, axis=-1, keepdims=True) + 1e-06)
    units[...] = (embedded * inv).astype(BF16)
    given = unit_grad[...]
    along = jnp.sum(embedded * given, axis=-1, keepdims=True)
    grad = inv * given - (inv * inv * inv) * embedded * along
    embed_grad[...] = grad
    low = (dot_right(grad.astype(BF16), third[...]) * second_slope).astype(BF16)
    second_low[...] = low
    low = (dot_right(low, second[...]) * first_slope).astype(BF16)
    first_low[...] = low
    pooled_grad[...] = dot_right(low, first[...])


def inner_back_body(windows, pieces, started, last, *refs):
    refs = list(refs)
    take = lambda n: [refs.pop(0) for _ in range(n)]
    count = len(pieces)
    low_in, normed = take(2)
    act_in, slope_in, wi_in = take(count), take(count), take(count)
    wo_in = [take(n) for n in pieces]
    before = take(1)[0] if started else None
    if last:
        mixed, out_grad, gains = take(3)
    outer_out, inner_out = take(count), take(count)
    sums_out = take(1)[0]
    if last:
        grad_out, low_out, norm_sums = take(3)
    else:
        total_out = take(1)[0]
    low, x, act, slope, wi, wo, outer, inner, pre, total, sems, out_sems = take(12)
    first_of = []
    pairs = [(low_in, low)]
    for k in range(count):
        first_of.append(len(pairs))
        pairs += pieces_of(wo_in[k], wo.at[k]) + [(slope_in[k], slope.at[k]), (act_in[k], act.at[k])]
        pairs += [(normed, x)] * (k == 0) + [(wi_in[k], wi.at[k])]
    if started:
        pairs.append((before, total))
    rows_all = total.shape[0]
    if last:
        mixed_v, flat = take(2)
        pairs += [(mixed, mixed_v), (out_grad, flat.at[pl.ds(0, rows_all), :])]
    copies = copies_of(pairs, sems)
    for c in copies:
        c.start()
    wait = lambda n: [copies.pop(0).wait() for _ in range(n)]
    out_pairs = [p for k in range(count) for p in ((outer.at[k], outer_out[k]), (inner.at[k], inner_out[k]))]
    outs = copies_of(out_pairs + ([] if last else [(total, total_out)]), out_sems)
    wait(1)
    for k in range(count):
        wait(pieces[k])
        raw = dot_right(low[...], wo[k])
        wait(2)
        outer_value = dot_left(low[...], act[k])
        value = (raw * slope[k].astype(F32)).astype(BF16)
        pre[k] = value
        sums_out[k : k + 1, :] = jnp.sum(value.astype(F32), axis=0, keepdims=True)
        outer[k] = outer_value.astype(BF16)
        outs[2 * k].start()
        wait(2 if k == 0 else 1)
        inner[k] = dot_left(x[...], pre[k]).astype(BF16)
        outs[2 * k + 1].start()
        share = dot_right(pre[k], wi[k])
        if k == 0 and not started:
            total[...] = share
        else:
            if k == 0:
                copies.pop(sum(pieces[1:]) + 3 * (count - 1)).wait()
            total[...] += share
    if not last:
        outs[-1].start()
    if last:
        wait(2)
        gain_sum = jnp.zeros((1, total.shape[1]), F32)
        shift_sum = gain_sum
        bias_sum = gain_sum
        for r in range(0, rows_all, CHUNK):
            rows = slice(r, r + CHUNK)
            nhat, inv = norm_parts(mixed_v[rows, :])
            grad = total[rows, :]
            gain_sum = gain_sum + jnp.sum(grad * nhat, axis=0, keepdims=True)
            shift_sum = shift_sum + jnp.sum(grad, axis=0, keepdims=True)
            out = flat[rows, :] + norm_back(nhat, inv, gains[1:2, :], grad)
            bias_sum = bias_sum + jnp.sum(out, axis=0, keepdims=True)
            grad_out[rows, :] = out
            flat[rows, :] = out
        norm_sums[0:1, :] = gain_sum
        norm_sums[1:2, :] = shift_sum
        norm_sums[2:3, :] = bias_sum
        widen(windows, flat, low_out)
    for c in outs:
        c.wait()


def weight_grad_body(x, low, d, att0, att1, even_a, odd_a, even_b, odd_b):
    width = att0.shape[1]
    quarter = width // 2
    big = dot_left(x[...], d[...])
    for t, (even, odd, at) in enumerate(((even_a, odd_a, 0), (even_a, odd_a, 1), (even_b, odd_b, 0))):
        lanes = slice(at * quarter, (at + 1) * quarter)
        even[0, :, lanes] = big[:, t * width : t * width + quarter].astype(BF16)
        odd[0, :, lanes] = big[:, t * width + quarter : (t + 1) * width].astype(BF16)
    for pair, att in enumerate((att0, att1)):

        @pl.when(pl.program_id(0) == 1 - pair)
        def _(att=att):
            side = dot_left(low[...], att[...])
            even_b[0, :, quarter:width] = side[:, 0:quarter].astype(BF16)
            odd_b[0, :, quarter:width] = side[:, quarter:width].astype(BF16)


def tokens_back_body(windows, grads, stacked0, stacked1, tokens, mixed_grad, gains, head, mid, ends, grad_out, packed, flat):
    half = stacked0.shape[0]
    group = 4
    for first in range(0, windows, group):
        here = slice(first * PAD, (first + group) * PAD)
        total = dot(grads[here, 0:half], stacked0[...]) + dot(grads[here, half : 2 * half], stacked1[...])
        for w in range(group):
            at = (first + w) * SPOTS
            flat[at : at + SPOTS, :] = total[w * PAD : w * PAD + SPOTS, :]
    gain_sum = jnp.zeros((1, tokens.shape[1]), F32)
    shift_sum = gain_sum
    for r in range(0, tokens.shape[0], CHUNK):
        rows = slice(r, r + CHUNK)
        nhat, inv = norm_parts(tokens[rows, :].astype(F32))
        grad = flat[rows, :]
        gain_sum = gain_sum + jnp.sum(grad * nhat, axis=0, keepdims=True)
        shift_sum = shift_sum + jnp.sum(grad, axis=0, keepdims=True)
        grad_out[rows, :] = mixed_grad[rows, :] + norm_back(nhat, inv, gains[0:1, :], grad)
    packed[0:1, :] = gain_sum
    packed[1:2, :] = mid[0:1, :]
    packed[2:3, :] = head[0:1, :]
    packed[3:4, :] = shift_sum
    packed[4:5, :] = mid[2:3, :]
    packed[5:6, :] = mid[1:2, :]
    packed[6:7, :] = head[2:3, :]
    packed[7:8, :] = head[1:2, :]
    packed[8 : 8 + ends.shape[0], :] = ends[...]


def swap(values, axis, bit):
    return lax.ppermute(values, axis, [(i, i ^ bit) for i in range(lax.axis_size(axis))])


def bits_of(axis):
    size = lax.axis_size(axis)
    bit, found = 1, []
    while bit < size:
        found.append(bit)
        bit *= 2
    return found


def has_bit(axis, bit):
    return (lax.axis_index(axis) // bit) % 2 == 1


def after(values, *others):
    return lax.optimization_barrier((values, *others))[0]


def sum_over(values, axes):
    for axis in axes:
        for bit in bits_of(axis):
            values = values + swap(values, axis, bit)
    return values


def ordered(mine, other, upper):
    return jnp.concatenate([jnp.where(upper, other, mine), jnp.where(upper, mine, other)], axis=0)


def gather_over(values, axis):
    for bit in bits_of(axis):
        values = ordered(values, swap(values, axis, bit), has_bit(axis, bit))
    return values


def by_distance(values, axis):
    for bit in bits_of(axis):
        size = values.shape[0]
        folded = values.reshape(size // (2 * bit), 2, bit, *values.shape[1:])
        folded = jnp.where(has_bit(axis, bit), folded[:, ::-1], folded)
        values = folded.reshape(values.shape)
    return values


def own_half(values, share, piece=0, pieces=1):
    parts = values.reshape(2 * pieces, values.shape[0] // (2 * pieces), *values.shape[1:])
    return lax.dynamic_index_in_dim(parts, 2 * piece + lax.axis_index("dp") // share % 2, 0, keepdims=False)


def halve_rows(values, bit):
    groups, rows, columns = values.shape
    folded = values.reshape(groups // 2, 2, rows, columns)
    mine = lax.axis_index("dp") // bit % 2
    keep = lax.dynamic_index_in_dim(folded, mine, 1, keepdims=False)
    send = lax.dynamic_index_in_dim(folded, 1 - mine, 1, keepdims=False)
    return keep, send


def add(kept, got):
    return kept.astype(F32) + got.astype(F32)


def offset_table():
    places = jnp.arange(PAD, dtype=jnp.int32)
    row_of = places // SIDE
    col_of = places % SIDE
    offset = (row_of[None, :] - row_of[:, None] + SIDE - 1) * (2 * SIDE - 1) + (
        col_of[None, :] - col_of[:, None] + SIDE - 1
    )
    inside = (places[:, None] < SPOTS) & (places[None, :] < SPOTS)
    offset = jnp.where(inside, offset, -1)
    entries = jnp.arange((2 * SIDE - 1) ** 2, dtype=jnp.int32)
    return (offset.reshape(-1)[:, None] == entries[None, :]).astype(F32)


def shards(
    tokens,
    input_projection,
    input_bias,
    position_bias,
    output_projection,
    inner_weight,
    inner_bias,
    outer_weight,
    norm_gains,
    offsets,
    head_first,
    head_first_bias,
    head_second,
    head_second_bias,
    head_third,
    head_third_bias,
    prototype_direction,
    prototype_gain,
    crop_windows,
    first_epoch,
    feature_cotangent,
    logit_cotangent,
):
    rows, width = tokens.shape
    windows = rows // SPOTS
    narrow_index = lax.axis_index("narrow")
    dp_index = lax.axis_index("dp")
    count = lax.axis_size("narrow")
    groups = lax.axis_size("dp")
    quarter = input_projection.shape[2]
    hidden = inner_weight.shape[1]
    heads = position_bias.shape[1] // count
    size = quarter // heads
    scale = size ** (-0.5)
    crops = crop_windows.shape[1]
    padded_rows = windows * PAD

    near, far = bits_of("narrow")
    data_bits = bits_of("dp")
    share, share_too = data_bits[0], data_bits[1]

    w_in0 = input_projection.swapaxes(1, 2)
    w_in1 = swap(w_in0, "narrow", near)
    in_half = swap(own_half(w_in0.reshape(3 * quarter, width), share), "narrow", far)
    w_att1 = swap(output_projection, "narrow", near)
    w_inner1 = swap(inner_weight, "narrow", near)
    w_outer1 = swap(outer_weight, "narrow", near)

    bias_in = by_distance(input_bias.reshape(2, count, quarter).swapaxes(0, 1), "narrow")
    bias_in = bias_in.swapaxes(0, 1).reshape(2, count * quarter)
    bias_inner = by_distance(inner_bias.reshape(count, 1, hidden), "narrow")
    table = offset_table()
    turned = by_distance(position_bias.T.reshape(count, heads, -1), "narrow").reshape(count * heads, -1)
    spread = jnp.dot(table, turned.T, precision=HIGH, preferred_element_type=F32)
    spread = spread.reshape(PAD, PAD, count * heads).transpose(0, 2, 1)
    inside = (jnp.arange(PAD) < SPOTS)[:, None, None]
    spread = jnp.where(inside, spread, NEG).reshape(PAD, count * heads * PAD)

    ends = jnp.cumsum(crop_windows[0])
    row_window = narrow_index * windows + jnp.arange(rows, dtype=jnp.int32) // SPOTS
    crop_of_row = jnp.sum((row_window[:, None] >= ends[None, :]).astype(jnp.int32), axis=1, keepdims=True)
    crop_tokens = (crop_windows[0] * SPOTS).astype(F32)

    padded = call(
        functools.partial(norm_one_body, windows),
        shape((padded_rows, width), BF16),
        (tokens, norm_gains, offsets),
        scratch=[pltpu.VMEM((rows + 16, width), F32)],
        us=3.5,
    )
    half = 2 * quarter
    pair_lanes = 2 * heads * PAD
    batch = 4 * PAD
    by_row = lambda n: pl.BlockSpec((batch, n), lambda i: (i, 0))
    fixed = lambda *dims: pl.BlockSpec(dims, lambda i: (0,) * len(dims))
    qkv, probs, attended, stacked_in = [], [], [], []

    def attend(pair, x, first, second):
        got = pl.pallas_call(
            functools.partial(attend_body, size, scale),
            grid=(padded_rows // batch,),
            out_shape=(
                shape((padded_rows, 3 * half), BF16),
                shape((padded_rows, pair_lanes), BF16),
                shape((padded_rows, half), BF16),
                shape((3, half, width), BF16),
            ),
            in_specs=[
                by_row(width),
                fixed(3, quarter, width),
                fixed(3, quarter, width),
                fixed(2, half),
                pl.BlockSpec((PAD, pair_lanes), lambda i, pair=pair: (0, pair)),
            ],
            out_specs=(by_row(3 * half), by_row(pair_lanes), by_row(half), fixed(3, half, width)),
            compiler_params=pltpu.CompilerParams(vmem_limit_bytes=VMEM_LIMIT),
            cost_estimate=cost(9.0),
        )(x, first, second, bias_in[:, pair * half : (pair + 1) * half], spread)
        for keep, value in zip((qkv, probs, attended, stacked_in), got):
            keep.append(value)
        return got

    def whole_of(mine, other, bit):
        return ordered(mine, other, has_bit("dp", bit))

    def bring(weight, bit, *others, piece=0, pieces=1):
        return swap(own_half(after(weight, *others), bit, piece, pieces), "narrow", far)

    in_half, w_in1 = after((in_half, w_in1), padded, spread)
    in_rest = swap(in_half, "dp", share)
    w_att2 = swap(after(output_projection, in_half), "narrow", far)
    got = attend(0, after(padded, in_half), w_in0, w_in1)
    in_rest, w_att2 = after((in_rest, w_att2), got)
    inner_half = bring(inner_weight, share, w_att2)
    w_in2 = whole_of(in_half, in_rest, share).reshape(w_in0.shape)
    w_in3 = swap(w_in2, "narrow", near)
    w_att3 = swap(w_att2, "narrow", near)
    got = attend(1, after(padded, got), w_in2, w_in3)
    w_att3, inner_half = after((w_att3, inner_half), got)
    outer_half = bring(outer_weight, share_too, inner_half)
    inner_rest = swap(inner_half, "dp", share)
    mixed, normed_two, stacked_att = call(
        functools.partial(mixed_body, windows, count),
        (shape((rows, width), F32), shape((rows, width), BF16), shape((count * quarter, width), BF16)),
        (
            *attended,
            output_projection, w_att1, w_att2, w_att3,
            after(tokens, inner_half),
            norm_gains,
            offsets,
        ),
        us=6.0,
    )
    anywhere = pl.BlockSpec(memory_space=pl.ANY)
    held = pl.BlockSpec(memory_space=pltpu.VMEM)
    row_held = pltpu.VMEM((rows, width), F32)
    low_held = pltpu.VMEM((rows, width), BF16)
    act_shape = shape((rows, hidden), BF16)

    def inner_call(x, bias, wi, wo, before=(), ending=()):
        n, pieces = len(wi), len(wo[0])
        wo = [p for w in wo for p in w]
        last = bool(ending)
        tail_shape = (shape((rows, width), F32),)
        tail_spec = (anywhere,)
        if last:
            tail_shape += (shape((rows, width), BF16), shape((crops, width), F32))
            tail_spec = (held,) * 3
        return pl.pallas_call(
            functools.partial(inner_body, n, pieces, bool(before), last),
            out_shape=(act_shape,) * (2 * n) + tail_shape,
            in_specs=[anywhere, held] + [anywhere] * (len(wi) + len(wo) + len(before)) + ([anywhere] + [held] * 3 if last else []),
            out_specs=(anywhere,) * (2 * n) + tail_spec,
            scratch_shapes=[
                low_held,
                pltpu.VMEM((n, width, hidden), BF16),
                pltpu.VMEM((n, hidden, width), BF16),
                pltpu.VMEM((n, rows, hidden), BF16),
                pltpu.VMEM((n, rows, hidden), BF16),
                row_held,
                pltpu.SemaphoreType.DMA((1 + n * (1 + pieces) + len(before) + last,)),
                pltpu.SemaphoreType.DMA((2 * n + 1,)),
            ] + ([row_held] if last else []),
            compiler_params=pltpu.CompilerParams(vmem_limit_bytes=VMEM_LIMIT),
            cost_estimate=cost(16.0 if last else 7.0),
        )(x, bias, *wi, *wo, *before, *ending)

    act0, slope0, inner_total = inner_call(normed_two, bias_inner[0:1], [inner_weight], [[outer_weight]])
    outer_half, inner_rest = after((outer_half, inner_rest), inner_total)
    outer_rest = swap(outer_half, "dp", share_too)
    w_inner2 = whole_of(inner_half, inner_rest, share)
    w_inner3 = swap(w_inner2, "narrow", near)
    act1, slope1, inner_total = inner_call(
        after(normed_two, outer_half, w_inner2), bias_inner[1:2], [w_inner1], [[w_outer1]], (inner_total,)
    )
    direction = after(prototype_direction, inner_total).astype(F32)
    column_inv = lax.rsqrt(jnp.sum(direction * direction, axis=0, keepdims=True) + 1e-06)
    columns_low = (prototype_gain * direction * column_inv).astype(BF16)
    unit_share = dot_right(logit_cotangent, columns_low)
    w_inner3, outer_rest = after((w_inner3, outer_rest), unit_share)
    w_outer2 = whole_of(outer_half, outer_rest, share_too)
    w_outer3 = swap(w_outer2, "narrow", near)
    outer2, outer3 = [w_outer2], [w_outer3]
    act2, act3, slope2, slope3, block_out, features, pool = inner_call(
        normed_two, bias_inner[2:4], [w_inner2, w_inner3], [outer2, outer3], (inner_total,),
        (mixed, norm_gains, offsets, crop_of_row),
    )

    flat_pool = pool.reshape(-1, LANES)
    pool_rows = flat_pool.shape[0]
    unit_rows = unit_share.reshape(-1, LANES)
    both = sum_over(jnp.concatenate([flat_pool, unit_rows]), ("narrow",))
    gathered, unit_rows = both[:pool_rows], both[pool_rows:]
    per_crop = jnp.repeat(crop_tokens, width // LANES)[:, None]
    gathered = gathered / per_crop
    for bit in data_bits:
        other = swap(jnp.concatenate([gathered, unit_rows]), "dp", bit)
        unit_rows = unit_rows + other[gathered.shape[0] :]
        gathered = ordered(gathered, other[: gathered.shape[0]], has_bit("dp", bit))
    unit_grad = unit_rows.reshape(unit_share.shape)
    pooled = gathered.reshape(-1, width).astype(BF16)
    all_crops, units_width = unit_grad.shape
    head_width = head_first.shape[1]
    first_act, second_act, units, embed_grad, second_low, first_low, pooled_grad = pl.pallas_call(
        head_body,
        out_shape=(
            shape((all_crops, head_width), BF16),
            shape((all_crops, head_width), BF16),
            shape((all_crops, units_width), BF16),
            shape((all_crops, units_width), F32),
            shape((all_crops, head_width), BF16),
            shape((all_crops, head_width), BF16),
            shape((all_crops, width), F32),
        ),
        in_specs=[held, held, anywhere, anywhere, anywhere, held, held, held],
        out_specs=(held,) * 7,
        scratch_shapes=[
            pltpu.VMEM(head_first.shape, BF16),
            pltpu.VMEM(head_second.shape, BF16),
            pltpu.VMEM(head_third.shape, BF16),
            pltpu.SemaphoreType.DMA((2 + head_second.shape[0] // 512,)),
        ],
        compiler_params=pltpu.CompilerParams(vmem_limit_bytes=VMEM_LIMIT),
        cost_estimate=cost(9.0),
    )(
        pooled, unit_grad, head_first, head_second, head_third,
        head_first_bias[None], head_second_bias[None], head_third_bias[None],
    )
    embed_low = embed_grad.astype(BF16)
    pooled_grad = lax.dynamic_slice_in_dim(pooled_grad, dp_index * crops, crops, 0) / crop_tokens[:, None]

    split = rows // 2
    by_chunk = lambda n: pl.BlockSpec((split, n), lambda i: (i, 0))
    out_grad, out_low, head_sums = pl.pallas_call(
        head_back_body,
        grid=(2,),
        out_shape=(shape((rows, width), F32), shape((rows, width), BF16), shape((3, width), F32)),
        in_specs=[by_chunk(width), by_chunk(width), by_chunk(1), fixed(crops, width), fixed(*norm_gains.shape)],
        out_specs=(by_chunk(width), by_chunk(width), fixed(3, width)),
        compiler_params=pltpu.CompilerParams(vmem_limit_bytes=VMEM_LIMIT),
        cost_estimate=cost(4.0),
    )(block_out, feature_cotangent, crop_of_row, pooled_grad, norm_gains)

    def by_group(part):
        return part.reshape(groups, part.shape[0] // groups, part.shape[1])

    def inner_back(act, slope, wi, wo, before=(), ending=()):
        last = bool(ending)
        n = len(wi)
        pieces = tuple(len(w) for w in wo)
        wo = [p for w in wo for p in w]
        outs = [shape((width, hidden), BF16)] * (2 * n) + [shape((n, hidden), F32), shape((rows, width), F32)]
        specs = [anywhere] * (2 * n) + [held, held if last else anywhere]
        if last:
            outs += [shape((padded_rows, width), BF16), shape((3, width), F32)]
            specs += [held, held]
        return pl.pallas_call(
            functools.partial(inner_back_body, windows, pieces, bool(before), last),
            out_shape=tuple(outs),
            in_specs=[anywhere] * (2 + 3 * n + len(wo) + len(before)) + ([anywhere, anywhere, held] if last else []),
            out_specs=tuple(specs),
            scratch_shapes=[
                low_held,
                low_held,
                pltpu.VMEM((n, rows, hidden), BF16),
                pltpu.VMEM((n, rows, hidden), BF16),
                pltpu.VMEM((n, width, hidden), BF16),
                pltpu.VMEM((n, hidden, width), BF16),
                pltpu.VMEM((n, width, hidden), BF16),
                pltpu.VMEM((n, width, hidden), BF16),
                pltpu.VMEM((n, rows, hidden), BF16),
                row_held,
                pltpu.SemaphoreType.DMA((2 + 3 * n + len(wo) + len(before) + 2 * last,)),
                pltpu.SemaphoreType.DMA((2 * n + 1,)),
            ] + ([row_held, pltpu.VMEM((rows + 16, width), F32)] if last else []),
            compiler_params=pltpu.CompilerParams(vmem_limit_bytes=VMEM_LIMIT),
            cost_estimate=cost(18.0 if last else 15.0),
        )(out_low, normed_two, *act, *slope, *wi, *wo, *before, *ending)

    o3, o1, i3, i1, sums_odd, total = inner_back([act3, act1], [slope3, slope1], [w_inner3, w_inner1], [outer3, [w_outer1]])
    got_o3, got_i3 = swap(o3, "narrow", near), swap(i3, "narrow", near)
    got_o1, got_i1 = swap(o1, "narrow", near), swap(i1, "narrow", near)
    o2, o0, i2, i0, sums_even, mixed_grad, mixed_low, mixed_sums = inner_back(
        [act2, act0], [slope2, slope0], [w_inner2, inner_weight], [outer2, [outer_weight]],
        (total,), (mixed, out_grad, norm_gains),
    )
    got_o3, got_i3, got_o1, got_i1 = after((got_o3, got_i3, got_o1, got_i1), mixed_low)
    sum_i2 = add(i2, got_i3).astype(BF16)
    keep_o2, send_o2 = halve_rows(by_group(add(o2, got_o3).astype(BF16)), share)
    keep_o0, send_o0 = halve_rows(by_group(add(o0, got_o1).astype(BF16)), share)
    got_i2 = swap(sum_i2, "narrow", far)
    got_o2 = swap(send_o2, "dp", share)
    got_o0 = swap(send_o0, "dp", share)
    sums0, sums1, sums2, sums3 = sums_even[1:2], sums_odd[1:2], sums_even[0:1], sums_odd[0:1]
    mixed_low = after(mixed_low, sum_i2, send_o0, send_o2)

    input_grads, pair_grads, input_sums = pl.pallas_call(
        functools.partial(attend_back_body, size, scale),
        grid=(padded_rows // batch,),
        out_shape=(
            shape((padded_rows, 6 * half), BF16),
            shape((PAD, 2 * pair_lanes), F32),
            shape((1, 6 * half), F32),
        ),
        in_specs=[
            by_row(width),
            fixed(count * quarter, width),
            by_row(3 * half),
            by_row(3 * half),
            by_row(pair_lanes),
            by_row(pair_lanes),
        ],
        out_specs=(by_row(6 * half), fixed(PAD, 2 * pair_lanes), fixed(1, 6 * half)),
        compiler_params=pltpu.CompilerParams(vmem_limit_bytes=VMEM_LIMIT),
        cost_estimate=cost(13.0),
    )(mixed_low, stacked_att, *qkv, *probs)

    input_sum = input_sums.reshape(2, 3, 2, quarter).transpose(0, 2, 1, 3).reshape(count, 3, quarter)
    input_sum = by_distance(input_sum, "narrow").swapaxes(0, 1).reshape(3, count * quarter)
    inner_sum = by_distance(jnp.concatenate([sums0, sums1, sums2, sums3]), "narrow").reshape(-1, width)
    ends_in = jnp.concatenate([input_sum[0:1], input_sum[2:3], inner_sum])
    packed_rows = 8 + ends_in.shape[0]
    tokens_grad, packed = call(
        functools.partial(tokens_back_body, windows),
        (shape((rows, width), F32), shape((packed_rows, width), F32)),
        (
            input_grads,
            *[v.reshape(3 * half, width) for v in stacked_in],
            tokens,
            mixed_grad,
            norm_gains,
            head_sums,
            mixed_sums,
            ends_in,
        ),
        scratch=[pltpu.VMEM((rows, width), F32)],
        us=10.0,
    )

    got_i2, got_o2, got_o0 = after((got_i2, got_o2, got_o0), tokens_grad)
    far_o = add(keep_o2, got_o2).astype(BF16)
    got_o = swap(far_o, "narrow", far)
    keep_i, send_i = halve_rows(by_group(add(add(i0, got_i1).astype(BF16), got_i2).astype(BF16)), share)
    got_i = swap(send_i, "dp", share)
    near_o = add(keep_o0, got_o0).astype(BF16)
    input_grads = after(input_grads, send_i, far_o)

    pair_shape = shape((2, width, half), BF16)
    pair_spec = pl.BlockSpec((1, width, half), lambda i: (1 - i, 0, 0))
    even_a, odd_a, even_b, odd_b = pl.pallas_call(
        weight_grad_body,
        grid=(2,),
        out_shape=(pair_shape,) * 4,
        in_specs=[
            fixed(padded_rows, width),
            fixed(padded_rows, width),
            pl.BlockSpec((padded_rows, 3 * half), lambda i: (0, 1 - i)),
            fixed(padded_rows, half),
            fixed(padded_rows, half),
        ],
        out_specs=(pair_spec,) * 4,
        compiler_params=pltpu.CompilerParams(vmem_limit_bytes=VMEM_LIMIT),
        cost_estimate=cost(12.0),
    )(padded, mixed_low, input_grads, *attended)
    got_a, got_b = swap(odd_a, "narrow", near), swap(odd_b, "narrow", near)

    got_i, got_o = after((got_i, got_o), even_a)
    mlp = jnp.concatenate([add(keep_i, got_i), add(near_o, got_o)], axis=2).astype(BF16)
    keep_m, send_m = halve_rows(mlp, data_bits[1])
    got_m = swap(send_m, "dp", data_bits[1])
    got_a, got_b = after((got_a, got_b), send_m)
    sum_a = add(even_a, got_a).astype(BF16)
    keep_b, send_b = halve_rows(add(even_b, got_b).astype(BF16).reshape(2 * groups, width // groups, half), share)
    got_a2 = swap(sum_a[1], "narrow", far)
    got_b2 = swap(send_b, "dp", share)

    pair_grads = after(pair_grads, sum_a, send_b)
    pair_grad = pair_grads.reshape(PAD, count * heads, PAD).transpose(1, 0, 2)
    table_grad = lax.dot_general(
        pair_grad.reshape(count * heads, PAD * PAD), table, (((1,), (0,)), ((), ())),
        precision=HIGH, preferred_element_type=F32,
    )
    offsets_count = table_grad.shape[1]
    table_grad = by_distance(table_grad.reshape(count, heads, offsets_count), "narrow").reshape(table_grad.shape)
    table_rows = jnp.pad(table_grad, ((0, 0), (0, 256 - offsets_count))).reshape(-1, width)
    small = jnp.concatenate([packed, table_rows])
    small_bits = [("narrow", near), ("narrow", far)] + [("dp", b) for b in data_bits]
    small_got = swap(small, *small_bits[0])

    got_a2, got_b2 = after((got_a2, got_b2), small)
    keep_a, send_a = halve_rows(by_group(add(sum_a[0], got_a2).astype(BF16)), share)
    got_a = swap(send_a, "dp", share)
    sum_b = add(keep_b, got_b2).astype(BF16).reshape(2, groups // 2, width // groups, half)
    got_b = swap(sum_b[1], "narrow", far)
    small_got, got_m = after((small_got, got_m), send_a, sum_b)
    small = small + small_got
    small_got = swap(small, *small_bits[1])
    keep_m, send_m = halve_rows(add(keep_m, got_m).astype(BF16), data_bits[2])
    got_m = swap(send_m, "dp", data_bits[2])

    units, columns_low, direction = after((units, columns_low, direction), send_m, small)
    logits = dot(units, columns_low)
    column_grad = dot_left(units, logit_cotangent)
    keep = (1 - first_epoch).astype(F32)[None, :]
    along = jnp.sum(column_grad * direction, axis=0, keepdims=True)
    gain_grad = (keep * column_inv * along)[0]
    direction_grad = (keep * prototype_gain) * (
        column_inv * column_grad - (column_inv**3 * along) * direction
    )

    got_a, got_b, small_got = after((got_a, got_b, small_got), direction_grad, logits)
    att_sum = jnp.concatenate([add(keep_a, got_a), add(sum_b[0], got_b)], axis=2).astype(BF16)
    keep_j, send_j = halve_rows(att_sum, data_bits[1])
    got_j = swap(send_j, "dp", data_bits[1])
    small = small + small_got
    small_got = swap(small, *small_bits[2])

    def own(values):
        part = values.shape[1] // groups
        return lax.dynamic_slice_in_dim(values, dp_index * part, part, 1)

    first_low, second_low, second_act, embed_grad = after((first_low, second_low, second_act, embed_grad), send_j, small)
    own_first, own_second = own(first_low), own(second_low)
    own_embed = own(embed_grad)
    first_grad = dot_left(pooled, own_first)
    second_grad = dot_left(first_act, own_second)
    third_grad = dot_left(own(second_act), embed_low)

    got_j, small_got = after((got_j, small_got), first_grad, second_grad, third_grad)
    joined = add(keep_j, got_j)
    for bit in data_bits[2:-1]:
        keep_j, send_j = halve_rows(joined.astype(BF16), bit)
        joined = add(keep_j, swap(send_j, "dp", bit))
    keep_j, send_j = halve_rows(joined.astype(BF16), data_bits[-1])
    got_j = swap(send_j, "dp", data_bits[-1])
    small = small + small_got
    small_got = swap(small, *small_bits[3])
    got_m = after(got_m, send_j)
    mlp = add(keep_m, got_m)
    for bit in data_bits[3:]:
        keep_m, send_m = halve_rows(mlp.astype(BF16), bit)
        mlp = add(keep_m, swap(send_m, "dp", bit))
    first_bias_grad = jnp.sum(own_first.astype(F32), axis=0)
    second_bias_grad = jnp.sum(own_second.astype(F32), axis=0)
    third_bias_grad = jnp.sum(own_embed, axis=0)
    small_got = after(small_got, mlp)
    small = small + small_got
    for place in small_bits[4:]:
        small = small + swap(small, *place)
    joined = add(keep_j, after(got_j, mlp))
    inner_total, outer_total = mlp[0, :, :hidden], mlp[0, :, hidden:]
    joined = joined[0]
    attend_total = joined[:, 3 * quarter :]
    input_total = jnp.stack([joined[:, i * quarter : (i + 1) * quarter] for i in range(3)])

    gain_total, offset_total, bias_total = small[0:3], small[3:8], small[8:10]
    inner_bias_total = small[10 : 10 + inner_sum.shape[0]].reshape(-1)
    table_total = small[10 + inner_sum.shape[0] :].reshape(count * heads, 256)[:, :offsets_count].T
    return (
        features,
        logits,
        tokens_grad,
        input_total,
        bias_total,
        table_total,
        attend_total.T,
        inner_total,
        inner_bias_total,
        outer_total.T,
        gain_total,
        offset_total,
        first_grad,
        first_bias_grad,
        second_grad,
        second_bias_grad,
        third_grad,
        third_bias_grad,
        direction_grad,
        gain_grad,
    )


def solution(mesh):
    placed = (
        P(("dp", "narrow"), None),
        P(None, None, "narrow"),
        P(),
        P(),
        P("narrow", None),
        P(None, "narrow"),
        P(),
        P("narrow", None),
        P(),
        P(),
        P(),
        P(),
        P(),
        P(),
        P(),
        P(),
        P(None, ("dp", "narrow")),
        P(("dp", "narrow")),
        P("dp", None),
        P(("dp", "narrow")),
        P(("dp", "narrow"), None),
        P(None, ("dp", "narrow")),
    )
    return jax.shard_map(
        shards,
        mesh=mesh,
        in_specs=placed,
        out_specs=(
            P(("dp", "narrow"), None),
            P(None, ("dp", "narrow")),
            P(("dp", "narrow"), None),
            P(None, "dp", "narrow"),
            P(),
            P(),
            P("narrow", "dp"),
            P("dp", "narrow"),
            P(),
            P("narrow", "dp"),
            P(),
            P(),
            P(None, "dp"),
            P("dp"),
            P(None, "dp"),
            P("dp"),
            P("dp", None),
            P("dp"),
            P(None, ("dp", "narrow")),
            P(("dp", "narrow")),
        ),
        check_vma=False,
    )
```

```python
import functools

import jax
import jax.numpy as jnp
from jax import lax
from jax.experimental import pallas as pl
from jax.experimental.pallas import tpu as pltpu
from jax.sharding import PartitionSpec as P

HIGH = lax.Precision.HIGHEST
F32 = jnp.float32
BF16 = jnp.bfloat16
SIDE = 7
SPOTS = SIDE * SIDE
PAD = 64
LANES = 128
CHUNK = 112
VMEM_LIMIT = 60 * 1024 * 1024
NEG = -1e30


def dot(left, right):
    return jnp.dot(left, right, preferred_element_type=F32)


def dot_left(left, right):
    return lax.dot_general(left, right, (((0,), (0,)), ((), ())), preferred_element_type=F32)


def dot_right(left, right):
    return lax.dot_general(left, right, (((1,), (1,)), ((), ())), preferred_element_type=F32)


def cost(us):
    return pl.CostEstimate(flops=0, bytes_accessed=int(us * 3.3e6), transcendentals=0)


def call(body, outs, ins, **kw):
    scratch = kw.pop("scratch", ())
    return pl.pallas_call(
        body,
        out_shape=outs,
        in_specs=[pl.BlockSpec(memory_space=pltpu.VMEM)] * len(ins),
        out_specs=jax.tree.map(lambda _: pl.BlockSpec(memory_space=pltpu.VMEM), outs),
        scratch_shapes=scratch,
        compiler_params=pltpu.CompilerParams(vmem_limit_bytes=VMEM_LIMIT),
        cost_estimate=cost(kw.pop("us")),
        **kw,
    )(*ins)


def shape(dims, kind):
    return jax.ShapeDtypeStruct(dims, kind)


def norm_parts(values):
    center = values - jnp.mean(values, axis=-1, keepdims=True)
    spread = jnp.mean(center * center, axis=-1, keepdims=True)
    inv = lax.rsqrt(spread + 1e-05)
    return center * inv, inv


def norm_back(nhat, inv, gain, grad):
    scaled = grad * gain
    first = jnp.mean(scaled, axis=-1, keepdims=True)
    second = jnp.mean(scaled * nhat, axis=-1, keepdims=True)
    return (scaled - first - nhat * second) * inv


def gelu_pair(pre):
    bell = jnp.exp(pre * pre * -0.5)
    dist = jnp.abs(pre) * (0.3275911 * 0.70710678118654752) + 1.0
    inv = 1.0 / dist
    poly = 0.5 * 1.061405429
    for coef in (-1.453152027, 1.421413741, -0.284496736, 0.254829592):
        poly = poly * inv + 0.5 * coef
    tail = poly * inv * bell
    cdf = jnp.where(pre < 0.0, tail, 1.0 - tail)
    return pre * cdf, cdf + pre * (bell * 0.3989422804014327)


def widen(windows, flat, padded):
    place = lax.broadcasted_iota(jnp.int32, (PAD, 1), 0)
    for w in range(windows):
        block = flat[w * SPOTS : w * SPOTS + PAD, :]
        padded[w * PAD : (w + 1) * PAD, :] = jnp.where(place < SPOTS, block, 0.0).astype(BF16)


def norm_one_body(windows, tokens, gains, offsets, padded, flat):
    for r in range(0, tokens.shape[0], CHUNK):
        nhat, _ = norm_parts(tokens[r : r + CHUNK, :].astype(F32))
        flat[r : r + CHUNK, :] = nhat * gains[0:1, :] + offsets[0:1, :]
    widen(windows, flat, padded)


def head_masks(size):
    lane = lax.broadcasted_iota(jnp.int32, (PAD, LANES), 1) // size
    return [lane == h for h in range(LANES // size)]


def spread_heads(values, masks):
    zero = jnp.zeros_like(values)
    return jnp.concatenate([jnp.where(m, values, zero) for m in masks], axis=0)


def fold_heads(values, masks):
    total = values[0:PAD, :]
    for h in range(1, len(masks)):
        total = jnp.where(masks[h], values[h * PAD : (h + 1) * PAD, :], total)
    return total


def attend_body(size, scale, padded, near, far, bias, table, qkv_out, p_out, att_out, stacked):
    quarter = near.shape[1]
    width = 2 * quarter
    per = LANES // size * PAD

    @pl.when(pl.program_id(0) == 0)
    def _():
        stacked[:, 0:quarter, :] = near[...]
        stacked[:, quarter:width, :] = far[...]

    x = padded[...]
    q = (dot_right(x, stacked[0]) + bias[0:1, :]).astype(BF16)
    k = dot_right(x, stacked[1]).astype(BF16)
    v = (dot_right(x, stacked[2]) + bias[1:2, :]).astype(BF16)
    qkv_out[:, 0:width] = q
    qkv_out[:, width : 2 * width] = k
    qkv_out[:, 2 * width : 3 * width] = v
    masks = head_masks(size)
    items = [
        (slice(w * PAD, (w + 1) * PAD), g) for w in range(x.shape[0] // PAD) for g in range(width // LANES)
    ]
    lanes = lambda g: slice(g * LANES, (g + 1) * LANES)
    scores = [
        dot_right(k[r, lanes(g)], spread_heads(q[r, lanes(g)], masks)) * scale
        + table[:, g * per : (g + 1) * per]
        for r, g in items
    ]
    e = [jnp.exp(s - jnp.max(s, axis=0, keepdims=True)) for s in scores]
    probs = [(s * (1.0 / jnp.sum(s, axis=0, keepdims=True))).astype(BF16) for s in e]
    folded = [fold_heads(dot_left(p, v[r, lanes(g)]), masks) for p, (r, g) in zip(probs, items)]
    for (r, g), p, o in zip(items, probs, folded):
        p_out[r, g * per : (g + 1) * per] = p
        att_out[r, lanes(g)] = o.astype(BF16)


def attend_back_body(size, scale, low, weight, qkv0, qkv1, p0, p1, d_out, table_out, sums_out):
    width = qkv0.shape[1] // 3
    per = LANES // size * PAD
    pair_groups = width // LANES

    @pl.when(pl.program_id(0) == 0)
    def _():
        table_out[...] = jnp.zeros_like(table_out)
        sums_out[...] = jnp.zeros_like(sums_out)

    given = dot_right(low[...], weight[...]).astype(BF16)
    masks = head_masks(size)
    windows = low.shape[0] // PAD
    both = 2
    for first in range(0, windows, both):
        items = [
            (slice(w * PAD, (w + 1) * PAD), pair, g)
            for w in range(first, first + both)
            for pair in range(2)
            for g in range(pair_groups)
        ]
        qkv = (qkv0, qkv1)
        probs_of = (p0, p1)

        def part(item, t):
            r, pair, g = item
            return qkv[pair][r, t * width + g * LANES : t * width + (g + 1) * LANES]

        gs = [
            spread_heads(given[r, pair * width + g * LANES : pair * width + (g + 1) * LANES], masks)
            for r, pair, g in items
        ]
        prob_grad = [dot_right(part(i, 2), s) for i, s in zip(items, gs)]
        low_probs = [probs_of[pair][r, g * per : (g + 1) * per] for r, pair, g in items]
        probs = [p.astype(F32) for p in low_probs]
        weighed = [p * s for p, s in zip(probs, prob_grad)]
        score_low = [
            (t - p * jnp.sum(t, axis=0, keepdims=True)).astype(BF16) for p, t in zip(probs, weighed)
        ]
        dv = [dot(p, s).astype(BF16) for p, s in zip(low_probs, gs)]
        dk = [
            (dot(s, spread_heads(part(i, 0), masks)) * scale).astype(BF16)
            for i, s in zip(items, score_low)
        ]
        dq = [
            (fold_heads(dot_left(s, part(i, 1)), masks) * scale).astype(BF16)
            for i, s in zip(items, score_low)
        ]
        for (r, pair, g), *parts in zip(items, dq, dk, dv):
            for t, value in enumerate(parts):
                at = (pair * 3 + t) * width + g * LANES
                d_out[r, at : at + LANES] = value
        for pair in range(2):
            for g in range(pair_groups):
                mine = [n for n, (_, p, h) in enumerate(items) if (p, h) == (pair, g)]
                at = (pair * pair_groups + g) * per
                table_out[:, at : at + per] += sum(score_low[n].astype(F32) for n in mine)
                for t, values in enumerate((dq, dk, dv)):
                    at = (pair * 3 + t) * width + g * LANES
                    sums_out[0:1, at : at + LANES] += sum(
                        jnp.sum(values[n].astype(F32), axis=0, keepdims=True) for n in mine
                    )


def mixed_body(windows, count, att0, att1, *refs):
    wo = refs[:count]
    tokens, gains, offsets, mixed, normed, stacked = refs[count:]
    quarter = wo[0].shape[0]
    half = att0.shape[1]
    for k in range(count):
        stacked[k * quarter : (k + 1) * quarter, :] = wo[k][...]
    group = 4
    for first in range(0, windows, group):
        here = slice(first * PAD, (first + group) * PAD)
        total = dot(att0[here, :], stacked[0:half, :]) + dot(att1[here, :], stacked[half : 2 * half, :])
        for w in range(group):
            at = (first + w) * SPOTS
            mixed[at : at + SPOTS, :] = total[w * PAD : w * PAD + SPOTS, :]
    for r in range(0, tokens.shape[0], CHUNK):
        rows = slice(r, r + CHUNK)
        value = tokens[rows, :].astype(F32) + mixed[rows, :] + offsets[1:2, :]
        mixed[rows, :] = value
        nhat, _ = norm_parts(value)
        normed[rows, :] = (nhat * gains[1:2, :] + offsets[2:3, :]).astype(BF16)


def copies_of(pairs, sems, first=0):
    return [pltpu.make_async_copy(a, b, sems.at[first + i]) for i, (a, b) in enumerate(pairs)]


def pieces_of(pieces, target):
    at, pairs = 0, []
    for p in pieces:
        pairs.append((p, target.at[pl.ds(at, p.shape[0]), :]))
        at += p.shape[0]
    return pairs


def inner_body(count, pieces, started, last, *refs):
    refs = list(refs)
    take = lambda n: [refs.pop(0) for _ in range(n)]
    normed, bias = take(2)
    wi = take(count)
    wo = [take(pieces) for _ in range(count)]
    before = take(1)[0] if started else None
    if last:
        mixed, gains, offsets, crop = take(4)
    act_out, slope_out = take(count), take(count)
    if last:
        block_out, features, pool = take(3)
    else:
        total_out = take(1)[0]
    x, wi_v, wo_v, act, slope, total, sems, out_sems = take(8)
    if last:
        mixed_v = take(1)[0]
    pairs = [(normed, x)]
    for k in range(count):
        pairs += [(wi[k], wi_v.at[k])] + pieces_of(wo[k], wo_v.at[k])
    if started:
        pairs.append((before, total))
    if last:
        pairs.append((mixed, mixed_v))
    copies = copies_of(pairs, sems)
    for c in copies:
        c.start()
    copies.pop(0).wait()
    weights = [[copies.pop(0) for _ in range(1 + pieces)] for _ in range(count)]
    half = x.shape[0] // 2
    work = [(k, h) for k in range(count) for h in range(2)]

    def first(k, h):
        if h == 0:
            weights[k][0].wait()
        return dot(x[h * half : (h + 1) * half, :], wi_v[k]) + bias[k]

    out_pairs = [p for k in range(count) for p in ((act.at[k], act_out[k]), (slope.at[k], slope_out[k]))]
    if not last:
        out_pairs.append((total, total_out))
    outs = copies_of(out_pairs, out_sems)
    ahead = first(*work[0])
    for n, (k, h) in enumerate(work):
        pre = ahead
        if n + 1 < len(work):
            ahead = first(*work[n + 1])
        rows = slice(h * half, (h + 1) * half)
        value, grad = gelu_pair(pre)
        value = value.astype(BF16)
        act[k, rows, :] = value
        slope[k, rows, :] = grad.astype(BF16)
        if h == 1:
            outs[2 * k].start()
            outs[2 * k + 1].start()
        else:
            for c in weights[k][1:]:
                c.wait()
            if n == 0 and started:
                copies.pop(0).wait()
        share = dot(value, wo_v[k])
        if k == 0 and not started:
            total[rows, :] = share
        else:
            total[rows, :] += share
    if last:
        copies.pop(0).wait()
        crops = pool.shape[0]
        sums = [jnp.zeros((1, total.shape[1]), F32)] * crops
        for r in range(0, total.shape[0], CHUNK):
            rows = slice(r, r + CHUNK)
            value = mixed_v[rows, :] + total[rows, :] + offsets[3:4, :]
            block_out[rows, :] = value
            features[rows, :] = value.astype(BF16)
            nhat, _ = norm_parts(value)
            head = nhat * gains[2:3, :] + offsets[4:5, :]
            for c in range(crops):
                sums[c] = sums[c] + jnp.sum(jnp.where(crop[rows, :] == c, head, 0.0), axis=0, keepdims=True)
        for c in range(crops):
            pool[c : c + 1, :] = sums[c]
    else:
        outs[-1].start()
    for c in outs:
        c.wait()


def head_back_body(block_out, cotangent, crop, pooled_grad, gains, grad_out, low_out, sums_out):
    crops = pooled_grad.shape[0]

    @pl.when(pl.program_id(0) == 0)
    def _():
        sums_out[...] = jnp.zeros_like(sums_out)

    nhat, inv = norm_parts(block_out[...])
    grad = jnp.zeros(nhat.shape, F32)
    for c in range(crops):
        grad = jnp.where(crop[...] == c, pooled_grad[c : c + 1, :], grad)
    out = cotangent[...].astype(F32) + norm_back(nhat, inv, gains[2:3, :], grad)
    grad_out[...] = out
    low_out[...] = out.astype(BF16)
    sums_out[0:1, :] += jnp.sum(grad * nhat, axis=0, keepdims=True)
    sums_out[1:2, :] += jnp.sum(grad, axis=0, keepdims=True)
    sums_out[2:3, :] += jnp.sum(out, axis=0, keepdims=True)


def head_body(
    pooled, unit_grad, first_hbm, second_hbm, third_hbm, first_bias, second_bias, third_bias,
    first_act, second_act, units, embed_grad, second_low, first_low, pooled_grad,
    first, second, third, sems,
):
    chunk = 512
    parts = second.shape[0] // chunk
    rows_of = lambda i: pl.ds(i * chunk, chunk)
    pairs = [(first_hbm, first)]
    pairs += [(second_hbm.at[rows_of(i), :], second.at[rows_of(i), :]) for i in range(parts)]
    pairs += [(third_hbm, third)]
    copies = copies_of(pairs, sems)
    for c in copies:
        c.start()
    copies[0].wait()
    act, first_slope = gelu_pair(dot(pooled[...], first[...]) + first_bias[...])
    act = act.astype(BF16)
    first_act[...] = act
    total = second_bias[...]
    for i in range(parts):
        copies[1 + i].wait()
        total = total + dot(act[:, i * chunk : (i + 1) * chunk], second[i * chunk : (i + 1) * chunk, :])
    act, second_slope = gelu_pair(total)
    act = act.astype(BF16)
    second_act[...] = act
    copies[-1].wait()
    embedded = dot(act, third[...]) + third_bias[...]
    inv = lax.rsqrt(jnp.sum(embedded * embedded, axis=-1, keepdims=True) + 1e-06)
    units[...] = (embedded * inv).astype(BF16)
    given = unit_grad[...]
    along = jnp.sum(embedded * given, axis=-1, keepdims=True)
    grad = inv * given - (inv * inv * inv) * embedded * along
    embed_grad[...] = grad
    low = (dot_right(grad.astype(BF16), third[...]) * second_slope).astype(BF16)
    second_low[...] = low
    low = (dot_right(low, second[...]) * first_slope).astype(BF16)
    first_low[...] = low
    pooled_grad[...] = dot_right(low, first[...])


def inner_back_body(windows, pieces, started, last, *refs):
    refs = list(refs)
    take = lambda n: [refs.pop(0) for _ in range(n)]
    count = len(pieces)
    low_in, normed = take(2)
    act_in, slope_in, wi_in = take(count), take(count), take(count)
    wo_in = [take(n) for n in pieces]
    before = take(1)[0] if started else None
    if last:
        mixed, out_grad, gains = take(3)
    outer_out, inner_out = take(count), take(count)
    sums_out = take(1)[0]
    if last:
        grad_out, low_out, norm_sums = take(3)
    else:
        total_out = take(1)[0]
    low, x, act, slope, wi, wo, outer, inner, pre, total, sems, out_sems = take(12)
    first_of = []
    pairs = [(low_in, low)]
    for k in range(count):
        first_of.append(len(pairs))
        pairs += pieces_of(wo_in[k], wo.at[k]) + [(slope_in[k], slope.at[k]), (act_in[k], act.at[k])]
        pairs += [(normed, x)] * (k == 0) + [(wi_in[k], wi.at[k])]
    if started:
        pairs.append((before, total))
    rows_all = total.shape[0]
    if last:
        mixed_v, flat = take(2)
        pairs += [(mixed, mixed_v), (out_grad, flat.at[pl.ds(0, rows_all), :])]
    copies = copies_of(pairs, sems)
    for c in copies:
        c.start()
    wait = lambda n: [copies.pop(0).wait() for _ in range(n)]
    out_pairs = [p for k in range(count) for p in ((outer.at[k], outer_out[k]), (inner.at[k], inner_out[k]))]
    outs = copies_of(out_pairs + ([] if last else [(total, total_out)]), out_sems)
    wait(1)
    for k in range(count):
        wait(pieces[k])
        raw = dot_right(low[...], wo[k])
        wait(2)
        outer_value = dot_left(low[...], act[k])
        value = (raw * slope[k].astype(F32)).astype(BF16)
        pre[k] = value
        sums_out[k : k + 1, :] = jnp.sum(value.astype(F32), axis=0, keepdims=True)
        outer[k] = outer_value.astype(BF16)
        outs[2 * k].start()
        wait(2 if k == 0 else 1)
        inner[k] = dot_left(x[...], pre[k]).astype(BF16)
        outs[2 * k + 1].start()
        share = dot_right(pre[k], wi[k])
        if k == 0 and not started:
            total[...] = share
        else:
            if k == 0:
                copies.pop(sum(pieces[1:]) + 3 * (count - 1)).wait()
            total[...] += share
    if not last:
        outs[-1].start()
    if last:
        wait(2)
        gain_sum = jnp.zeros((1, total.shape[1]), F32)
        shift_sum = gain_sum
        bias_sum = gain_sum
        for r in range(0, rows_all, CHUNK):
            rows = slice(r, r + CHUNK)
            nhat, inv = norm_parts(mixed_v[rows, :])
            grad = total[rows, :]
            gain_sum = gain_sum + jnp.sum(grad * nhat, axis=0, keepdims=True)
            shift_sum = shift_sum + jnp.sum(grad, axis=0, keepdims=True)
            out = flat[rows, :] + norm_back(nhat, inv, gains[1:2, :], grad)
            bias_sum = bias_sum + jnp.sum(out, axis=0, keepdims=True)
            grad_out[rows, :] = out
            flat[rows, :] = out
        norm_sums[0:1, :] = gain_sum
        norm_sums[1:2, :] = shift_sum
        norm_sums[2:3, :] = bias_sum
        widen(windows, flat, low_out)
    for c in outs:
        c.wait()


def weight_grad_body(x, low, d, att0, att1, even_a, odd_a, even_b, odd_b):
    width = att0.shape[1]
    quarter = width // 2
    big = dot_left(x[...], d[...])
    for t, (even, odd, at) in enumerate(((even_a, odd_a, 0), (even_a, odd_a, 1), (even_b, odd_b, 0))):
        lanes = slice(at * quarter, (at + 1) * quarter)
        even[0, :, lanes] = big[:, t * width : t * width + quarter].astype(BF16)
        odd[0, :, lanes] = big[:, t * width + quarter : (t + 1) * width].astype(BF16)
    for pair, att in enumerate((att0, att1)):

        @pl.when(pl.program_id(0) == 1 - pair)
        def _(att=att):
            side = dot_left(low[...], att[...])
            even_b[0, :, quarter:width] = side[:, 0:quarter].astype(BF16)
            odd_b[0, :, quarter:width] = side[:, quarter:width].astype(BF16)


def tokens_back_body(windows, grads, stacked0, stacked1, tokens, mixed_grad, gains, head, mid, ends, grad_out, packed, flat):
    half = stacked0.shape[0]
    group = 4
    for first in range(0, windows, group):
        here = slice(first * PAD, (first + group) * PAD)
        total = dot(grads[here, 0:half], stacked0[...]) + dot(grads[here, half : 2 * half], stacked1[...])
        for w in range(group):
            at = (first + w) * SPOTS
            flat[at : at + SPOTS, :] = total[w * PAD : w * PAD + SPOTS, :]
    gain_sum = jnp.zeros((1, tokens.shape[1]), F32)
    shift_sum = gain_sum
    for r in range(0, tokens.shape[0], CHUNK):
        rows = slice(r, r + CHUNK)
        nhat, inv = norm_parts(tokens[rows, :].astype(F32))
        grad = flat[rows, :]
        gain_sum = gain_sum + jnp.sum(grad * nhat, axis=0, keepdims=True)
        shift_sum = shift_sum + jnp.sum(grad, axis=0, keepdims=True)
        grad_out[rows, :] = mixed_grad[rows, :] + norm_back(nhat, inv, gains[0:1, :], grad)
    packed[0:1, :] = gain_sum
    packed[1:2, :] = mid[0:1, :]
    packed[2:3, :] = head[0:1, :]
    packed[3:4, :] = shift_sum
    packed[4:5, :] = mid[2:3, :]
    packed[5:6, :] = mid[1:2, :]
    packed[6:7, :] = head[2:3, :]
    packed[7:8, :] = head[1:2, :]
    packed[8 : 8 + ends.shape[0], :] = ends[...]


def prototype_body(units, columns, cotangent, direction, inv, gain, flags, logits, direction_grad, gain_grad):
    logits[...] = dot(units[...], columns[...])
    grad = dot_left(units[...], cotangent[...])
    keep = (1 - flags[...]).astype(F32)
    value = direction[...].astype(F32)
    along = jnp.sum(grad * value, axis=0, keepdims=True)
    scale = inv[...]
    gain_grad[...] = keep * scale * along
    direction_grad[...] = (keep * gain[...]) * (scale * grad - (scale * scale * scale * along) * value)


def head_grads_body(
    pooled, first_act, second_act, first_low, second_low, embed_low, embed_grad,
    first_grad, second_grad, third_grad, first_bias, second_bias, third_bias,
):
    first_grad[...] = dot_left(pooled[...], first_low[...])
    second_grad[...] = dot_left(first_act[...], second_low[...])
    third_grad[...] = dot_left(second_act[...], embed_low[...])
    first_bias[...] = jnp.sum(first_low[...].astype(F32), axis=0, keepdims=True)
    second_bias[...] = jnp.sum(second_low[...].astype(F32), axis=0, keepdims=True)
    third_bias[...] = jnp.sum(embed_grad[...], axis=0, keepdims=True)


def swap(values, axis, bit):
    return lax.ppermute(values, axis, [(i, i ^ bit) for i in range(lax.axis_size(axis))])


def bits_of(axis):
    size = lax.axis_size(axis)
    bit, found = 1, []
    while bit < size:
        found.append(bit)
        bit *= 2
    return found


def has_bit(axis, bit):
    return (lax.axis_index(axis) // bit) % 2 == 1


def after(values, *others):
    return lax.optimization_barrier((values, *others))[0]


def sum_over(values, axes):
    for axis in axes:
        for bit in bits_of(axis):
            values = values + swap(values, axis, bit)
    return values


def ordered(mine, other, upper):
    return jnp.concatenate([jnp.where(upper, other, mine), jnp.where(upper, mine, other)], axis=0)


def gather_over(values, axis):
    for bit in bits_of(axis):
        values = ordered(values, swap(values, axis, bit), has_bit(axis, bit))
    return values


def by_distance(values, axis):
    for bit in bits_of(axis):
        size = values.shape[0]
        folded = values.reshape(size // (2 * bit), 2, bit, *values.shape[1:])
        folded = jnp.where(has_bit(axis, bit), folded[:, ::-1], folded)
        values = folded.reshape(values.shape)
    return values


def own_half(values, share, piece=0, pieces=1):
    parts = values.reshape(2 * pieces, values.shape[0] // (2 * pieces), *values.shape[1:])
    return lax.dynamic_index_in_dim(parts, 2 * piece + lax.axis_index("dp") // share % 2, 0, keepdims=False)


def rows_by_bit(values, bit, own):
    groups, rows, columns = values.shape
    folded = values.reshape(groups // 2, 2, rows, columns)
    mine = lax.axis_index("dp") // bit % 2
    return lax.dynamic_index_in_dim(folded, mine if own else 1 - mine, 1, keepdims=False)


def halve_rows(values, bit):
    groups, rows, columns = values.shape
    folded = values.reshape(groups // 2, 2, rows, columns)
    mine = lax.axis_index("dp") // bit % 2
    keep = lax.dynamic_index_in_dim(folded, mine, 1, keepdims=False)
    send = lax.dynamic_index_in_dim(folded, 1 - mine, 1, keepdims=False)
    return keep, send


def add(kept, got):
    return kept.astype(F32) + got.astype(F32)


def offset_table(columns):
    places = jnp.arange(PAD, dtype=jnp.int32)
    row_of = places // SIDE
    col_of = places % SIDE
    offset = (row_of[None, :] - row_of[:, None] + SIDE - 1) * (2 * SIDE - 1) + (
        col_of[None, :] - col_of[:, None] + SIDE - 1
    )
    inside = (places[:, None] < SPOTS) & (places[None, :] < SPOTS)
    offset = jnp.where(inside, offset, -1)
    entries = jnp.arange(columns, dtype=jnp.int32)
    return (offset.reshape(-1)[:, None] == entries[None, :]).astype(F32)


def shards(
    tokens,
    input_projection,
    input_bias,
    position_bias,
    output_projection,
    inner_weight,
    inner_bias,
    outer_weight,
    norm_gains,
    offsets,
    head_first,
    head_first_bias,
    head_second,
    head_second_bias,
    head_third,
    head_third_bias,
    prototype_direction,
    prototype_gain,
    crop_windows,
    first_epoch,
    feature_cotangent,
    logit_cotangent,
):
    rows, width = tokens.shape
    windows = rows // SPOTS
    narrow_index = lax.axis_index("narrow")
    dp_index = lax.axis_index("dp")
    count = lax.axis_size("narrow")
    groups = lax.axis_size("dp")
    quarter = input_projection.shape[2]
    hidden = inner_weight.shape[1]
    heads = position_bias.shape[1] // count
    size = quarter // heads
    scale = size ** (-0.5)
    crops = crop_windows.shape[1]
    padded_rows = windows * PAD

    near, far = bits_of("narrow")
    data_bits = bits_of("dp")
    share, share_too = data_bits[0], data_bits[1]

    w_in0 = input_projection.swapaxes(1, 2)
    w_in1 = swap(w_in0, "narrow", near)
    in_half = swap(own_half(w_in0.reshape(3 * quarter, width), share), "narrow", far)
    w_att1 = swap(output_projection, "narrow", near)
    w_inner1 = swap(inner_weight, "narrow", near)
    w_outer1 = swap(outer_weight, "narrow", near)

    bias_in = by_distance(input_bias.reshape(2, count, quarter).swapaxes(0, 1), "narrow")
    bias_in = bias_in.swapaxes(0, 1).reshape(2, count * quarter)
    bias_inner = by_distance(inner_bias.reshape(count, 1, hidden), "narrow")
    offsets_count = position_bias.shape[0]
    table = offset_table(offsets_count)
    turned = by_distance(position_bias.T.reshape(count, heads, -1), "narrow").reshape(count * heads, -1)
    spread = jnp.dot(table, turned.T, precision=HIGH, preferred_element_type=F32)
    spread = spread.reshape(PAD, PAD, count * heads).transpose(0, 2, 1)
    inside = (jnp.arange(PAD) < SPOTS)[:, None, None]
    spread = jnp.where(inside, spread, NEG).reshape(PAD, count * heads * PAD)

    ends = jnp.cumsum(crop_windows[0])
    row_window = narrow_index * windows + jnp.arange(rows, dtype=jnp.int32) // SPOTS
    crop_of_row = jnp.sum((row_window[:, None] >= ends[None, :]).astype(jnp.int32), axis=1, keepdims=True)
    crop_tokens = (crop_windows[0] * SPOTS).astype(F32)

    padded = call(
        functools.partial(norm_one_body, windows),
        shape((padded_rows, width), BF16),
        (tokens, norm_gains, offsets),
        scratch=[pltpu.VMEM((rows + 16, width), F32)],
        us=3.5,
    )
    half = 2 * quarter
    pair_lanes = 2 * heads * PAD
    batch = 4 * PAD
    by_row = lambda n: pl.BlockSpec((batch, n), lambda i: (i, 0))
    fixed = lambda *dims: pl.BlockSpec(dims, lambda i: (0,) * len(dims))
    qkv, probs, attended, stacked_in = [], [], [], []

    def attend(pair, x, first, second):
        got = pl.pallas_call(
            functools.partial(attend_body, size, scale),
            grid=(padded_rows // batch,),
            out_shape=(
                shape((padded_rows, 3 * half), BF16),
                shape((padded_rows, pair_lanes), BF16),
                shape((padded_rows, half), BF16),
                shape((3, half, width), BF16),
            ),
            in_specs=[
                by_row(width),
                fixed(3, quarter, width),
                fixed(3, quarter, width),
                fixed(2, half),
                pl.BlockSpec((PAD, pair_lanes), lambda i, pair=pair: (0, pair)),
            ],
            out_specs=(by_row(3 * half), by_row(pair_lanes), by_row(half), fixed(3, half, width)),
            compiler_params=pltpu.CompilerParams(vmem_limit_bytes=VMEM_LIMIT),
            cost_estimate=cost(9.0),
        )(x, first, second, bias_in[:, pair * half : (pair + 1) * half], spread)
        for keep, value in zip((qkv, probs, attended, stacked_in), got):
            keep.append(value)
        return got

    def whole_of(mine, other, bit):
        return ordered(mine, other, has_bit("dp", bit))

    def bring(weight, bit, *others, piece=0, pieces=1):
        return swap(own_half(after(weight, *others), bit, piece, pieces), "narrow", far)

    in_half, w_in1 = after((in_half, w_in1), padded, spread)
    in_rest = swap(in_half, "dp", share)
    w_att2 = swap(after(output_projection, in_half), "narrow", far)
    got = attend(0, after(padded, in_half), w_in0, w_in1)
    in_rest, w_att2 = after((in_rest, w_att2), got)
    inner_half = bring(inner_weight, share, w_att2)
    w_in2 = whole_of(in_half, in_rest, share).reshape(w_in0.shape)
    w_in3 = swap(w_in2, "narrow", near)
    w_att3 = swap(w_att2, "narrow", near)
    got = attend(1, after(padded, got), w_in2, w_in3)
    w_att3, inner_half = after((w_att3, inner_half), got)
    outer_half = bring(outer_weight, share_too, inner_half)
    inner_rest = swap(inner_half, "dp", share)
    mixed, normed_two, stacked_att = call(
        functools.partial(mixed_body, windows, count),
        (shape((rows, width), F32), shape((rows, width), BF16), shape((count * quarter, width), BF16)),
        (
            *attended,
            output_projection, w_att1, w_att2, w_att3,
            after(tokens, inner_half),
            norm_gains,
            offsets,
        ),
        us=6.0,
    )
    anywhere = pl.BlockSpec(memory_space=pl.ANY)
    held = pl.BlockSpec(memory_space=pltpu.VMEM)
    row_held = pltpu.VMEM((rows, width), F32)
    low_held = pltpu.VMEM((rows, width), BF16)
    act_shape = shape((rows, hidden), BF16)

    def inner_call(x, bias, wi, wo, before=(), ending=()):
        n, pieces = len(wi), len(wo[0])
        wo = [p for w in wo for p in w]
        last = bool(ending)
        tail_shape = (shape((rows, width), F32),)
        tail_spec = (anywhere,)
        if last:
            tail_shape += (shape((rows, width), BF16), shape((crops, width), F32))
            tail_spec = (held,) * 3
        return pl.pallas_call(
            functools.partial(inner_body, n, pieces, bool(before), last),
            out_shape=(act_shape,) * (2 * n) + tail_shape,
            in_specs=[anywhere, held] + [anywhere] * (len(wi) + len(wo) + len(before)) + ([anywhere] + [held] * 3 if last else []),
            out_specs=(anywhere,) * (2 * n) + tail_spec,
            scratch_shapes=[
                low_held,
                pltpu.VMEM((n, width, hidden), BF16),
                pltpu.VMEM((n, hidden, width), BF16),
                pltpu.VMEM((n, rows, hidden), BF16),
                pltpu.VMEM((n, rows, hidden), BF16),
                row_held,
                pltpu.SemaphoreType.DMA((1 + n * (1 + pieces) + len(before) + last,)),
                pltpu.SemaphoreType.DMA((2 * n + 1,)),
            ] + ([row_held] if last else []),
            compiler_params=pltpu.CompilerParams(vmem_limit_bytes=VMEM_LIMIT),
            cost_estimate=cost(16.0 if last else 7.0),
        )(x, bias, *wi, *wo, *before, *ending)

    act0, slope0, inner_total = inner_call(normed_two, bias_inner[0:1], [inner_weight], [[outer_weight]])
    outer_half, inner_rest = after((outer_half, inner_rest), inner_total)
    outer_rest = swap(outer_half, "dp", share_too)
    w_inner2 = whole_of(inner_half, inner_rest, share)
    w_inner3 = swap(w_inner2, "narrow", near)
    act1, slope1, inner_total = inner_call(
        after(normed_two, outer_half, w_inner2), bias_inner[1:2], [w_inner1], [[w_outer1]], (inner_total,)
    )
    direction = after(prototype_direction, inner_total).astype(F32)
    column_inv = lax.rsqrt(jnp.sum(direction * direction, axis=0, keepdims=True) + 1e-06)
    columns_low = (prototype_gain * direction * column_inv).astype(BF16)
    unit_share = dot_right(logit_cotangent, columns_low)
    w_inner3, outer_rest = after((w_inner3, outer_rest), unit_share)
    w_outer2 = whole_of(outer_half, outer_rest, share_too)
    w_outer3 = swap(w_outer2, "narrow", near)
    outer2, outer3 = [w_outer2], [w_outer3]
    act2, act3, slope2, slope3, block_out, features, pool = inner_call(
        normed_two, bias_inner[2:4], [w_inner2, w_inner3], [outer2, outer3], (inner_total,),
        (mixed, norm_gains, offsets, crop_of_row),
    )

    flat_pool = pool.reshape(-1, LANES)
    pool_rows = flat_pool.shape[0]
    unit_rows = unit_share.reshape(-1, LANES)
    both = sum_over(jnp.concatenate([flat_pool, unit_rows]), ("narrow",))
    gathered, unit_rows = both[:pool_rows], both[pool_rows:]
    per_crop = jnp.repeat(crop_tokens, width // LANES)[:, None]
    gathered = gathered / per_crop
    for bit in data_bits:
        other = swap(jnp.concatenate([gathered, unit_rows]), "dp", bit)
        unit_rows = unit_rows + other[gathered.shape[0] :]
        gathered = ordered(gathered, other[: gathered.shape[0]], has_bit("dp", bit))
    unit_grad = unit_rows.reshape(unit_share.shape)
    pooled = gathered.reshape(-1, width).astype(BF16)
    all_crops, units_width = unit_grad.shape
    head_width = head_first.shape[1]
    first_act, second_act, units, embed_grad, second_low, first_low, pooled_grad = pl.pallas_call(
        head_body,
        out_shape=(
            shape((all_crops, head_width), BF16),
            shape((all_crops, head_width), BF16),
            shape((all_crops, units_width), BF16),
            shape((all_crops, units_width), F32),
            shape((all_crops, head_width), BF16),
            shape((all_crops, head_width), BF16),
            shape((all_crops, width), F32),
        ),
        in_specs=[held, held, anywhere, anywhere, anywhere, held, held, held],
        out_specs=(held,) * 7,
        scratch_shapes=[
            pltpu.VMEM(head_first.shape, BF16),
            pltpu.VMEM(head_second.shape, BF16),
            pltpu.VMEM(head_third.shape, BF16),
            pltpu.SemaphoreType.DMA((2 + head_second.shape[0] // 512,)),
        ],
        compiler_params=pltpu.CompilerParams(vmem_limit_bytes=VMEM_LIMIT),
        cost_estimate=cost(9.0),
    )(
        pooled, unit_grad, head_first, head_second, head_third,
        head_first_bias[None], head_second_bias[None], head_third_bias[None],
    )
    def own(values):
        part = values.shape[1] // groups
        return lax.dynamic_slice_in_dim(values, dp_index * part, part, 1)

    pooled_grad = lax.dynamic_slice_in_dim(pooled_grad, dp_index * crops, crops, 0) / crop_tokens[:, None]

    split = rows // 2
    by_chunk = lambda n: pl.BlockSpec((split, n), lambda i: (i, 0))
    out_grad, out_low, head_sums = pl.pallas_call(
        head_back_body,
        grid=(2,),
        out_shape=(shape((rows, width), F32), shape((rows, width), BF16), shape((3, width), F32)),
        in_specs=[by_chunk(width), by_chunk(width), by_chunk(1), fixed(crops, width), fixed(*norm_gains.shape)],
        out_specs=(by_chunk(width), by_chunk(width), fixed(3, width)),
        compiler_params=pltpu.CompilerParams(vmem_limit_bytes=VMEM_LIMIT),
        cost_estimate=cost(4.0),
    )(block_out, feature_cotangent, crop_of_row, pooled_grad, norm_gains)

    def by_group(part):
        return part.reshape(groups, part.shape[0] // groups, part.shape[1])

    def inner_back(act, slope, wi, wo, before=(), ending=()):
        last = bool(ending)
        n = len(wi)
        pieces = tuple(len(w) for w in wo)
        wo = [p for w in wo for p in w]
        outs = [shape((width, hidden), BF16)] * (2 * n) + [shape((n, hidden), F32), shape((rows, width), F32)]
        specs = [anywhere] * (2 * n) + [held, held if last else anywhere]
        if last:
            outs += [shape((padded_rows, width), BF16), shape((3, width), F32)]
            specs += [held, held]
        return pl.pallas_call(
            functools.partial(inner_back_body, windows, pieces, bool(before), last),
            out_shape=tuple(outs),
            in_specs=[anywhere] * (2 + 3 * n + len(wo) + len(before)) + ([anywhere, anywhere, held] if last else []),
            out_specs=tuple(specs),
            scratch_shapes=[
                low_held,
                low_held,
                pltpu.VMEM((n, rows, hidden), BF16),
                pltpu.VMEM((n, rows, hidden), BF16),
                pltpu.VMEM((n, width, hidden), BF16),
                pltpu.VMEM((n, hidden, width), BF16),
                pltpu.VMEM((n, width, hidden), BF16),
                pltpu.VMEM((n, width, hidden), BF16),
                pltpu.VMEM((n, rows, hidden), BF16),
                row_held,
                pltpu.SemaphoreType.DMA((2 + 3 * n + len(wo) + len(before) + 2 * last,)),
                pltpu.SemaphoreType.DMA((2 * n + 1,)),
            ] + ([row_held, pltpu.VMEM((rows + 16, width), F32)] if last else []),
            compiler_params=pltpu.CompilerParams(vmem_limit_bytes=VMEM_LIMIT),
            cost_estimate=cost(18.0 if last else 15.0),
        )(out_low, normed_two, *act, *slope, *wi, *wo, *before, *ending)

    o3, o1, i3, i1, sums_odd, total = inner_back([act3, act1], [slope3, slope1], [w_inner3, w_inner1], [outer3, [w_outer1]])
    got_o3, got_i3 = swap(o3, "narrow", near), swap(i3, "narrow", near)
    got_o1, got_i1 = swap(o1, "narrow", near), swap(i1, "narrow", near)
    o2, o0, i2, i0, sums_even, mixed_grad, mixed_low, mixed_sums = inner_back(
        [act2, act0], [slope2, slope0], [w_inner2, inner_weight], [outer2, [outer_weight]],
        (total,), (mixed, out_grad, norm_gains),
    )
    got_o3, got_i3, got_o1, got_i1 = after((got_o3, got_i3, got_o1, got_i1), mixed_low)
    grouped = lambda *parts: [by_group(p) for p in parts]
    o0, o1, o2, o3, i0, i1, i2, i3 = grouped(o0, got_o1, o2, got_o3, i0, got_i1, i2, got_i3)

    def halved(own, first, *more):
        total = rows_by_bit(first, share, own).astype(F32)
        for part in more:
            total = total + rows_by_bit(part, share, own).astype(F32)
        return total

    def rounded(value):
        return value.astype(BF16)

    send_i2 = rounded(halved(False, i2, i3))
    send_o2 = rounded(halved(False, o2, o3))
    got_i2s = swap(send_i2, "narrow", far)
    got_o2 = swap(send_o2, "dp", share)
    mixed_low = after(mixed_low, send_i2, send_o2)

    input_grads, pair_grads, input_sums = pl.pallas_call(
        functools.partial(attend_back_body, size, scale),
        grid=(padded_rows // batch,),
        out_shape=(
            shape((padded_rows, 6 * half), BF16),
            shape((PAD, 2 * pair_lanes), F32),
            shape((1, 6 * half), F32),
        ),
        in_specs=[
            by_row(width),
            fixed(count * quarter, width),
            by_row(3 * half),
            by_row(3 * half),
            by_row(pair_lanes),
            by_row(pair_lanes),
        ],
        out_specs=(by_row(6 * half), fixed(PAD, 2 * pair_lanes), fixed(1, 6 * half)),
        compiler_params=pltpu.CompilerParams(vmem_limit_bytes=VMEM_LIMIT),
        cost_estimate=cost(13.0),
    )(mixed_low, stacked_att, *qkv, *probs)

    pair_grad = pair_grads.reshape(PAD, count * heads, PAD).transpose(1, 0, 2)
    table_grad = lax.dot_general(
        pair_grad.reshape(count * heads, PAD * PAD), offset_table(256), (((1,), (0,)), ((), ())),
        precision=HIGH, preferred_element_type=F32,
    )
    got_i2s, got_o2, i2, i3, o0, o1 = after((got_i2s, got_o2, i2, i3, o0, o1), table_grad)
    send_i2 = rounded(halved(True, i2, i3))
    send_o0 = rounded(halved(False, o0, o1))
    got_i2k = swap(send_i2, "narrow", far)
    got_o0 = swap(send_o0, "dp", share)
    weight_rows = after(input_grads, send_i2, send_o0, got_i2s, got_o2)

    pair_shape = shape((2, width, half), BF16)
    pair_spec = pl.BlockSpec((1, width, half), lambda i: (1 - i, 0, 0))
    even_a, odd_a, even_b, odd_b = pl.pallas_call(
        weight_grad_body,
        grid=(2,),
        out_shape=(pair_shape,) * 4,
        in_specs=[
            fixed(padded_rows, width),
            fixed(padded_rows, width),
            pl.BlockSpec((padded_rows, 3 * half), lambda i: (0, 1 - i)),
            fixed(padded_rows, half),
            fixed(padded_rows, half),
        ],
        out_specs=(pair_spec,) * 4,
        compiler_params=pltpu.CompilerParams(vmem_limit_bytes=VMEM_LIMIT),
        cost_estimate=cost(12.0),
    )(padded, mixed_low, weight_rows, *attended)

    got_i2k, got_o0, got_i2s, got_o2 = after((got_i2k, got_o0, got_i2s, got_o2), even_a)
    far_o = rounded(halved(True, o2, o3) + got_o2.astype(F32))
    send_i = rounded(halved(False, i0, i1) + got_i2s.astype(F32))
    got_o = swap(far_o, "narrow", far)
    got_i = swap(send_i, "dp", share)
    odd_a, odd_b = after((odd_a, odd_b), far_o, send_i)
    got_a, got_b = swap(odd_a, "narrow", near), swap(odd_b, "narrow", near)
    sum_a = rounded(add(even_a[1], got_a[1]))
    keep_b, send_b = halve_rows(rounded(add(even_b, got_b)).reshape(2 * groups, width // groups, half), share)
    got_a2 = swap(sum_a, "narrow", far)
    got_b2 = swap(send_b, "dp", share)

    sums_even, sums_odd, input_sums = after((sums_even, sums_odd, input_sums), sum_a, send_b)
    sums0, sums1, sums2, sums3 = sums_even[1:2], sums_odd[1:2], sums_even[0:1], sums_odd[0:1]
    input_sum = input_sums.reshape(2, 3, 2, quarter).transpose(0, 2, 1, 3).reshape(count, 3, quarter)
    input_sum = by_distance(input_sum, "narrow").swapaxes(0, 1).reshape(3, count * quarter)
    inner_sum = by_distance(jnp.concatenate([sums0, sums1, sums2, sums3]), "narrow").reshape(-1, width)
    ends_in = jnp.concatenate([input_sum[0:1], input_sum[2:3], inner_sum])
    packed_rows = 8 + ends_in.shape[0]
    tokens_grad, packed = call(
        functools.partial(tokens_back_body, windows),
        (shape((rows, width), F32), shape((packed_rows, width), F32)),
        (
            after(input_grads, sum_a, send_b),
            *[v.reshape(3 * half, width) for v in stacked_in],
            tokens,
            mixed_grad,
            norm_gains,
            head_sums,
            mixed_sums,
            ends_in,
        ),
        scratch=[pltpu.VMEM((rows, width), F32)],
        us=10.0,
    )

    table_rows = by_distance(after(table_grad, tokens_grad).reshape(count, -1, width), "narrow").reshape(-1, width)
    small = jnp.concatenate([packed, table_rows])
    small_bits = [("narrow", near), ("narrow", far)] + [("dp", b) for b in data_bits]
    small_got = swap(small, *small_bits[0])
    got_i, got_o = after((got_i, got_o), tokens_grad)
    mlp = rounded(jnp.concatenate([
        halved(True, i0, i1) + got_i2k.astype(F32) + got_i.astype(F32),
        halved(True, o0, o1) + got_o0.astype(F32) + got_o.astype(F32),
    ], axis=2))
    keep_m, send_m = halve_rows(mlp, data_bits[1])
    got_m = swap(send_m, "dp", data_bits[1])
    owned = [own(v) for v in after((first_low, second_low, second_act, embed_grad), send_m)]
    embed_low = after(embed_grad, send_m).astype(BF16)
    got_a2, got_b2, small_got = after((got_a2, got_b2, small_got), embed_low, *owned)
    keep_a, send_a = halve_rows(by_group(rounded(add(even_a[0], got_a[0]) + got_a2.astype(F32))), share)
    got_a = swap(send_a, "dp", share)
    sum_b = rounded(add(keep_b, got_b2)).reshape(2, groups // 2, width // groups, half)
    got_b = swap(sum_b[1], "narrow", far)
    small = small + small_got
    small_got = swap(small, *small_bits[1])

    own_protos = prototype_gain.shape[0]
    logits, direction_grad, gain_grad = call(
        prototype_body,
        (
            shape((all_crops, own_protos), F32),
            shape(prototype_direction.shape, F32),
            shape((1, own_protos), F32),
        ),
        (
            after(units, send_a, sum_b, small), columns_low, logit_cotangent, prototype_direction,
            column_inv, prototype_gain[None], first_epoch[None],
        ),
        us=4.0,
    )

    got_a, got_b, got_m, small_got = after((got_a, got_b, got_m, small_got), logits)
    mlp = add(keep_m, got_m)
    for bit in data_bits[2:-1]:
        keep_m, send_m = halve_rows(mlp.astype(BF16), bit)
        mlp = add(keep_m, swap(send_m, "dp", bit))
    keep_m, send_m = halve_rows(mlp.astype(BF16), data_bits[-1])
    got_m = swap(send_m, "dp", data_bits[-1])
    att_sum = rounded(jnp.concatenate([add(keep_a, got_a), add(sum_b[0], got_b)], axis=2))
    keep_j, send_j = halve_rows(att_sum, data_bits[1])
    got_j = swap(send_j, "dp", data_bits[1])
    small = small + small_got
    small_got = swap(small, *small_bits[2])

    own_first, own_second, own_act, own_embed = owned
    first_grad, second_grad, third_grad, first_bias_grad, second_bias_grad, third_bias_grad = call(
        head_grads_body,
        (
            shape((pooled.shape[1], own_first.shape[1]), F32),
            shape((first_act.shape[1], own_second.shape[1]), F32),
            shape((own_act.shape[1], embed_low.shape[1]), F32),
            shape((1, own_first.shape[1]), F32),
            shape((1, own_second.shape[1]), F32),
            shape((1, own_embed.shape[1]), F32),
        ),
        (after(pooled, send_m, send_j, small), first_act, own_act, own_first, own_second, embed_low, own_embed),
        us=5.0,
    )

    got_j, got_m, small_got = after((got_j, got_m, small_got), first_grad)
    small = small + small_got
    small_got = swap(small, *small_bits[3])
    joined = add(keep_j, got_j)
    for bit in data_bits[2:-1]:
        keep_j, send_j = halve_rows(joined.astype(BF16), bit)
        joined = add(keep_j, swap(send_j, "dp", bit))
    keep_j, send_j = halve_rows(joined.astype(BF16), data_bits[-1])
    got_j = swap(send_j, "dp", data_bits[-1])
    mlp = add(keep_m, after(got_m, send_j))
    small = small + after(small_got, send_j)
    for place in small_bits[4:]:
        small = small + swap(small, *place)
    joined = add(keep_j, after(got_j, mlp))
    inner_total, outer_total = mlp[0, :, :hidden], mlp[0, :, hidden:]
    joined = joined[0]
    attend_total = joined[:, 3 * quarter :]
    input_total = jnp.stack([joined[:, i * quarter : (i + 1) * quarter] for i in range(3)])

    gain_total, offset_total, bias_total = small[0:3], small[3:8], small[8:10]
    inner_bias_total = small[10 : 10 + inner_sum.shape[0]].reshape(-1)
    table_total = small[10 + inner_sum.shape[0] :].reshape(count * heads, 256)[:, :offsets_count].T
    return (
        features,
        logits,
        tokens_grad,
        input_total,
        bias_total,
        table_total,
        attend_total.T,
        inner_total,
        inner_bias_total,
        outer_total.T,
        gain_total,
        offset_total,
        first_grad,
        first_bias_grad[0],
        second_grad,
        second_bias_grad[0],
        third_grad,
        third_bias_grad[0],
        direction_grad,
        gain_grad[0],
    )


def solution(mesh):
    placed = (
        P(("dp", "narrow"), None),
        P(None, None, "narrow"),
        P(),
        P(),
        P("narrow", None),
        P(None, "narrow"),
        P(),
        P("narrow", None),
        P(),
        P(),
        P(),
        P(),
        P(),
        P(),
        P(),
        P(),
        P(None, ("dp", "narrow")),
        P(("dp", "narrow")),
        P("dp", None),
        P(("dp", "narrow")),
        P(("dp", "narrow"), None),
        P(None, ("dp", "narrow")),
    )
    return jax.shard_map(
        shards,
        mesh=mesh,
        in_specs=placed,
        out_specs=(
            P(("dp", "narrow"), None),
            P(None, ("dp", "narrow")),
            P(("dp", "narrow"), None),
            P(None, "dp", "narrow"),
            P(),
            P(),
            P("narrow", "dp"),
            P("dp", "narrow"),
            P(),
            P("narrow", "dp"),
            P(),
            P(),
            P(None, "dp"),
            P("dp"),
            P(None, "dp"),
            P("dp"),
            P("dp", None),
            P("dp"),
            P(None, ("dp", "narrow")),
            P(("dp", "narrow")),
        ),
        check_vma=False,
    )
```

```python
import functools

import jax
import jax.numpy as jnp
from jax import lax
from jax.experimental import pallas as pl
from jax.experimental.pallas import tpu as pltpu
from jax.sharding import PartitionSpec as P

HIGH = lax.Precision.HIGHEST
F32 = jnp.float32
BF16 = jnp.bfloat16
SIDE = 7
SPOTS = SIDE * SIDE
PAD = 64
LANES = 128
CHUNK = 112
VMEM_LIMIT = 60 * 1024 * 1024
NEG = -1e30


def dot(left, right):
    return jnp.dot(left, right, preferred_element_type=F32)


def dot_left(left, right):
    return lax.dot_general(left, right, (((0,), (0,)), ((), ())), preferred_element_type=F32)


def dot_right(left, right):
    return lax.dot_general(left, right, (((1,), (1,)), ((), ())), preferred_element_type=F32)


def cost(us):
    return pl.CostEstimate(flops=0, bytes_accessed=int(us * 3.3e6), transcendentals=0)


def call(body, outs, ins, **kw):
    scratch = kw.pop("scratch", ())
    return pl.pallas_call(
        body,
        out_shape=outs,
        in_specs=[pl.BlockSpec(memory_space=pltpu.VMEM)] * len(ins),
        out_specs=jax.tree.map(lambda _: pl.BlockSpec(memory_space=pltpu.VMEM), outs),
        scratch_shapes=scratch,
        compiler_params=pltpu.CompilerParams(vmem_limit_bytes=VMEM_LIMIT),
        cost_estimate=cost(kw.pop("us")),
        **kw,
    )(*ins)


def shape(dims, kind):
    return jax.ShapeDtypeStruct(dims, kind)


def norm_parts(values):
    center = values - jnp.mean(values, axis=-1, keepdims=True)
    spread = jnp.mean(center * center, axis=-1, keepdims=True)
    inv = lax.rsqrt(spread + 1e-05)
    return center * inv, inv


def norm_back(nhat, inv, gain, grad):
    scaled = grad * gain
    first = jnp.mean(scaled, axis=-1, keepdims=True)
    second = jnp.mean(scaled * nhat, axis=-1, keepdims=True)
    return (scaled - first - nhat * second) * inv


def gelu_pair(pre):
    bell = jnp.exp(pre * pre * -0.5)
    dist = jnp.abs(pre) * (0.3275911 * 0.70710678118654752) + 1.0
    inv = 1.0 / dist
    poly = 0.5 * 1.061405429
    for coef in (-1.453152027, 1.421413741, -0.284496736, 0.254829592):
        poly = poly * inv + 0.5 * coef
    tail = poly * inv * bell
    cdf = jnp.where(pre < 0.0, tail, 1.0 - tail)
    return pre * cdf, cdf + pre * (bell * 0.3989422804014327)


def widen(windows, flat, padded):
    place = lax.broadcasted_iota(jnp.int32, (PAD, 1), 0)
    for w in range(windows):
        block = flat[w * SPOTS : w * SPOTS + PAD, :]
        padded[w * PAD : (w + 1) * PAD, :] = jnp.where(place < SPOTS, block, 0.0).astype(BF16)


def norm_one_body(windows, tokens, gains, offsets, padded, flat):
    for r in range(0, tokens.shape[0], CHUNK):
        nhat, _ = norm_parts(tokens[r : r + CHUNK, :].astype(F32))
        flat[r : r + CHUNK, :] = nhat * gains[0:1, :] + offsets[0:1, :]
    widen(windows, flat, padded)


def head_masks(size):
    lane = lax.broadcasted_iota(jnp.int32, (PAD, LANES), 1) // size
    return [lane == h for h in range(LANES // size)]


def spread_heads(values, masks):
    zero = jnp.zeros_like(values)
    return jnp.concatenate([jnp.where(m, values, zero) for m in masks], axis=0)


def fold_heads(values, masks):
    total = values[0:PAD, :]
    for h in range(1, len(masks)):
        total = jnp.where(masks[h], values[h * PAD : (h + 1) * PAD, :], total)
    return total


def attend_body(size, scale, padded, near, far, bias, table, qkv_out, p_out, att_out, stacked):
    quarter = near.shape[1]
    width = 2 * quarter
    per = LANES // size * PAD

    @pl.when(pl.program_id(0) == 0)
    def _():
        stacked[:, 0:quarter, :] = near[...]
        stacked[:, quarter:width, :] = far[...]

    x = padded[...]
    q = (dot_right(x, stacked[0]) + bias[0:1, :]).astype(BF16)
    k = dot_right(x, stacked[1]).astype(BF16)
    v = (dot_right(x, stacked[2]) + bias[1:2, :]).astype(BF16)
    qkv_out[:, 0:width] = q
    qkv_out[:, width : 2 * width] = k
    qkv_out[:, 2 * width : 3 * width] = v
    masks = head_masks(size)
    items = [
        (slice(w * PAD, (w + 1) * PAD), g) for w in range(x.shape[0] // PAD) for g in range(width // LANES)
    ]
    lanes = lambda g: slice(g * LANES, (g + 1) * LANES)
    scores = [
        dot_right(k[r, lanes(g)], spread_heads(q[r, lanes(g)], masks)) * scale
        + table[:, g * per : (g + 1) * per]
        for r, g in items
    ]
    e = [jnp.exp(s - jnp.max(s, axis=0, keepdims=True)) for s in scores]
    probs = [(s * (1.0 / jnp.sum(s, axis=0, keepdims=True))).astype(BF16) for s in e]
    folded = [fold_heads(dot_left(p, v[r, lanes(g)]), masks) for p, (r, g) in zip(probs, items)]
    for (r, g), p, o in zip(items, probs, folded):
        p_out[r, g * per : (g + 1) * per] = p
        att_out[r, lanes(g)] = o.astype(BF16)


def attend_back_body(size, scale, low, weight, qkv0, qkv1, p0, p1, d_out, table_out, sums_out):
    width = qkv0.shape[1] // 3
    per = LANES // size * PAD
    pair_groups = width // LANES

    @pl.when(pl.program_id(0) == 0)
    def _():
        table_out[...] = jnp.zeros_like(table_out)
        sums_out[...] = jnp.zeros_like(sums_out)

    given = dot_right(low[...], weight[...]).astype(BF16)
    masks = head_masks(size)
    windows = low.shape[0] // PAD
    both = 2
    for first in range(0, windows, both):
        items = [
            (slice(w * PAD, (w + 1) * PAD), pair, g)
            for w in range(first, first + both)
            for pair in range(2)
            for g in range(pair_groups)
        ]
        qkv = (qkv0, qkv1)
        probs_of = (p0, p1)

        def part(item, t):
            r, pair, g = item
            return qkv[pair][r, t * width + g * LANES : t * width + (g + 1) * LANES]

        gs = [
            spread_heads(given[r, pair * width + g * LANES : pair * width + (g + 1) * LANES], masks)
            for r, pair, g in items
        ]
        prob_grad = [dot_right(part(i, 2), s) for i, s in zip(items, gs)]
        low_probs = [probs_of[pair][r, g * per : (g + 1) * per] for r, pair, g in items]
        probs = [p.astype(F32) for p in low_probs]
        weighed = [p * s for p, s in zip(probs, prob_grad)]
        score_low = [
            (t - p * jnp.sum(t, axis=0, keepdims=True)).astype(BF16) for p, t in zip(probs, weighed)
        ]
        dv = [dot(p, s).astype(BF16) for p, s in zip(low_probs, gs)]
        dk = [
            (dot(s, spread_heads(part(i, 0), masks)) * scale).astype(BF16)
            for i, s in zip(items, score_low)
        ]
        dq = [
            (fold_heads(dot_left(s, part(i, 1)), masks) * scale).astype(BF16)
            for i, s in zip(items, score_low)
        ]
        for (r, pair, g), *parts in zip(items, dq, dk, dv):
            for t, value in enumerate(parts):
                at = (pair * 3 + t) * width + g * LANES
                d_out[r, at : at + LANES] = value
        for pair in range(2):
            for g in range(pair_groups):
                mine = [n for n, (_, p, h) in enumerate(items) if (p, h) == (pair, g)]
                at = (pair * pair_groups + g) * per
                table_out[:, at : at + per] += sum(score_low[n].astype(F32) for n in mine)
                for t, values in enumerate((dq, dk, dv)):
                    at = (pair * 3 + t) * width + g * LANES
                    sums_out[0:1, at : at + LANES] += sum(
                        jnp.sum(values[n].astype(F32), axis=0, keepdims=True) for n in mine
                    )


def mixed_body(windows, count, att0, att1, *refs):
    wo = refs[:count]
    tokens, gains, offsets, mixed, normed, stacked = refs[count:]
    quarter = wo[0].shape[0]
    half = att0.shape[1]
    for k in range(count):
        stacked[k * quarter : (k + 1) * quarter, :] = wo[k][...]
    group = 4
    for first in range(0, windows, group):
        here = slice(first * PAD, (first + group) * PAD)
        total = dot(att0[here, :], stacked[0:half, :]) + dot(att1[here, :], stacked[half : 2 * half, :])
        for w in range(group):
            at = (first + w) * SPOTS
            mixed[at : at + SPOTS, :] = total[w * PAD : w * PAD + SPOTS, :]
    for r in range(0, tokens.shape[0], CHUNK):
        rows = slice(r, r + CHUNK)
        value = tokens[rows, :].astype(F32) + mixed[rows, :] + offsets[1:2, :]
        mixed[rows, :] = value
        nhat, _ = norm_parts(value)
        normed[rows, :] = (nhat * gains[1:2, :] + offsets[2:3, :]).astype(BF16)


def copies_of(pairs, sems, first=0):
    return [pltpu.make_async_copy(a, b, sems.at[first + i]) for i, (a, b) in enumerate(pairs)]


def pieces_of(pieces, target):
    at, pairs = 0, []
    for p in pieces:
        pairs.append((p, target.at[pl.ds(at, p.shape[0]), :]))
        at += p.shape[0]
    return pairs


def inner_body(count, pieces, started, last, *refs):
    refs = list(refs)
    take = lambda n: [refs.pop(0) for _ in range(n)]
    normed, bias = take(2)
    wi = take(count)
    wo = [take(pieces) for _ in range(count)]
    before = take(1)[0] if started else None
    if last:
        mixed, gains, offsets, crop = take(4)
    act_out, slope_out = take(count), take(count)
    if last:
        block_out, features, pool = take(3)
    else:
        total_out = take(1)[0]
    x, wi_v, wo_v, act, slope, total, sems, out_sems = take(8)
    if last:
        mixed_v = take(1)[0]
    pairs = [(normed, x)]
    for k in range(count):
        pairs += [(wi[k], wi_v.at[k])] + pieces_of(wo[k], wo_v.at[k])
    if started:
        pairs.append((before, total))
    if last:
        pairs.append((mixed, mixed_v))
    copies = copies_of(pairs, sems)
    for c in copies:
        c.start()
    copies.pop(0).wait()
    weights = [[copies.pop(0) for _ in range(1 + pieces)] for _ in range(count)]
    half = x.shape[0] // 2
    work = [(k, h) for k in range(count) for h in range(2)]

    def first(k, h):
        if h == 0:
            weights[k][0].wait()
        return dot(x[h * half : (h + 1) * half, :], wi_v[k]) + bias[k]

    out_pairs = [p for k in range(count) for p in ((act.at[k], act_out[k]), (slope.at[k], slope_out[k]))]
    if not last:
        out_pairs.append((total, total_out))
    outs = copies_of(out_pairs, out_sems)
    ahead = first(*work[0])
    for n, (k, h) in enumerate(work):
        pre = ahead
        if n + 1 < len(work):
            ahead = first(*work[n + 1])
        rows = slice(h * half, (h + 1) * half)
        value, grad = gelu_pair(pre)
        value = value.astype(BF16)
        act[k, rows, :] = value
        slope[k, rows, :] = grad.astype(BF16)
        if h == 1:
            outs[2 * k].start()
            outs[2 * k + 1].start()
        else:
            for c in weights[k][1:]:
                c.wait()
            if n == 0 and started:
                copies.pop(0).wait()
        share = dot(value, wo_v[k])
        if k == 0 and not started:
            total[rows, :] = share
        else:
            total[rows, :] += share
    if last:
        copies.pop(0).wait()
        crops = pool.shape[0]
        sums = [jnp.zeros((1, total.shape[1]), F32)] * crops
        for r in range(0, total.shape[0], CHUNK):
            rows = slice(r, r + CHUNK)
            value = mixed_v[rows, :] + total[rows, :] + offsets[3:4, :]
            block_out[rows, :] = value
            features[rows, :] = value.astype(BF16)
            nhat, _ = norm_parts(value)
            head = nhat * gains[2:3, :] + offsets[4:5, :]
            for c in range(crops):
                sums[c] = sums[c] + jnp.sum(jnp.where(crop[rows, :] == c, head, 0.0), axis=0, keepdims=True)
        for c in range(crops):
            pool[c : c + 1, :] = sums[c]
    else:
        outs[-1].start()
    for c in outs:
        c.wait()


def head_back_body(block_out, cotangent, crop, pooled_grad, gains, grad_out, low_out, sums_out):
    crops = pooled_grad.shape[0]

    @pl.when(pl.program_id(0) == 0)
    def _():
        sums_out[...] = jnp.zeros_like(sums_out)

    nhat, inv = norm_parts(block_out[...])
    grad = jnp.zeros(nhat.shape, F32)
    for c in range(crops):
        grad = jnp.where(crop[...] == c, pooled_grad[c : c + 1, :], grad)
    out = cotangent[...].astype(F32) + norm_back(nhat, inv, gains[2:3, :], grad)
    grad_out[...] = out
    low_out[...] = out.astype(BF16)
    sums_out[0:1, :] += jnp.sum(grad * nhat, axis=0, keepdims=True)
    sums_out[1:2, :] += jnp.sum(grad, axis=0, keepdims=True)
    sums_out[2:3, :] += jnp.sum(out, axis=0, keepdims=True)


def head_body(
    pooled, unit_grad, first_hbm, second_hbm, third_hbm, first_bias, second_bias, third_bias,
    first_act, second_act, units, embed_grad, second_low, first_low, pooled_grad,
    first, second, third, sems,
):
    chunk = 512
    parts = second.shape[0] // chunk
    rows_of = lambda i: pl.ds(i * chunk, chunk)
    pairs = [(first_hbm, first)]
    pairs += [(second_hbm.at[rows_of(i), :], second.at[rows_of(i), :]) for i in range(parts)]
    pairs += [(third_hbm, third)]
    copies = copies_of(pairs, sems)
    for c in copies:
        c.start()
    copies[0].wait()
    act, first_slope = gelu_pair(dot(pooled[...], first[...]) + first_bias[...])
    act = act.astype(BF16)
    first_act[...] = act
    total = second_bias[...]
    for i in range(parts):
        copies[1 + i].wait()
        total = total + dot(act[:, i * chunk : (i + 1) * chunk], second[i * chunk : (i + 1) * chunk, :])
    act, second_slope = gelu_pair(total)
    act = act.astype(BF16)
    second_act[...] = act
    copies[-1].wait()
    embedded = dot(act, third[...]) + third_bias[...]
    inv = lax.rsqrt(jnp.sum(embedded * embedded, axis=-1, keepdims=True) + 1e-06)
    units[...] = (embedded * inv).astype(BF16)
    given = unit_grad[...]
    along = jnp.sum(embedded * given, axis=-1, keepdims=True)
    grad = inv * given - (inv * inv * inv) * embedded * along
    embed_grad[...] = grad
    low = (dot_right(grad.astype(BF16), third[...]) * second_slope).astype(BF16)
    second_low[...] = low
    low = (dot_right(low, second[...]) * first_slope).astype(BF16)
    first_low[...] = low
    pooled_grad[...] = dot_right(low, first[...])


def inner_back_body(windows, pieces, started, last, *refs):
    refs = list(refs)
    take = lambda n: [refs.pop(0) for _ in range(n)]
    count = len(pieces)
    low_in, normed = take(2)
    act_in, slope_in, wi_in = take(count), take(count), take(count)
    wo_in = [take(n) for n in pieces]
    before = take(1)[0] if started else None
    if last:
        mixed, out_grad, gains = take(3)
    outer_out, inner_out = take(count), take(count)
    sums_out = take(1)[0]
    if last:
        grad_out, low_out, norm_sums = take(3)
    else:
        total_out = take(1)[0]
    low, x, act, slope, wi, wo, outer, inner, pre, total, sems, out_sems = take(12)
    first_of = []
    pairs = [(low_in, low)]
    for k in range(count):
        first_of.append(len(pairs))
        pairs += pieces_of(wo_in[k], wo.at[k]) + [(slope_in[k], slope.at[k]), (act_in[k], act.at[k])]
        pairs += [(normed, x)] * (k == 0) + [(wi_in[k], wi.at[k])]
    if started:
        pairs.append((before, total))
    rows_all = total.shape[0]
    if last:
        mixed_v, flat = take(2)
        pairs += [(mixed, mixed_v), (out_grad, flat.at[pl.ds(0, rows_all), :])]
    copies = copies_of(pairs, sems)
    for c in copies:
        c.start()
    wait = lambda n: [copies.pop(0).wait() for _ in range(n)]
    out_pairs = [p for k in range(count) for p in ((outer.at[k], outer_out[k]), (inner.at[k], inner_out[k]))]
    outs = copies_of(out_pairs + ([] if last else [(total, total_out)]), out_sems)
    wait(1)
    for k in range(count):
        wait(pieces[k])
        raw = dot_right(low[...], wo[k])
        wait(2)
        outer_value = dot_left(low[...], act[k])
        value = (raw * slope[k].astype(F32)).astype(BF16)
        pre[k] = value
        sums_out[k : k + 1, :] = jnp.sum(value.astype(F32), axis=0, keepdims=True)
        outer[k] = outer_value.astype(BF16)
        outs[2 * k].start()
        wait(2 if k == 0 else 1)
        inner[k] = dot_left(x[...], pre[k]).astype(BF16)
        outs[2 * k + 1].start()
        share = dot_right(pre[k], wi[k])
        if k == 0 and not started:
            total[...] = share
        else:
            if k == 0:
                copies.pop(sum(pieces[1:]) + 3 * (count - 1)).wait()
            total[...] += share
    if not last:
        outs[-1].start()
    if last:
        wait(2)
        gain_sum = jnp.zeros((1, total.shape[1]), F32)
        shift_sum = gain_sum
        bias_sum = gain_sum
        for r in range(0, rows_all, CHUNK):
            rows = slice(r, r + CHUNK)
            nhat, inv = norm_parts(mixed_v[rows, :])
            grad = total[rows, :]
            gain_sum = gain_sum + jnp.sum(grad * nhat, axis=0, keepdims=True)
            shift_sum = shift_sum + jnp.sum(grad, axis=0, keepdims=True)
            out = flat[rows, :] + norm_back(nhat, inv, gains[1:2, :], grad)
            bias_sum = bias_sum + jnp.sum(out, axis=0, keepdims=True)
            grad_out[rows, :] = out
            flat[rows, :] = out
        norm_sums[0:1, :] = gain_sum
        norm_sums[1:2, :] = shift_sum
        norm_sums[2:3, :] = bias_sum
        widen(windows, flat, low_out)
    for c in outs:
        c.wait()


def weight_grad_body(x, low, d, att0, att1, even_a, odd_a, even_b, odd_b):
    width = att0.shape[1]
    quarter = width // 2
    big = dot_left(x[...], d[...])
    for t, (even, odd, at) in enumerate(((even_a, odd_a, 0), (even_a, odd_a, 1), (even_b, odd_b, 0))):
        lanes = slice(at * quarter, (at + 1) * quarter)
        even[0, :, lanes] = big[:, t * width : t * width + quarter].astype(BF16)
        odd[0, :, lanes] = big[:, t * width + quarter : (t + 1) * width].astype(BF16)
    for pair, att in enumerate((att0, att1)):

        @pl.when(pl.program_id(0) == 1 - pair)
        def _(att=att):
            side = dot_left(low[...], att[...])
            even_b[0, :, quarter:width] = side[:, 0:quarter].astype(BF16)
            odd_b[0, :, quarter:width] = side[:, quarter:width].astype(BF16)


def tokens_back_body(windows, grads, stacked0, stacked1, tokens, mixed_grad, gains, head, mid, ends, grad_out, packed, flat):
    half = stacked0.shape[0]
    group = 4
    for first in range(0, windows, group):
        here = slice(first * PAD, (first + group) * PAD)
        total = dot(grads[here, 0:half], stacked0[...]) + dot(grads[here, half : 2 * half], stacked1[...])
        for w in range(group):
            at = (first + w) * SPOTS
            flat[at : at + SPOTS, :] = total[w * PAD : w * PAD + SPOTS, :]
    gain_sum = jnp.zeros((1, tokens.shape[1]), F32)
    shift_sum = gain_sum
    for r in range(0, tokens.shape[0], CHUNK):
        rows = slice(r, r + CHUNK)
        nhat, inv = norm_parts(tokens[rows, :].astype(F32))
        grad = flat[rows, :]
        gain_sum = gain_sum + jnp.sum(grad * nhat, axis=0, keepdims=True)
        shift_sum = shift_sum + jnp.sum(grad, axis=0, keepdims=True)
        grad_out[rows, :] = mixed_grad[rows, :] + norm_back(nhat, inv, gains[0:1, :], grad)
    packed[0:1, :] = gain_sum
    packed[1:2, :] = mid[0:1, :]
    packed[2:3, :] = head[0:1, :]
    packed[3:4, :] = shift_sum
    packed[4:5, :] = mid[2:3, :]
    packed[5:6, :] = mid[1:2, :]
    packed[6:7, :] = head[2:3, :]
    packed[7:8, :] = head[1:2, :]
    packed[8 : 8 + ends.shape[0], :] = ends[...]


def prototype_body(units, columns, cotangent, direction, inv, gain, flags, logits, direction_grad, gain_grad):
    logits[...] = dot(units[...], columns[...])
    grad = dot_left(units[...], cotangent[...])
    keep = (1 - flags[...]).astype(F32)
    value = direction[...].astype(F32)
    along = jnp.sum(grad * value, axis=0, keepdims=True)
    scale = inv[...]
    gain_grad[...] = keep * scale * along
    direction_grad[...] = (keep * gain[...]) * (scale * grad - (scale * scale * scale * along) * value)


def head_grads_body(
    pooled, first_act, second_act, first_low, second_low, embed_low, embed_grad,
    first_grad, second_grad, third_grad, first_bias, second_bias, third_bias,
):
    first_grad[...] = dot_left(pooled[...], first_low[...])
    second_grad[...] = dot_left(first_act[...], second_low[...])
    third_grad[...] = dot_left(second_act[...], embed_low[...])
    first_bias[...] = jnp.sum(first_low[...].astype(F32), axis=0, keepdims=True)
    second_bias[...] = jnp.sum(second_low[...].astype(F32), axis=0, keepdims=True)
    third_bias[...] = jnp.sum(embed_grad[...], axis=0, keepdims=True)


def swap(values, axis, bit):
    return lax.ppermute(values, axis, [(i, i ^ bit) for i in range(lax.axis_size(axis))])


def bits_of(axis):
    size = lax.axis_size(axis)
    bit, found = 1, []
    while bit < size:
        found.append(bit)
        bit *= 2
    return found


def has_bit(axis, bit):
    return (lax.axis_index(axis) // bit) % 2 == 1


def after(values, *others):
    return lax.optimization_barrier((values, *others))[0]


def sum_over(values, axes):
    for axis in axes:
        for bit in bits_of(axis):
            values = values + swap(values, axis, bit)
    return values


def ordered(mine, other, upper):
    return jnp.concatenate([jnp.where(upper, other, mine), jnp.where(upper, mine, other)], axis=0)


def gather_over(values, axis):
    for bit in bits_of(axis):
        values = ordered(values, swap(values, axis, bit), has_bit(axis, bit))
    return values


def by_distance(values, axis):
    for bit in bits_of(axis):
        size = values.shape[0]
        folded = values.reshape(size // (2 * bit), 2, bit, *values.shape[1:])
        folded = jnp.where(has_bit(axis, bit), folded[:, ::-1], folded)
        values = folded.reshape(values.shape)
    return values


def own_half(values, share, piece=0, pieces=1):
    parts = values.reshape(2 * pieces, values.shape[0] // (2 * pieces), *values.shape[1:])
    return lax.dynamic_index_in_dim(parts, 2 * piece + lax.axis_index("dp") // share % 2, 0, keepdims=False)


def rows_by_bit(values, bit, own):
    groups, rows, columns = values.shape
    folded = values.reshape(groups // 2, 2, rows, columns)
    mine = lax.axis_index("dp") // bit % 2
    return lax.dynamic_index_in_dim(folded, mine if own else 1 - mine, 1, keepdims=False)


def halve_rows(values, bit):
    groups, rows, columns = values.shape
    folded = values.reshape(groups // 2, 2, rows, columns)
    mine = lax.axis_index("dp") // bit % 2
    keep = lax.dynamic_index_in_dim(folded, mine, 1, keepdims=False)
    send = lax.dynamic_index_in_dim(folded, 1 - mine, 1, keepdims=False)
    return keep, send


def add(kept, got):
    return kept.astype(F32) + got.astype(F32)


def offset_table(columns):
    places = jnp.arange(PAD, dtype=jnp.int32)
    row_of = places // SIDE
    col_of = places % SIDE
    offset = (row_of[None, :] - row_of[:, None] + SIDE - 1) * (2 * SIDE - 1) + (
        col_of[None, :] - col_of[:, None] + SIDE - 1
    )
    inside = (places[:, None] < SPOTS) & (places[None, :] < SPOTS)
    offset = jnp.where(inside, offset, -1)
    entries = jnp.arange(columns, dtype=jnp.int32)
    return (offset.reshape(-1)[:, None] == entries[None, :]).astype(F32)


def shards(
    tokens,
    input_projection,
    input_bias,
    position_bias,
    output_projection,
    inner_weight,
    inner_bias,
    outer_weight,
    norm_gains,
    offsets,
    head_first,
    head_first_bias,
    head_second,
    head_second_bias,
    head_third,
    head_third_bias,
    prototype_direction,
    prototype_gain,
    crop_windows,
    first_epoch,
    feature_cotangent,
    logit_cotangent,
):
    rows, width = tokens.shape
    windows = rows // SPOTS
    narrow_index = lax.axis_index("narrow")
    dp_index = lax.axis_index("dp")
    count = lax.axis_size("narrow")
    groups = lax.axis_size("dp")
    quarter = input_projection.shape[2]
    hidden = inner_weight.shape[1]
    heads = position_bias.shape[1] // count
    size = quarter // heads
    scale = size ** (-0.5)
    crops = crop_windows.shape[1]
    padded_rows = windows * PAD

    near, far = bits_of("narrow")
    data_bits = bits_of("dp")
    share, share_too = data_bits[0], data_bits[1]

    w_in0 = input_projection.swapaxes(1, 2)
    w_in1 = swap(w_in0, "narrow", near)
    in_half = swap(own_half(w_in0.reshape(3 * quarter, width), share), "narrow", far)
    w_att1 = swap(output_projection, "narrow", near)
    w_inner1 = swap(inner_weight, "narrow", near)
    w_outer1 = swap(outer_weight, "narrow", near)

    bias_in = by_distance(input_bias.reshape(2, count, quarter).swapaxes(0, 1), "narrow")
    bias_in = bias_in.swapaxes(0, 1).reshape(2, count * quarter)
    bias_inner = by_distance(inner_bias.reshape(count, 1, hidden), "narrow")
    offsets_count = position_bias.shape[0]
    table = offset_table(offsets_count)
    turned = by_distance(position_bias.T.reshape(count, heads, -1), "narrow").reshape(count * heads, -1)
    spread = jnp.dot(table, turned.T, precision=HIGH, preferred_element_type=F32)
    spread = spread.reshape(PAD, PAD, count * heads).transpose(0, 2, 1)
    inside = (jnp.arange(PAD) < SPOTS)[:, None, None]
    spread = jnp.where(inside, spread, NEG).reshape(PAD, count * heads * PAD)

    ends = jnp.cumsum(crop_windows[0])
    row_window = narrow_index * windows + jnp.arange(rows, dtype=jnp.int32) // SPOTS
    crop_of_row = jnp.sum((row_window[:, None] >= ends[None, :]).astype(jnp.int32), axis=1, keepdims=True)
    crop_tokens = (crop_windows[0] * SPOTS).astype(F32)

    padded = call(
        functools.partial(norm_one_body, windows),
        shape((padded_rows, width), BF16),
        (tokens, norm_gains, offsets),
        scratch=[pltpu.VMEM((rows + 16, width), F32)],
        us=3.5,
    )
    half = 2 * quarter
    pair_lanes = 2 * heads * PAD
    batch = 4 * PAD
    by_row = lambda n: pl.BlockSpec((batch, n), lambda i: (i, 0))
    fixed = lambda *dims: pl.BlockSpec(dims, lambda i: (0,) * len(dims))
    qkv, probs, attended, stacked_in = [], [], [], []

    def attend(pair, x, first, second):
        got = pl.pallas_call(
            functools.partial(attend_body, size, scale),
            grid=(padded_rows // batch,),
            out_shape=(
                shape((padded_rows, 3 * half), BF16),
                shape((padded_rows, pair_lanes), BF16),
                shape((padded_rows, half), BF16),
                shape((3, half, width), BF16),
            ),
            in_specs=[
                by_row(width),
                fixed(3, quarter, width),
                fixed(3, quarter, width),
                fixed(2, half),
                pl.BlockSpec((PAD, pair_lanes), lambda i, pair=pair: (0, pair)),
            ],
            out_specs=(by_row(3 * half), by_row(pair_lanes), by_row(half), fixed(3, half, width)),
            compiler_params=pltpu.CompilerParams(vmem_limit_bytes=VMEM_LIMIT),
            cost_estimate=cost(9.0),
        )(x, first, second, bias_in[:, pair * half : (pair + 1) * half], spread)
        for keep, value in zip((qkv, probs, attended, stacked_in), got):
            keep.append(value)
        return got

    def whole_of(mine, other, bit):
        return ordered(mine, other, has_bit("dp", bit))

    def bring(weight, bit, *others, piece=0, pieces=1):
        return swap(own_half(after(weight, *others), bit, piece, pieces), "narrow", far)

    in_half, w_in1 = after((in_half, w_in1), padded, spread)
    in_rest = swap(in_half, "dp", share)
    w_att2 = swap(after(output_projection, in_half), "narrow", far)
    got = attend(0, after(padded, in_half), w_in0, w_in1)
    in_rest, w_att2 = after((in_rest, w_att2), got)
    inner_half = bring(inner_weight, share, w_att2)
    w_in2 = whole_of(in_half, in_rest, share).reshape(w_in0.shape)
    w_in3 = swap(w_in2, "narrow", near)
    w_att3 = swap(w_att2, "narrow", near)
    got = attend(1, after(padded, got), w_in2, w_in3)
    w_att3, inner_half = after((w_att3, inner_half), got)
    outer_half = bring(outer_weight, share_too, inner_half)
    inner_rest = swap(inner_half, "dp", share)
    mixed, normed_two, stacked_att = call(
        functools.partial(mixed_body, windows, count),
        (shape((rows, width), F32), shape((rows, width), BF16), shape((count * quarter, width), BF16)),
        (
            *attended,
            output_projection, w_att1, w_att2, w_att3,
            after(tokens, inner_half),
            norm_gains,
            offsets,
        ),
        us=6.0,
    )
    anywhere = pl.BlockSpec(memory_space=pl.ANY)
    held = pl.BlockSpec(memory_space=pltpu.VMEM)
    row_held = pltpu.VMEM((rows, width), F32)
    low_held = pltpu.VMEM((rows, width), BF16)
    act_shape = shape((rows, hidden), BF16)

    def inner_call(x, bias, wi, wo, before=(), ending=()):
        n, pieces = len(wi), len(wo[0])
        wo = [p for w in wo for p in w]
        last = bool(ending)
        tail_shape = (shape((rows, width), F32),)
        tail_spec = (anywhere,)
        if last:
            tail_shape += (shape((rows, width), BF16), shape((crops, width), F32))
            tail_spec = (held,) * 3
        return pl.pallas_call(
            functools.partial(inner_body, n, pieces, bool(before), last),
            out_shape=(act_shape,) * (2 * n) + tail_shape,
            in_specs=[anywhere, held] + [anywhere] * (len(wi) + len(wo) + len(before)) + ([anywhere] + [held] * 3 if last else []),
            out_specs=(anywhere,) * (2 * n) + tail_spec,
            scratch_shapes=[
                low_held,
                pltpu.VMEM((n, width, hidden), BF16),
                pltpu.VMEM((n, hidden, width), BF16),
                pltpu.VMEM((n, rows, hidden), BF16),
                pltpu.VMEM((n, rows, hidden), BF16),
                row_held,
                pltpu.SemaphoreType.DMA((1 + n * (1 + pieces) + len(before) + last,)),
                pltpu.SemaphoreType.DMA((2 * n + 1,)),
            ] + ([row_held] if last else []),
            compiler_params=pltpu.CompilerParams(vmem_limit_bytes=VMEM_LIMIT),
            cost_estimate=cost(16.0 if last else 7.0),
        )(x, bias, *wi, *wo, *before, *ending)

    act0, slope0, inner_total = inner_call(normed_two, bias_inner[0:1], [inner_weight], [[outer_weight]])
    outer_half, inner_rest = after((outer_half, inner_rest), inner_total)
    outer_rest = swap(outer_half, "dp", share_too)
    w_inner2 = whole_of(inner_half, inner_rest, share)
    w_inner3 = swap(w_inner2, "narrow", near)
    act1, slope1, inner_total = inner_call(
        after(normed_two, outer_half, w_inner2), bias_inner[1:2], [w_inner1], [[w_outer1]], (inner_total,)
    )
    direction = after(prototype_direction, inner_total).astype(F32)
    column_inv = lax.rsqrt(jnp.sum(direction * direction, axis=0, keepdims=True) + 1e-06)
    columns_low = (prototype_gain * direction * column_inv).astype(BF16)
    unit_share = dot_right(logit_cotangent, columns_low)
    w_inner3, outer_rest = after((w_inner3, outer_rest), unit_share)
    w_outer2 = whole_of(outer_half, outer_rest, share_too)
    w_outer3 = swap(w_outer2, "narrow", near)
    outer2, outer3 = [w_outer2], [w_outer3]
    act2, act3, slope2, slope3, block_out, features, pool = inner_call(
        normed_two, bias_inner[2:4], [w_inner2, w_inner3], [outer2, outer3], (inner_total,),
        (mixed, norm_gains, offsets, crop_of_row),
    )

    flat_pool = pool.reshape(-1, LANES)
    pool_rows = flat_pool.shape[0]
    unit_rows = unit_share.reshape(-1, LANES)
    both = sum_over(jnp.concatenate([flat_pool, unit_rows]), ("narrow",))
    gathered, unit_rows = both[:pool_rows], both[pool_rows:]
    per_crop = jnp.repeat(crop_tokens, width // LANES)[:, None]
    gathered = gathered / per_crop
    for bit in data_bits:
        other = swap(jnp.concatenate([gathered, unit_rows]), "dp", bit)
        unit_rows = unit_rows + other[gathered.shape[0] :]
        gathered = ordered(gathered, other[: gathered.shape[0]], has_bit("dp", bit))
    unit_grad = unit_rows.reshape(unit_share.shape)
    pooled = gathered.reshape(-1, width).astype(BF16)
    all_crops, units_width = unit_grad.shape
    head_width = head_first.shape[1]
    first_act, second_act, units, embed_grad, second_low, first_low, pooled_grad = pl.pallas_call(
        head_body,
        out_shape=(
            shape((all_crops, head_width), BF16),
            shape((all_crops, head_width), BF16),
            shape((all_crops, units_width), BF16),
            shape((all_crops, units_width), F32),
            shape((all_crops, head_width), BF16),
            shape((all_crops, head_width), BF16),
            shape((all_crops, width), F32),
        ),
        in_specs=[held, held, anywhere, anywhere, anywhere, held, held, held],
        out_specs=(held,) * 7,
        scratch_shapes=[
            pltpu.VMEM(head_first.shape, BF16),
            pltpu.VMEM(head_second.shape, BF16),
            pltpu.VMEM(head_third.shape, BF16),
            pltpu.SemaphoreType.DMA((2 + head_second.shape[0] // 512,)),
        ],
        compiler_params=pltpu.CompilerParams(vmem_limit_bytes=VMEM_LIMIT),
        cost_estimate=cost(9.0),
    )(
        pooled, unit_grad, head_first, head_second, head_third,
        head_first_bias[None], head_second_bias[None], head_third_bias[None],
    )
    def own(values):
        part = values.shape[1] // groups
        return lax.dynamic_slice_in_dim(values, dp_index * part, part, 1)

    pooled_grad = lax.dynamic_slice_in_dim(pooled_grad, dp_index * crops, crops, 0) / crop_tokens[:, None]

    split = rows // 2
    by_chunk = lambda n: pl.BlockSpec((split, n), lambda i: (i, 0))
    out_grad, out_low, head_sums = pl.pallas_call(
        head_back_body,
        grid=(2,),
        out_shape=(shape((rows, width), F32), shape((rows, width), BF16), shape((3, width), F32)),
        in_specs=[by_chunk(width), by_chunk(width), by_chunk(1), fixed(crops, width), fixed(*norm_gains.shape)],
        out_specs=(by_chunk(width), by_chunk(width), fixed(3, width)),
        compiler_params=pltpu.CompilerParams(vmem_limit_bytes=VMEM_LIMIT),
        cost_estimate=cost(4.0),
    )(block_out, feature_cotangent, crop_of_row, pooled_grad, norm_gains)

    def by_group(part):
        return part.reshape(groups, part.shape[0] // groups, part.shape[1])

    def inner_back(act, slope, wi, wo, before=(), ending=()):
        last = bool(ending)
        n = len(wi)
        pieces = tuple(len(w) for w in wo)
        wo = [p for w in wo for p in w]
        outs = [shape((width, hidden), BF16)] * (2 * n) + [shape((n, hidden), F32), shape((rows, width), F32)]
        specs = [anywhere] * (2 * n) + [held, held if last else anywhere]
        if last:
            outs += [shape((padded_rows, width), BF16), shape((3, width), F32)]
            specs += [held, held]
        return pl.pallas_call(
            functools.partial(inner_back_body, windows, pieces, bool(before), last),
            out_shape=tuple(outs),
            in_specs=[anywhere] * (2 + 3 * n + len(wo) + len(before)) + ([anywhere, anywhere, held] if last else []),
            out_specs=tuple(specs),
            scratch_shapes=[
                low_held,
                low_held,
                pltpu.VMEM((n, rows, hidden), BF16),
                pltpu.VMEM((n, rows, hidden), BF16),
                pltpu.VMEM((n, width, hidden), BF16),
                pltpu.VMEM((n, hidden, width), BF16),
                pltpu.VMEM((n, width, hidden), BF16),
                pltpu.VMEM((n, width, hidden), BF16),
                pltpu.VMEM((n, rows, hidden), BF16),
                row_held,
                pltpu.SemaphoreType.DMA((2 + 3 * n + len(wo) + len(before) + 2 * last,)),
                pltpu.SemaphoreType.DMA((2 * n + 1,)),
            ] + ([row_held, pltpu.VMEM((rows + 16, width), F32)] if last else []),
            compiler_params=pltpu.CompilerParams(vmem_limit_bytes=VMEM_LIMIT),
            cost_estimate=cost(18.0 if last else 15.0),
        )(out_low, normed_two, *act, *slope, *wi, *wo, *before, *ending)

    o3, o1, i3, i1, sums_odd, total = inner_back([act3, act1], [slope3, slope1], [w_inner3, w_inner1], [outer3, [w_outer1]])
    got_o3, got_i3 = swap(o3, "narrow", near), swap(i3, "narrow", near)
    got_o1, got_i1 = swap(o1, "narrow", near), swap(i1, "narrow", near)
    o2, o0, i2, i0, sums_even, mixed_grad, mixed_low, mixed_sums = inner_back(
        [act2, act0], [slope2, slope0], [w_inner2, inner_weight], [outer2, [outer_weight]],
        (total,), (mixed, out_grad, norm_gains),
    )
    got_o3, got_i3, got_o1, got_i1 = after((got_o3, got_i3, got_o1, got_i1), mixed_low)
    grouped = lambda *parts: [by_group(p) for p in parts]
    o0, o1, o2, o3, i0, i1, i2, i3 = grouped(o0, got_o1, o2, got_o3, i0, got_i1, i2, got_i3)

    def halved(own, first, *more):
        total = rows_by_bit(first, share, own).astype(F32)
        for part in more:
            total = total + rows_by_bit(part, share, own).astype(F32)
        return total

    def rounded(value):
        return value.astype(BF16)

    send_i2 = rounded(halved(False, i2, i3))
    send_o2 = rounded(halved(False, o2, o3))
    got_i2s = swap(send_i2, "narrow", far)
    got_o2 = swap(send_o2, "dp", share)
    mixed_low = after(mixed_low, send_i2, send_o2)

    input_grads, pair_grads, input_sums = pl.pallas_call(
        functools.partial(attend_back_body, size, scale),
        grid=(padded_rows // batch,),
        out_shape=(
            shape((padded_rows, 6 * half), BF16),
            shape((PAD, 2 * pair_lanes), F32),
            shape((1, 6 * half), F32),
        ),
        in_specs=[
            by_row(width),
            fixed(count * quarter, width),
            by_row(3 * half),
            by_row(3 * half),
            by_row(pair_lanes),
            by_row(pair_lanes),
        ],
        out_specs=(by_row(6 * half), fixed(PAD, 2 * pair_lanes), fixed(1, 6 * half)),
        compiler_params=pltpu.CompilerParams(vmem_limit_bytes=VMEM_LIMIT),
        cost_estimate=cost(13.0),
    )(mixed_low, stacked_att, *qkv, *probs)

    pair_grad = pair_grads.reshape(PAD, count * heads, PAD).transpose(1, 0, 2)
    table_grad = lax.dot_general(
        pair_grad.reshape(count * heads, PAD * PAD), offset_table(256), (((1,), (0,)), ((), ())),
        precision=HIGH, preferred_element_type=F32,
    )
    got_i2s, got_o2, i2, i3, o0, o1 = after((got_i2s, got_o2, i2, i3, o0, o1), table_grad)
    send_i2 = rounded(halved(True, i2, i3))
    send_o0 = rounded(halved(False, o0, o1))
    got_i2k = swap(send_i2, "narrow", far)
    got_o0 = swap(send_o0, "dp", share)
    weight_rows = after(input_grads, send_i2, send_o0, got_i2s, got_o2)

    pair_shape = shape((2, width, half), BF16)
    pair_spec = pl.BlockSpec((1, width, half), lambda i: (1 - i, 0, 0))
    even_a, odd_a, even_b, odd_b = pl.pallas_call(
        weight_grad_body,
        grid=(2,),
        out_shape=(pair_shape,) * 4,
        in_specs=[
            fixed(padded_rows, width),
            fixed(padded_rows, width),
            pl.BlockSpec((padded_rows, 3 * half), lambda i: (0, 1 - i)),
            fixed(padded_rows, half),
            fixed(padded_rows, half),
        ],
        out_specs=(pair_spec,) * 4,
        compiler_params=pltpu.CompilerParams(vmem_limit_bytes=VMEM_LIMIT),
        cost_estimate=cost(12.0),
    )(padded, mixed_low, weight_rows, *attended)

    got_i2k, got_o0, got_i2s, got_o2 = after((got_i2k, got_o0, got_i2s, got_o2), even_a)
    far_o = rounded(halved(True, o2, o3) + got_o2.astype(F32))
    send_i = rounded(halved(False, i0, i1) + got_i2s.astype(F32))
    got_o = swap(far_o, "narrow", far)
    got_i = swap(send_i, "dp", share)
    odd_a, odd_b = after((odd_a, odd_b), far_o, send_i)
    got_a, got_b = swap(odd_a, "narrow", near), swap(odd_b, "narrow", near)
    sum_a = rounded(add(even_a[1], got_a[1]))
    keep_b, send_b = halve_rows(rounded(add(even_b, got_b)).reshape(2 * groups, width // groups, half), share)
    got_a2 = swap(sum_a, "narrow", far)
    got_b2 = swap(send_b, "dp", share)

    sums_even, sums_odd, input_sums = after((sums_even, sums_odd, input_sums), sum_a, send_b)
    sums0, sums1, sums2, sums3 = sums_even[1:2], sums_odd[1:2], sums_even[0:1], sums_odd[0:1]
    input_sum = input_sums.reshape(2, 3, 2, quarter).transpose(0, 2, 1, 3).reshape(count, 3, quarter)
    input_sum = by_distance(input_sum, "narrow").swapaxes(0, 1).reshape(3, count * quarter)
    inner_sum = by_distance(jnp.concatenate([sums0, sums1, sums2, sums3]), "narrow").reshape(-1, width)
    ends_in = jnp.concatenate([input_sum[0:1], input_sum[2:3], inner_sum])
    packed_rows = 8 + ends_in.shape[0]
    tokens_grad, packed = call(
        functools.partial(tokens_back_body, windows),
        (shape((rows, width), F32), shape((packed_rows, width), F32)),
        (
            after(input_grads, sum_a, send_b),
            *[v.reshape(3 * half, width) for v in stacked_in],
            tokens,
            mixed_grad,
            norm_gains,
            head_sums,
            mixed_sums,
            ends_in,
        ),
        scratch=[pltpu.VMEM((rows, width), F32)],
        us=10.0,
    )

    table_rows = by_distance(after(table_grad, tokens_grad).reshape(count, -1, width), "narrow").reshape(-1, width)
    small = jnp.concatenate([packed, table_rows])
    small_bits = [("narrow", near), ("narrow", far)] + [("dp", b) for b in data_bits]
    small_got = swap(small, *small_bits[0])
    got_i, got_o = after((got_i, got_o), tokens_grad)
    mlp = rounded(jnp.concatenate([
        halved(True, i0, i1) + got_i2k.astype(F32) + got_i.astype(F32),
        halved(True, o0, o1) + got_o0.astype(F32) + got_o.astype(F32),
    ], axis=2))
    keep_m, send_m = halve_rows(mlp, data_bits[1])
    got_m = swap(send_m, "dp", data_bits[1])
    got_a2, got_b2, small_got = after((got_a2, got_b2, small_got), send_m)
    keep_a, send_a = halve_rows(by_group(rounded(add(even_a[0], got_a[0]) + got_a2.astype(F32))), share)
    got_a = swap(send_a, "dp", share)
    sum_b = rounded(add(keep_b, got_b2)).reshape(2, groups // 2, width // groups, half)
    got_b = swap(sum_b[1], "narrow", far)
    small = small + small_got
    small_got = swap(small, *small_bits[1])

    own_protos = prototype_gain.shape[0]
    logits, direction_grad, gain_grad = call(
        prototype_body,
        (
            shape((all_crops, own_protos), F32),
            shape(prototype_direction.shape, F32),
            shape((1, own_protos), F32),
        ),
        (
            after(units, send_a, sum_b, small), columns_low, logit_cotangent, prototype_direction,
            column_inv, prototype_gain[None], first_epoch[None],
        ),
        us=4.0,
    )

    got_a, got_b, got_m, small_got = after((got_a, got_b, got_m, small_got), logits)
    mlp = add(keep_m, got_m)
    for bit in data_bits[2:-1]:
        keep_m, send_m = halve_rows(mlp.astype(BF16), bit)
        mlp = add(keep_m, swap(send_m, "dp", bit))
    keep_m, send_m = halve_rows(mlp.astype(BF16), data_bits[-1])
    got_m = swap(send_m, "dp", data_bits[-1])
    att_sum = rounded(jnp.concatenate([add(keep_a, got_a), add(sum_b[0], got_b)], axis=2))
    keep_j, send_j = halve_rows(att_sum, data_bits[1])
    got_j = swap(send_j, "dp", data_bits[1])
    small = small + small_got
    small_got = swap(small, *small_bits[2])

    first_low, second_low, second_act, embed_grad = after((first_low, second_low, second_act, embed_grad), send_m, send_j, small)
    own_first, own_second, own_act, own_embed = [own(v) for v in (first_low, second_low, second_act, embed_grad)]
    embed_low = embed_grad.astype(BF16)
    first_grad, second_grad, third_grad, first_bias_grad, second_bias_grad, third_bias_grad = call(
        head_grads_body,
        (
            shape((pooled.shape[1], own_first.shape[1]), F32),
            shape((first_act.shape[1], own_second.shape[1]), F32),
            shape((own_act.shape[1], embed_low.shape[1]), F32),
            shape((1, own_first.shape[1]), F32),
            shape((1, own_second.shape[1]), F32),
            shape((1, own_embed.shape[1]), F32),
        ),
        (after(pooled, send_m, send_j, small), first_act, own_act, own_first, own_second, embed_low, own_embed),
        us=5.0,
    )

    got_j, got_m, small_got = after((got_j, got_m, small_got), first_grad)
    small = small + small_got
    small_got = swap(small, *small_bits[3])
    joined = add(keep_j, got_j)
    for bit in data_bits[2:-1]:
        keep_j, send_j = halve_rows(joined.astype(BF16), bit)
        joined = add(keep_j, swap(send_j, "dp", bit))
    keep_j, send_j = halve_rows(joined.astype(BF16), data_bits[-1])
    got_j = swap(send_j, "dp", data_bits[-1])
    mlp = add(keep_m, after(got_m, send_j))
    small = small + after(small_got, send_j)
    for place in small_bits[4:]:
        small = small + swap(small, *place)
    joined = add(keep_j, after(got_j, mlp))
    inner_total, outer_total = mlp[0, :, :hidden], mlp[0, :, hidden:]
    joined = joined[0]
    attend_total = joined[:, 3 * quarter :]
    input_total = jnp.stack([joined[:, i * quarter : (i + 1) * quarter] for i in range(3)])

    gain_total, offset_total, bias_total = small[0:3], small[3:8], small[8:10]
    inner_bias_total = small[10 : 10 + inner_sum.shape[0]].reshape(-1)
    table_total = small[10 + inner_sum.shape[0] :].reshape(count * heads, 256)[:, :offsets_count].T
    return (
        features,
        logits,
        tokens_grad,
        input_total,
        bias_total,
        table_total,
        attend_total.T,
        inner_total,
        inner_bias_total,
        outer_total.T,
        gain_total,
        offset_total,
        first_grad,
        first_bias_grad[0],
        second_grad,
        second_bias_grad[0],
        third_grad,
        third_bias_grad[0],
        direction_grad,
        gain_grad[0],
    )


def solution(mesh):
    placed = (
        P(("dp", "narrow"), None),
        P(None, None, "narrow"),
        P(),
        P(),
        P("narrow", None),
        P(None, "narrow"),
        P(),
        P("narrow", None),
        P(),
        P(),
        P(),
        P(),
        P(),
        P(),
        P(),
        P(),
        P(None, ("dp", "narrow")),
        P(("dp", "narrow")),
        P("dp", None),
        P(("dp", "narrow")),
        P(("dp", "narrow"), None),
        P(None, ("dp", "narrow")),
    )
    return jax.shard_map(
        shards,
        mesh=mesh,
        in_specs=placed,
        out_specs=(
            P(("dp", "narrow"), None),
            P(None, ("dp", "narrow")),
            P(("dp", "narrow"), None),
            P(None, "dp", "narrow"),
            P(),
            P(),
            P("narrow", "dp"),
            P("dp", "narrow"),
            P(),
            P("narrow", "dp"),
            P(),
            P(),
            P(None, "dp"),
            P("dp"),
            P(None, "dp"),
            P("dp"),
            P("dp", None),
            P("dp"),
            P(None, ("dp", "narrow")),
            P(("dp", "narrow")),
        ),
        check_vma=False,
    )
```
